512 devices in a mesh: gx: 32 (over x, z), gy: 16 (over y, core).
Axes of the slice: x: 4, y: 8, z: 8, core: 2. Of those that a mesh axis runs over, the one named last changes fastest.
Arguments:
- forcing: float32 [256, 128, 256], P('gx', 'gy'), may hold values from -5 to 5
- coefficient: float32 [256, 128, 256], P('gx', 'gy'), may hold values from 0.2 to 5
Outputs:
- correction: float32 [256, 128, 256], P('gx', 'gy')
- residual: float32 [256, 128, 256], P('gx', 'gy')
The draws below stay inside these ranges and needn't reach their ends.
All inputs are finite; a program needn't handle non-finite values.
Results may differ from the reference program's by a relative error of at most 0.0003.
Values sent between devices are 32-bit elements; how exact they have to be, the bound alone decides.
No kernel may reach another device: no remote copies, remote signals or barrier semaphores. Data moves between devices by JAX's collectives and lax.ppermute only.
A program may use at most 64 MiB of HBM per device.

```python
import math
from functools import partial
import jax
import jax.numpy as jnp

NZ = 256
LEVELS = 4
SWEEPS = 2
COARSE_STEPS = 8
NX = 256
NY = 128


def draw_forcing(key, part):
    key = jax.random.fold_in(key, 11)
    grid_shape = (NX, NY, NZ)
    return jax.random.truncated_normal(key, -5.0, 5.0, grid_shape, jnp.float32)


def shard_levels(rng, shape, pieces, smallest, largest):
    level, own = 1.0, jax.random.fold_in(rng, 6)
    for position, parts in pieces:
        draws = jnp.exp(jax.random.uniform(jax.random.fold_in(own, position), (parts,), jnp.float32, smallest / len(pieces), largest / len(pieces)))
        level = level * jnp.repeat(draws, shape[position] // parts).reshape([-1 if axis == position else 1 for axis in range(len(shape))])
    return level


def setup_inputs(seed: int = 0) -> dict:
    key_of = jax.random.split(jax.random.key(seed), 3)
    forcing = draw_forcing(jax.random.fold_in(key_of[2], 71), 0)
    coefficient = jnp.clip(jnp.exp(math.log(5.0) - 3.218876 * jax.random.uniform(key_of[1], (NX, NY, NZ), jnp.float32) ** shard_levels(key_of[1], (NX, NY, NZ), ((0, 32), (1, 16)), -0.2, 0.2)), 0.2, 5.0)
    return dict(forcing=forcing, coefficient=coefficient)


smooth_low = 0.4
coarse_low = 0.02
upper_bound = 2.0


def neighbours(grid_values):
    padded = jnp.pad(grid_values, 1)
    return (padded[:-2, 1:-1, 1:-1], padded[2:, 1:-1, 1:-1],
            padded[1:-1, :-2, 1:-1], padded[1:-1, 2:, 1:-1],
            padded[1:-1, 1:-1, :-2], padded[1:-1, 1:-1, 2:])


def operator_parts(coefficient):
    return tuple(0.5 * (coefficient + near_coeff) for near_coeff in neighbours(coefficient))


def diagonal_inverse(coefficient):
    weights = operator_parts(coefficient)
    summed = weights[0] + weights[1] + weights[2] + weights[3] + weights[4] + weights[5]
    return 1.0 / summed


def apply_operator(grid_values, coefficient):
    summed = jnp.zeros_like(grid_values)
    for weight, near_value in zip(operator_parts(coefficient), neighbours(grid_values)):
        summed = summed + weight * (grid_values - near_value)
    return summed


def chebyshev(forcing, initial, sweeps_count, low_end, keep_last, operate, inverse):
    center = 0.5 * (upper_bound + low_end)
    radius = 0.5 * (upper_bound - low_end)
    sigma_value = center / radius
    ratio_now = 1.0 / sigma_value
    if initial is None:
        solution = jnp.zeros_like(forcing)
        residual = forcing
    else:
        solution = initial
        residual = forcing - operate(initial)
    direction = None
    for sweep_index in range(sweeps_count):
        if sweep_index == 0:
            direction = inverse * residual / center
        else:
            ratio_next = 1.0 / (2.0 * sigma_value - ratio_now)
            direction = (ratio_next * ratio_now) * direction + (2.0 * ratio_next / radius) * (inverse * residual)
            ratio_now = ratio_next
        solution = solution + direction
        if keep_last or sweep_index + 1 < sweeps_count:
            residual = residual - operate(direction)
    return solution, residual


def coarsen(grid_values):
    size_x, size_y, size_z = grid_values.shape
    return grid_values.reshape(size_x // 2, 2, size_y // 2, 2, size_z // 2, 2).sum(axis=(1, 3, 5))


def refine(grid_values):
    return jnp.repeat(jnp.repeat(jnp.repeat(grid_values, 2, axis=0), 2, axis=1), 2, axis=2)


def reference(forcing, coefficient):
    right_sides = [forcing]
    coeffs = [coefficient]
    solutions = []
    for level_index in range(LEVELS - 1):
        coeff_now = coeffs[level_index]
        solution, residual = chebyshev(right_sides[level_index], None, SWEEPS, smooth_low, True,
                                       partial(apply_operator, coefficient=coeff_now), diagonal_inverse(coeff_now))
        solutions.append(solution)
        right_sides.append(0.5 * coarsen(residual))
        coeffs.append(0.125 * coarsen(coeff_now))
    coeff_now = coeffs[LEVELS - 1]
    result, residual = chebyshev(right_sides[LEVELS - 1], None, COARSE_STEPS, coarse_low, False,
                                 partial(apply_operator, coefficient=coeff_now), diagonal_inverse(coeff_now))
    for level_index in reversed(range(LEVELS - 1)):
        coeff_now = coeffs[level_index]
        result, residual = chebyshev(right_sides[level_index], solutions[level_index] + refine(result), SWEEPS,
                                     smooth_low, level_index == 0,
                                     partial(apply_operator, coefficient=coeff_now), diagonal_inverse(coeff_now))
    return result, residual
```

```python
import jax
import jax.numpy as jnp
from jax import lax
from jax.experimental import pallas as pl
from jax.experimental.pallas import tpu as pltpu
from jax.sharding import PartitionSpec as P

INTERPRET = False
COARSE_STEPS = 8
F32 = jnp.float32
HIGHEST = lax.Precision.HIGHEST
VMEM_LIMIT = 56 * 1024 * 1024


def step_factors(low_end, steps):
    center, radius = 0.5 * (2.0 + low_end), 0.5 * (2.0 - low_end)
    sigma = center / radius
    ratio = 1.0 / sigma
    factors = [(0.0, 1.0 / center)]
    for _ in range(steps - 1):
        ratio_next = 1.0 / (2.0 * sigma - ratio)
        factors.append((ratio_next * ratio, 2.0 * ratio_next / radius))
        ratio = ratio_next
    return factors


(_, FIRST), (KEEP, ADD) = step_factors(0.4, 2)
COARSE_FACTORS = step_factors(0.02, COARSE_STEPS)


def iota(shape, dim):
    return lax.broadcasted_iota(jnp.int32, shape, dim)


def shifted(value, step, axis):
    return pltpu.roll(value, (-step) % value.shape[axis], axis)


def dot(a, b):
    return jnp.dot(a, b, precision=HIGHEST, preferred_element_type=F32)


def ones_where(condition):
    return jnp.where(condition, 1.0, 0.0).astype(F32)


def planes(first, last, step):
    def one(index, carry):
        step(index)
        return carry

    lax.fori_loop(first, last, one, 0)


def near(ref, index):
    plane = ref[index]
    return (ref[index - 1], ref[index + 1], shifted(plane, -1, 0), shifted(plane, 1, 0),
            shifted(plane, -1, 1), shifted(plane, 1, 1))


def near_inside(ref, index):
    x_low, x_high, y_low, y_high, z_low, z_high = near(ref, index)
    lane = iota(z_low.shape, 1)
    z_low = jnp.where(lane == 0, 0.0, z_low)
    z_high = jnp.where(lane == z_low.shape[1] - 1, 0.0, z_high)
    return x_low, x_high, y_low, y_high, z_low, z_high


def coupling(center, around, masked):
    total = 6.0 * center
    for value in around:
        total = total + value
    half_inverse = jnp.where(center > 0.0, 1.0 / jnp.where(center > 0.0, total, 1.0), 0.0)
    couplings = []
    for number, value in enumerate(around):
        c = (center + value) * half_inverse
        couplings.append(jnp.where(value > 0.0, c, 0.0) if number in masked else c)
    return couplings, 2.0 * half_inverse, 0.5 * total


def spread(c_ref, c_index, around):
    total = c_ref[0, c_index] * around[0]
    for number in range(1, 6):
        total = total + c_ref[number, c_index] * around[number]
    return total


def fine_kernel(low_ref, own_ref, high_ref, gather_ref, share_ref, x0_ref,
                k0, c0, diag0, g0, d0, e0, sums, zsums, k1, f1, c1, diag1, g1, d1, e1, out):
    def join(index):
        k0[index] = jnp.concatenate([low_ref[index], own_ref[index], high_ref[index]], 0)

    planes(0, 22, join)

    def setup(index):
        couplings, inverse, diagonal = coupling(k0[index + 1], near_inside(k0, index + 1), (4, 5))
        for number in range(6):
            c0[number, index] = couplings[number]
        diag0[index] = diagonal
        force = jnp.concatenate([low_ref[index + 22], own_ref[index + 22], high_ref[index + 22]], 0)
        scaled = inverse * force
        g0[index] = scaled
        d0[index] = FIRST * scaled

    planes(0, 20, setup)

    def second(index):
        scaled = g0[index] - d0[index] + spread(c0, index, near(d0, index))
        g0[index] = scaled
        e0[index] = KEEP * d0[index] + ADD * scaled

    planes(1, 19, second)

    def guess(index):
        total = d0[index + 3] + e0[index + 3]
        x0_ref[index] = shifted(total, 4, 0)[0:16]

    planes(0, 14, guess)

    def left(index):
        return diag0[index] * (g0[index] - e0[index] + spread(c0, index, near(e0, index)))

    def pair(index):
        sums[index] = 0.5 * (left(2 * index + 2) + left(2 * index + 3))

    planes(0, 8, pair)

    def pair_k(index):
        sums[index + 8] = 0.125 * (k0[2 * index + 1] + k0[2 * index + 2])

    planes(0, 10, pair_k)
    fold = ones_where(iota((256, 128), 0) // 2 == iota((256, 128), 1))
    zsums[...] = dot(sums[...].reshape(18 * 24, 256), fold).reshape(18, 24, 128)

    k1[...] = jnp.zeros_like(k1)
    f1[...] = jnp.zeros_like(f1)

    def halve(index):
        rows = zsums[index, pl.ds(0, 12, stride=2), :] + zsums[index, pl.ds(1, 12, stride=2), :]

        @pl.when(index < 8)
        def _():
            f1[index, 2:14, :] = rows

        @pl.when(index >= 8)
        def _():
            k1[index - 8, 2:14, :] = rows

    planes(0, 18, halve)

    def share(index):
        share_ref[index] = k1[index + 1, 4:12, :]
        share_ref[index + 8] = f1[index, 4:12, :]

    planes(0, 8, share)

    def setup1(index):
        couplings, inverse, diagonal = coupling(k1[index + 1], near_inside(k1, index + 1), (4, 5))
        for number in range(6):
            c1[number, index] = couplings[number]
        diag1[index] = diagonal
        scaled = inverse * f1[index]
        g1[index] = scaled
        d1[index] = FIRST * scaled

    planes(0, 8, setup1)

    def second1(index):
        scaled = g1[index] - d1[index] + spread(c1, index, near(d1, index))
        g1[index] = scaled
        e1[index] = KEEP * d1[index] + ADD * scaled

    planes(1, 7, second1)

    def left1(index):
        return diag1[index] * (g1[index] - e1[index] + spread(c1, index, near(e1, index)))

    for half in range(2):
        out[half] = 0.5 * (left1(2 * half + 2) + left1(2 * half + 3))
        out[half + 2] = 0.125 * (k1[2 * half + 3] + k1[2 * half + 4])
    row, lane = iota((128, 256), 0), iota((128, 256), 1)
    fold = ones_where((lane == row // 2) | (lane == 192 + row // 2))
    folded = dot(out[...].reshape(64, 128), fold).reshape(4, 16, 256)
    for number in range(4):
        gather_ref[number:number + 1, :] = (folded[number, 6:7, 0:128] + folded[number, 7:8, 0:128]
                                            + folded[number, 8:9, 128:256] + folded[number, 9:10, 128:256])


def near2(ref, index):
    plane = ref[index]
    swapped = shifted(plane, 64, 1)
    first = iota(plane.shape, 1) < 64
    y_low = jnp.where(first, shifted(swapped, -1, 0), swapped)
    y_high = jnp.where(first, swapped, shifted(swapped, 1, 0))
    return ref[index - 1], ref[index + 1], y_low, y_high, shifted(plane, -1, 1), shifted(plane, 1, 1)


def near2_inside(ref, index):
    x_low, x_high, y_low, y_high, z_low, z_high = near2(ref, index)
    lane, row, rows = iota(z_low.shape, 1), iota(z_low.shape, 0), z_low.shape[0]
    y_low = jnp.where((row == 0) & (lane < 64), 0.0, y_low)
    y_high = jnp.where((row == rows - 1) & (lane >= 64), 0.0, y_high)
    z_low = jnp.where(lane % 64 == 0, 0.0, z_low)
    z_high = jnp.where(lane % 64 == 63, 0.0, z_high)
    return x_low, x_high, y_low, y_high, z_low, z_high


def near3(values, index, count):
    plane = values[index]
    x_low = values[index - 1] if index else shifted(values[count - 1], -32, 1)
    x_high = values[index + 1] if index + 1 < count else shifted(values[0], 32, 1)
    return (x_low, x_high, shifted(plane, -1, 0), shifted(plane, 1, 0),
            shifted(plane, -1, 1), shifted(plane, 1, 1))


def near3_inside(values, index, count):
    x_low, x_high, y_low, y_high, z_low, z_high = near3(values, index, count)
    lane, row, rows = iota(z_low.shape, 1), iota(z_low.shape, 0), z_low.shape[0]
    if index == 0:
        x_low = jnp.where(lane < 32, 0.0, x_low)
    if index == count - 1:
        x_high = jnp.where(lane >= 96, 0.0, x_high)
    y_low = jnp.where(row == 0, 0.0, y_low)
    y_high = jnp.where(row == rows - 1, 0.0, y_high)
    z_low = jnp.where(lane % 32 == 0, 0.0, z_low)
    z_high = jnp.where(lane % 32 == 31, 0.0, z_high)
    return x_low, x_high, y_low, y_high, z_low, z_high


def make_coarse_kernel(count_x, count_y):
    planes2, rows, count3 = 2 * count_x, count_y, count_x // 4

    def coarse_kernel(place_ref, data_ref, near_ref,
                      k2, c2, diag2, g2, d2, e2, sums, c3, h3, e3, x0, u0, u1):
        for ref in (k2, g2, d2, e2):
            for end in range(4):
                ref[end] = jnp.zeros((rows, 128), F32)
                ref[planes2 + 4 + end] = jnp.zeros((rows, 128), F32)
        for number in range(6):
            for end in range(4):
                c2[number, end] = jnp.zeros((rows, 128), F32)
                c2[number, planes2 + 4 + end] = jnp.zeros((rows, 128), F32)

        def load(index):
            for half in range(2):
                start = index * (4 * rows) + half
                k2[2 * index + half + 4] = data_ref[pl.ds(start + 2, rows, stride=4), :]
                e2[2 * index + half + 4] = data_ref[pl.ds(start, rows, stride=4), :]

        planes(0, count_x, load)

        def setup(index):
            couplings, inverse, diagonal = coupling(k2[index], near2_inside(k2, index), (2, 3, 4, 5))
            for number in range(6):
                c2[number, index] = couplings[number]
            diag2[index] = diagonal
            scaled = inverse * e2[index]
            g2[index] = scaled
            d2[index] = FIRST * scaled

        planes(4, planes2 + 4, setup)

        def second(index):
            scaled = g2[index] - d2[index] + spread(c2, index, near2(d2, index))
            u0[index] = scaled
            e2[index] = KEEP * d2[index] + ADD * scaled

        planes(4, planes2 + 4, second)

        def left(index):
            return diag2[index] * (u0[index] - e2[index] + spread(c2, index, near2(e2, index)))

        def pair(index):
            sums[index] = 0.5 * (left(2 * index + 4) + left(2 * index + 5))
            sums[index + count_x] = 0.125 * (k2[2 * index + 4] + k2[2 * index + 5])

        planes(0, count_x, pair)

        f3 = jnp.zeros((count3 * rows, 128), F32)
        k3 = jnp.zeros((count3 * rows, 128), F32)
        row, lane = iota((128, 128), 0), iota((128, 128), 1)
        for quarter in range(4):
            fold = ones_where(lane == 32 * quarter + (row % 64) // 2)
            part = sums[pl.ds(quarter * count3, count3)].reshape(count3 * rows, 128)
            f3 = f3 + dot(part, fold)
            part = sums[pl.ds(count_x + quarter * count3, count3)].reshape(count3 * rows, 128)
            k3 = k3 + dot(part, fold)
        f3 = f3.reshape(count3, rows, 128)
        k3 = k3.reshape(count3, rows, 128)

        g3, d3, total = [], [], []
        for index in range(count3):
            around = near3_inside([k3[i] for i in range(count3)], index, count3)
            couplings, inverse, _ = coupling(k3[index], around, (0, 1, 2, 3, 4, 5))
            for number in range(6):
                c3[number, index] = couplings[number]
            scaled = inverse * f3[index]
            g3.append(scaled)
            d3.append(COARSE_FACTORS[0][1] * scaled)
            total.append(d3[-1])
        for keep, add in COARSE_FACTORS[1:]:
            d3_new = []
            for index in range(count3):
                g3[index] = g3[index] - d3[index] + spread(c3, index, near3(d3, index, count3))
                d3_new.append(keep * d3[index] + add * g3[index])
                total[index] = total[index] + d3_new[-1]
            d3 = d3_new
        for index in range(count3):
            e3[index] = total[index]

        at_x, at_y = place_ref[0], place_ref[1]
        base = 2 * at_x
        parts = []
        for number in range(5):
            x3 = at_x - 2 + number
            inside = (x3 >= 0) & (x3 < count_x)
            safe = jnp.clip(x3, 0, count_x - 1)
            plane = pltpu.roll(e3[safe % count3], (128 - 32 * (safe // count3)) % 128, 1)
            parts.append(jnp.where(inside, plane, 0.0))
        unfold = ones_where((row < 32) & ((lane % 64) // 2 == row))
        up = dot(jnp.concatenate(parts, 0), unfold).reshape(5, rows, 128)
        for index in range(10):
            x0[index] = d2[base + index] + e2[base + index] + up[index // 2]
        for index in range(1, 9):
            u0[index] = g2[base + index] - x0[index] + spread(c2, base + index, near2(x0, index))
        for index in range(1, 9):
            u1[index] = FIRST * u0[index]
        for index in range(2, 8):
            scaled = u0[index] - u1[index] + spread(c2, base + index, near2(u1, index))
            x0[index] = x0[index] + (1.0 + KEEP) * u1[index] + ADD * scaled

        widen = ones_where((iota((128, 256), 0) == 64 * (iota((128, 256), 1) // 128) + (iota((128, 256), 1) % 128) // 2))
        wide = dot(x0[2:8].reshape(6 * rows, 128), widen)
        target, source = iota((16, rows), 0), iota((16, rows), 1)
        inside = (target >= 2) & (target < 14) & (source == at_y - 1 + (target - 2) // 4)
        first = ones_where(inside & ((target - 2) % 4 < 2))
        other = ones_where(inside & ((target - 2) % 4 >= 2))
        for index in range(6):
            block = wide[index * rows:(index + 1) * rows]
            near_ref[index] = dot(first, block[:, 0:128]) + dot(other, block[:, 128:256])

    return coarse_kernel


def post_kernel(near_ref, low1_ref, own1_ref, high1_ref, low_ref, own_ref, high_ref, x0_ref,
                correction_ref, residual_ref,
                k1, c1, g1, d1, h1, x1, wide, k0, c0, diag0, g0, y0, d0, h0):
    def join(ref_index):
        row = iota((8, 128), 0)
        middle = shifted(own1_ref[ref_index], 4, 0)
        return jnp.concatenate([jnp.where(row < 6, low1_ref[ref_index], middle),
                                jnp.where(row < 2, middle, high1_ref[ref_index])], 0)

    def load(index):
        k1[index] = join(index)

    planes(0, 16, load)

    def setup1(index):
        couplings, inverse, _ = coupling(k1[index], near_inside(k1, index), (4, 5))
        for number in range(6):
            c1[number, index] = couplings[number]
        scaled = inverse * join(index + 16)
        g1[index] = scaled
        d1[index] = FIRST * scaled

    planes(1, 15, setup1)

    def guess1(index):
        scaled = g1[index] - d1[index] + spread(c1, index, near(d1, index))
        x1[index] = (1.0 + KEEP) * d1[index] + ADD * scaled + near_ref[index // 2 - 1]

    planes(2, 14, guess1)

    def first1(index):
        scaled = g1[index] - x1[index] + spread(c1, index, near(x1, index))
        h1[index] = scaled
        d1[index] = FIRST * scaled

    planes(3, 13, first1)

    def second1(index):
        scaled = h1[index] - d1[index] + spread(c1, index, near(d1, index))
        value = x1[index] + (1.0 + KEEP) * d1[index] + ADD * scaled
        wide[index - 4, pl.ds(0, 8, stride=2), :] = value[4:12]
        wide[index - 4, pl.ds(1, 8, stride=2), :] = value[4:12]

    planes(4, 12, second1)
    unfold = ones_where(iota((128, 256), 0) == iota((128, 256), 1) // 2)
    up = dot(wide[...].reshape(128, 128), unfold).reshape(8, 16, 256)

    for index in range(1, 15):
        y0[index] = x0_ref[index - 1] + up[index // 2]

    def cut(ref_index):
        both = jnp.concatenate([low_ref[ref_index], own_ref[ref_index], high_ref[ref_index]], 0)
        return shifted(both, 4, 0)[0:16]

    def load0(index):
        k0[index] = cut(index + 3)

    planes(1, 15, load0)

    def setup0(index):
        couplings, inverse, diagonal = coupling(k0[index], near_inside(k0, index), (4, 5))
        for number in range(6):
            c0[number, index] = couplings[number]
        diag0[index] = diagonal
        scaled = inverse * cut(index + 24) - y0[index] + spread(c0, index, near(y0, index))
        g0[index] = scaled
        d0[index] = FIRST * scaled

    planes(2, 14, setup0)

    def second0(index):
        scaled = g0[index] - d0[index] + spread(c0, index, near(d0, index))
        g0[index] = scaled
        h0[index] = KEEP * d0[index] + ADD * scaled

    planes(3, 13, second0)

    def last0(index):
        value = y0[index] + d0[index] + h0[index]
        correction_ref[index - 4] = value[4:12]
        scaled = g0[index] - h0[index] + spread(c0, index, near(h0, index))
        residual_ref[index - 4] = (diag0[index] * scaled)[4:12]

    planes(4, 12, last0)


def call(kernel, shapes, scratch, *operands, scalars=0):
    specs = [pl.BlockSpec(memory_space=pltpu.SMEM)] * scalars
    specs += [pl.BlockSpec(memory_space=pltpu.VMEM)] * (len(operands) - scalars)
    return pl.pallas_call(
        kernel,
        out_shape=[jax.ShapeDtypeStruct(shape, F32) for shape in shapes],
        in_specs=specs,
        out_specs=[pl.BlockSpec(memory_space=pltpu.VMEM)] * len(shapes),
        scratch_shapes=[pltpu.VMEM(shape, F32) for shape in scratch],
        compiler_params=pltpu.CompilerParams(vmem_limit_bytes=VMEM_LIMIT),
        interpret=INTERPRET,
    )(*operands)


def both_sides(value, axis):
    count = lax.axis_size(axis)
    low = lax.ppermute(value, axis, [(i, i + 1) for i in range(count - 1)])
    high = lax.ppermute(value, axis, [(i + 1, i) for i in range(count - 1)])
    return low, high


def body(forcing, coefficient):
    count_x, count_y = lax.axis_size("gx"), lax.axis_size("gy")
    block = jnp.concatenate([coefficient, forcing], 0)
    low, high = both_sides(block, "gx")
    own = jnp.concatenate([low[1:8], coefficient, high[0:7], low[10:16], forcing, high[8:14]], 0)
    low, high = both_sides(own, "gy")

    full, full1 = (24, 256), (16, 128)
    payload, share, guess = call(
        fine_kernel,
        [(4, 128), (16, 8, 128), (14, 16, 256)],
        [(22, *full), (6, 20, *full)] + [(20, *full)] * 4 + [(18, *full), (18, 24, 128)]
        + [(10, *full1), (8, *full1), (6, 8, *full1)] + [(8, *full1)] * 4 + [(4, *full1)],
        low, own, high)

    copies = jnp.broadcast_to(payload[None], (count_x * count_y, *payload.shape))
    everything = lax.all_to_all(copies, ("gx", "gy"), 0, 0).reshape(-1, 128)

    low1, high1 = both_sides(share, "gx")
    own1 = jnp.concatenate([low1[0:6], share[2:6], high1[2:8], low1[8:14], share[10:14], high1[10:16]], 0)
    low1, high1 = both_sides(own1, "gy")

    place = jnp.stack([lax.axis_index("gx"), lax.axis_index("gy")]).astype(jnp.int32)
    padded = 2 * count_x + 8
    plane2 = (count_y, 128)
    near_e, = call(
        make_coarse_kernel(count_x, count_y),
        [(6, 16, 128)],
        [(padded, *plane2), (6, padded, *plane2)] + [(padded, *plane2)] * 4
        + [(2 * count_x, *plane2), (6, count_x // 4, *plane2)] + [(count_x // 4, *plane2)] * 2
        + [(10, *plane2), (padded, *plane2), (10, *plane2)],
        place, everything, scalars=1)

    half = (16, 256)
    correction, residual = call(
        post_kernel,
        [forcing.shape, forcing.shape],
        [(16, *full1), (6, 16, *full1)] + [(16, *full1)] * 4 + [(8, *full1)]
        + [(16, *half), (6, 16, *half)] + [(16, *half)] * 5,
        near_e, low1, own1, high1, low, own, high, guess)
    return correction, residual


def solution(mesh):
    spec = P("gx", "gy", None)
    return jax.shard_map(body, mesh=mesh, in_specs=(spec, spec), out_specs=(spec, spec), check_vma=False)
```

```python
import math

import jax
import jax.numpy as jnp
from jax import lax
from jax.experimental import pallas as pl
from jax.experimental.pallas import tpu as pltpu
from jax.sharding import PartitionSpec as P

INTERPRET = False
COARSE_STEPS = 8
F32 = jnp.float32
HIGHEST = lax.Precision.HIGHEST
MIB = 1024 * 1024


def step_factors(low_end, steps):
    center, radius = 0.5 * (2.0 + low_end), 0.5 * (2.0 - low_end)
    sigma = center / radius
    ratio = 1.0 / sigma
    factors = [(0.0, 1.0 / center)]
    for _ in range(steps - 1):
        ratio_next = 1.0 / (2.0 * sigma - ratio)
        factors.append((ratio_next * ratio, 2.0 * ratio_next / radius))
        ratio = ratio_next
    return factors


(_, FIRST), (KEEP, ADD) = step_factors(0.4, 2)
COARSE_FACTORS = step_factors(0.02, COARSE_STEPS)


def iota(shape, dim):
    return lax.broadcasted_iota(jnp.int32, shape, dim)


def shifted(value, step, axis):
    return pltpu.roll(value, (-step) % value.shape[axis], axis)


def dot(a, b):
    return jnp.dot(a, b, precision=HIGHEST, preferred_element_type=F32)


def ones_where(condition):
    return jnp.where(condition, 1.0, 0.0).astype(F32)


def blocks(first, last, size, step):
    count = (last - first) // size
    assert first + count * size == last
    if count == 1:
        step(first)
        return

    def one(number, carry):
        step(first + number * size)
        return carry

    lax.fori_loop(0, count, one, 0)


def near(ref, start, size):
    here = ref[pl.ds(start, size)]
    return (ref[pl.ds(start - 1, size)], ref[pl.ds(start + 1, size)],
            shifted(here, -1, 1), shifted(here, 1, 1), shifted(here, -1, 2), shifted(here, 1, 2))


def near_inside(ref, start, size):
    x_low, x_high, y_low, y_high, z_low, z_high = near(ref, start, size)
    lane = iota(z_low.shape, 2)
    z_low = jnp.where(lane == 0, 0.0, z_low)
    z_high = jnp.where(lane == z_low.shape[2] - 1, 0.0, z_high)
    return x_low, x_high, y_low, y_high, z_low, z_high


def coupling(center, around, masked):
    total = 6.0 * center
    for value in around:
        total = total + value
    inside = center > 0.0
    half_inverse = jnp.where(inside, 1.0 / jnp.where(inside, total, 1.0), 0.0)
    couplings = []
    for number, value in enumerate(around):
        c = (center + value) * half_inverse
        couplings.append(jnp.where(value > 0.0, c, 0.0) if number in masked else c)
    return couplings, 2.0 * half_inverse, 0.5 * total


def pick(c_ref, number, where):
    return c_ref.at[number][where] if where else c_ref[number]


def spread(c_ref, where, around):
    total = pick(c_ref, 0, where) * around[0]
    for number in range(1, 6):
        total = total + pick(c_ref, number, where) * around[number]
    return total


def fine_kernel(low_ref, own_ref, high_ref, copies_ref, share_ref,
                k0, c0, diag0, g0, d0, e0, sums, zsums, k1, f1, c1, diag1, g1, d1, e1, out):
    for index in range(22):
        k0[index, 0:8] = low_ref[index]
        k0[index, 8:16] = own_ref[index]
        k0[index, 16:24] = high_ref[index]

    def setup(start):
        at = pl.ds(start, 2)
        couplings, inverse, diagonal = coupling(k0[pl.ds(start + 1, 2)], near_inside(k0, start + 1, 2), (4, 5))
        for number in range(6):
            c0.at[number][at] = couplings[number]
        diag0[at] = diagonal
        force = pl.ds(start + 22, 2)
        scaled = inverse * jnp.concatenate([low_ref[force], own_ref[force], high_ref[force]], 1)
        g0[at] = scaled
        d0[at] = FIRST * scaled

    blocks(0, 20, 2, setup)

    def second(start):
        at = pl.ds(start, 2)
        here = d0[at]
        scaled = g0[at] - here + spread(c0, (at,), near(d0, start, 2))
        g0[at] = scaled
        e0[at] = KEEP * here + ADD * scaled

    blocks(1, 19, 2, second)

    def left(start):
        at = pl.ds(start, 2)
        rest = diag0[at] * (g0[at] - e0[at] + spread(c0, (at,), near(e0, start, 2)))
        sums[start // 2 - 1] = 0.5 * (rest[0] + rest[1])

    blocks(2, 18, 2, left)
    for index in range(10):
        sums[index + 8] = 0.125 * (k0[2 * index + 1] + k0[2 * index + 2])
    fold = ones_where(iota((256, 128), 0) // 2 == iota((256, 128), 1))
    zsums[...] = dot(sums[...].reshape(18 * 24, 256), fold).reshape(18, 24, 128)

    k1[...] = jnp.zeros_like(k1)
    f1[...] = jnp.zeros_like(f1)
    rows = zsums[:, pl.ds(0, 12, stride=2), :] + zsums[:, pl.ds(1, 12, stride=2), :]
    f1[:, 2:14, :] = rows[0:8]
    k1[:, 2:14, :] = rows[8:18]
    share_ref[0:8] = k1[1:9, 4:12, :]
    share_ref[8:16] = f1[:, 4:12, :]

    def setup1(start):
        at = pl.ds(start, 4)
        couplings, inverse, diagonal = coupling(k1[pl.ds(start + 1, 4)], near_inside(k1, start + 1, 4), (4, 5))
        for number in range(6):
            c1.at[number][at] = couplings[number]
        diag1[at] = diagonal
        scaled = inverse * f1[at]
        g1[at] = scaled
        d1[at] = FIRST * scaled

    blocks(0, 8, 4, setup1)
    at = pl.ds(1, 6)
    scaled = g1[at] - d1[at] + spread(c1, (at,), near(d1, 1, 6))
    g1[at] = scaled
    e1[at] = KEEP * d1[at] + ADD * scaled
    at = pl.ds(2, 4)
    rest = diag1[at] * (g1[at] - e1[at] + spread(c1, (at,), near(e1, 2, 4)))
    for half in range(2):
        out[half] = 0.5 * (rest[2 * half] + rest[2 * half + 1])
        out[half + 2] = 0.125 * (k1[2 * half + 3] + k1[2 * half + 4])
    row, lane = iota((128, 256), 0), iota((128, 256), 1)
    fold = ones_where((lane == row // 2) | (lane == 192 + row // 2))
    folded = dot(out[...].reshape(64, 128), fold).reshape(4, 16, 256)
    lines = [folded[number, 6:7, 0:128] + folded[number, 7:8, 0:128]
             + folded[number, 8:9, 128:256] + folded[number, 9:10, 128:256] for number in range(4)]
    payload = jnp.concatenate(lines, 0)

    def copy(start):
        copies_ref[pl.ds(start, 8)] = jnp.broadcast_to(payload[None], (8, 4, 128))

    blocks(0, copies_ref.shape[0], 8, copy)


def near2(ref, start, size):
    here = ref[pl.ds(start, size)]
    below, above = ref[pl.ds(start - 1, size)], ref[pl.ds(start + 1, size)]
    z_low, z_high = shifted(here, -1, 3), shifted(here, 1, 3)
    turned = shifted(here, 64, 3)
    turned0, turned1 = turned[:, 0:1], turned[:, 1:2]
    first = iota(turned0.shape, 3) < 64
    y_high = [jnp.where(first, turned0, turned1), jnp.where(first, turned1, shifted(turned0, 1, 2))]
    y_low = [jnp.where(first, shifted(turned1, -1, 2), turned0), jnp.where(first, turned0, turned1)]
    return below, above, jnp.concatenate(y_low, 1), jnp.concatenate(y_high, 1), z_low, z_high


def near2_inside(ref, start, size):
    x_low, x_high, y_low, y_high, z_low, z_high = near2(ref, start, size)
    core, row, lane = (iota(z_low.shape, dim) for dim in (1, 2, 3))
    last = z_low.shape[2] - 1
    y_low = jnp.where((core == 0) & (row == 0) & (lane < 64), 0.0, y_low)
    y_high = jnp.where((core == 1) & (row == last) & (lane >= 64), 0.0, y_high)
    z_low = jnp.where(lane % 64 == 0, 0.0, z_low)
    z_high = jnp.where(lane % 64 == 63, 0.0, z_high)
    return x_low, x_high, y_low, y_high, z_low, z_high


def near3(value):
    count = value.shape[0]
    before, after = shifted(value[count - 1:], -32, 3), shifted(value[0:1], 32, 3)
    x_low = jnp.concatenate([before, value[:count - 1]], 0) if count > 1 else before
    x_high = jnp.concatenate([value[1:], after], 0) if count > 1 else after
    core0, core1 = value[:, 0:1], value[:, 1:2]
    y_low = jnp.concatenate([shifted(core1, -1, 2), core0], 1)
    y_high = jnp.concatenate([core1, shifted(core0, 1, 2)], 1)
    return x_low, x_high, y_low, y_high, shifted(value, -1, 3), shifted(value, 1, 3)


def near3_inside(value):
    x_low, x_high, y_low, y_high, z_low, z_high = near3(value)
    plane, core, row, lane = (iota(value.shape, dim) for dim in range(4))
    count, rows = value.shape[0], value.shape[2]
    x_low = jnp.where((plane == 0) & (lane < 32), 0.0, x_low)
    x_high = jnp.where((plane == count - 1) & (lane >= 96), 0.0, x_high)
    y_low = jnp.where((core == 0) & (row == 0), 0.0, y_low)
    y_high = jnp.where((core == 1) & (row == rows - 1), 0.0, y_high)
    z_low = jnp.where(lane % 32 == 0, 0.0, z_low)
    z_high = jnp.where(lane % 32 == 31, 0.0, z_high)
    return x_low, x_high, y_low, y_high, z_low, z_high


def make_coarse_kernel(count_x, count_y):
    planes2, rows, count3 = 2 * count_x, count_y // 2, count_x // 4
    size = 8
    line = (2, rows, 128)

    def coarse_kernel(place_ref, mine_ref, other_ref, near_ref,
                      k2, c2, diag2, g2, d2, e2, h2, sums, c3, e3, x0):
        at_x, at_y = place_ref[0], place_ref[1]
        zero = jnp.zeros((4, *line), F32)
        for ends in (pl.ds(0, 4), pl.ds(planes2 + 4, 4)):
            for ref in (k2, g2, d2, e2):
                ref[ends] = zero
            for number in range(6):
                c2.at[number][ends] = zero

        core = at_y % 2

        def load(index):
            for half in range(2):
                start = index * (4 * rows) + half
                to = 2 * index + half + 4
                for ref, side in ((mine_ref, core), (other_ref, 1 - core)):
                    k2[to, side] = ref[pl.ds(start + 2, rows, stride=4), :]
                    e2[to, side] = ref[pl.ds(start, rows, stride=4), :]

        def load_some(start):
            for index in range(4):
                load(start + index)

        blocks(0, count_x, 4, load_some)

        def setup(start):
            at = pl.ds(start, size)
            couplings, inverse, diagonal = coupling(k2[at], near2_inside(k2, start, size), (2, 3, 4, 5))
            for number in range(6):
                c2.at[number][at] = couplings[number]
            diag2[at] = diagonal
            scaled = inverse * e2[at]
            g2[at] = scaled
            d2[at] = FIRST * scaled

        blocks(4, planes2 + 4, size, setup)

        def second(start):
            at = pl.ds(start, size)
            here = d2[at]
            scaled = g2[at] - here + spread(c2, (at,), near2(d2, start, size))
            h2[at] = scaled
            e2[at] = KEEP * here + ADD * scaled

        blocks(4, planes2 + 4, size, second)

        def left(start):
            at = pl.ds(start, size)
            rest = diag2[at] * (h2[at] - e2[at] + spread(c2, (at,), near2(e2, start, size)))
            rest = rest.reshape(size // 2, 2, *line)
            here = k2[at].reshape(size // 2, 2, *line)
            to = (start - 4) // 2
            sums[pl.ds(to, size // 2)] = 0.5 * (rest[:, 0] + rest[:, 1])
            sums[pl.ds(to + count_x, size // 2)] = 0.125 * (here[:, 0] + here[:, 1])

        blocks(4, planes2 + 4, size, left)

        flat = count3 * 2 * rows
        f3 = jnp.zeros((flat, 128), F32)
        k3 = jnp.zeros((flat, 128), F32)
        row, lane = iota((128, 128), 0), iota((128, 128), 1)
        for quarter in range(4):
            fold = ones_where(lane == 32 * quarter + (row % 64) // 2)
            f3 = f3 + dot(sums[pl.ds(quarter * count3, count3)].reshape(flat, 128), fold)
            k3 = k3 + dot(sums[pl.ds(count_x + quarter * count3, count3)].reshape(flat, 128), fold)
        f3 = f3.reshape(count3, *line)
        k3 = k3.reshape(count3, *line)
        couplings, inverse, _ = coupling(k3, near3_inside(k3), (0, 1, 2, 3, 4, 5))
        for number in range(6):
            c3[number] = couplings[number]
        scaled = inverse * f3
        step = COARSE_FACTORS[0][1] * scaled
        total = step
        for keep, add in COARSE_FACTORS[1:]:
            scaled = scaled - step + spread(c3, (), near3(step))
            step = keep * step + add * scaled
            total = total + step
        e3[...] = total

        base = 2 * at_x
        parts = []
        for number in range(5):
            x3 = at_x - 2 + number
            inside = (x3 >= 0) & (x3 < count_x)
            safe = jnp.clip(x3, 0, count_x - 1)
            plane = pltpu.roll(e3[safe % count3].reshape(2 * rows, 128), (128 - 32 * (safe // count3)) % 128, 1)
            parts.append(jnp.where(inside, plane, 0.0))
        unfold = ones_where((row < 32) & ((lane % 64) // 2 == row))
        up = dot(jnp.concatenate(parts, 0), unfold).reshape(5, *line)
        local = pl.ds(base, 10)
        twice = jnp.stack([up, up], 1).reshape(10, *line)
        x0[...] = d2[local] + e2[local] + twice
        inner = pl.ds(base + 1, 8)
        scaled = g2[inner] - x0[1:9] + spread(c2, (inner,), near2(x0, 1, 8))
        h2[0:8] = scaled
        d2[0:8] = FIRST * scaled
        inner = pl.ds(base + 2, 6)
        here = d2[1:7]
        scaled = h2[1:7] - here + spread(c2, (inner,), near2(d2, 1, 6))
        found = x0[2:8] + (1.0 + KEEP) * here + ADD * scaled

        row, lane = iota((128, 256), 0), iota((128, 256), 1)
        widen = ones_where(row == 64 * (lane // 128) + (lane % 128) // 2)
        wide = dot(found.reshape(6 * 2 * rows, 128), widen)
        target, source = iota((16, 2 * rows), 0), iota((16, 2 * rows), 1)
        source = 2 * (source % rows) + source // rows
        inside = (target >= 2) & (target < 14) & (source == at_y - 1 + (target - 2) // 4)
        first = ones_where(inside & ((target - 2) % 4 < 2))
        other = ones_where(inside & ((target - 2) % 4 >= 2))
        for index in range(6):
            block = wide[index * 2 * rows:(index + 1) * 2 * rows]
            near_ref[index] = dot(first, block[:, 0:128]) + dot(other, block[:, 128:256])

    return coarse_kernel


def prepare_kernel(low1_ref, own1_ref, high1_ref, low_ref, own_ref, high_ref,
                   c1, g1, x1, c0, diag0, g0, x0, k1, d1, k0, d0, all0):
    def join(start, size):
        at = pl.ds(start, size)
        row = iota((size, 8, 128), 1)
        middle = shifted(own1_ref[at], 4, 1)
        return jnp.concatenate([jnp.where(row < 6, low1_ref[at], middle),
                                jnp.where(row < 2, middle, high1_ref[at])], 1)

    k1[0:8] = join(0, 8)
    k1[8:16] = join(8, 8)

    def setup1(start):
        at = pl.ds(start, 7)
        couplings, inverse, _ = coupling(k1[at], near_inside(k1, start, 7), (4, 5))
        for number in range(6):
            c1.at[number][at] = couplings[number]
        scaled = inverse * join(start + 16, 7)
        g1[at] = scaled
        d1[at] = FIRST * scaled

    blocks(1, 15, 7, setup1)

    def guess1(start):
        at = pl.ds(start, 6)
        here = d1[at]
        scaled = g1[at] - here + spread(c1, (at,), near(d1, start, 6))
        x1[at] = (1.0 + KEEP) * here + ADD * scaled

    blocks(2, 14, 6, guess1)

    def load0(start):
        at = pl.ds(start + 2, 2)
        k0[pl.ds(start, 2)] = jnp.concatenate([low_ref[at], own_ref[at], high_ref[at]], 1)

    blocks(0, 18, 2, load0)

    def setup0(start):
        def cut(value):
            return shifted(value, 4, 1)[:, 0:16]

        at = pl.ds(start, 2)
        couplings, inverse, diagonal = coupling(k0[pl.ds(start + 1, 2)], near_inside(k0, start + 1, 2), (4, 5))
        for number in range(6):
            c0.at[number][at] = cut(couplings[number])
        diag0[at] = cut(diagonal)
        force = pl.ds(start + 24, 2)
        scaled = cut(inverse * jnp.concatenate([low_ref[force], own_ref[force], high_ref[force]], 1))
        g0[at] = scaled
        d0[at] = FIRST * scaled

    blocks(0, 16, 2, setup0)

    def guess0(start):
        at = pl.ds(start, 2)
        here = d0[at]
        scaled = g0[at] - here + spread(c0, (at,), near(d0, start, 2))
        x0[at] = (1.0 + KEEP) * here + ADD * scaled

    blocks(1, 15, 2, guess0)


def post_kernel(near_ref, c1, g1, x1, c0, diag0, g0, x0, correction_ref, residual_ref,
                y1, d1, h1, wide, y0, d0, h0, v0):
    up = near_ref[...]
    y1[2:14] = x1[2:14] + jnp.stack([up, up], 1).reshape(12, 16, 128)
    scaled = g1[3:13] - y1[3:13] + spread(c1, (pl.ds(3, 10),), near(y1, 3, 10))
    h1[3:13] = scaled
    d1[3:13] = FIRST * scaled
    here = d1[4:12]
    scaled = h1[4:12] - here + spread(c1, (pl.ds(4, 8),), near(d1, 4, 8))
    found = y1[4:12] + (1.0 + KEEP) * here + ADD * scaled
    wide[:, pl.ds(0, 8, stride=2), :] = found[:, 4:12]
    wide[:, pl.ds(1, 8, stride=2), :] = found[:, 4:12]
    unfold = ones_where(iota((128, 256), 0) == iota((128, 256), 1) // 2)
    up = dot(wide[...].reshape(128, 128), unfold).reshape(8, 16, 256)

    for index in range(1, 15):
        y0[index] = x0[index] + up[index // 2]

    def first0(start):
        at = pl.ds(start, 3)
        scaled = g0[at] - y0[at] + spread(c0, (at,), near(y0, start, 3))
        h0[at] = scaled
        d0[at] = FIRST * scaled

    blocks(2, 14, 3, first0)

    def second0(start):
        at = pl.ds(start, 2)
        here = d0[at]
        scaled = h0[at] - here + spread(c0, (at,), near(d0, start, 2))
        h0[at] = scaled
        v0[at] = KEEP * here + ADD * scaled

    blocks(3, 13, 2, second0)

    def last0(start):
        at, to = pl.ds(start, 2), pl.ds(start - 4, 2)
        here = v0[at]
        correction_ref[to] = (y0[at] + d0[at] + here)[:, 4:12]
        scaled = h0[at] - here + spread(c0, (at,), near(v0, start, 2))
        residual_ref[to] = (diag0[at] * scaled)[:, 4:12]

    blocks(4, 12, 2, last0)


def call(kernel, limit, shapes, scratch, *operands, scalars=0):
    specs = [pl.BlockSpec(memory_space=pltpu.SMEM)] * scalars
    specs += [pl.BlockSpec(memory_space=pltpu.VMEM)] * (len(operands) - scalars)
    return pl.pallas_call(
        kernel,
        out_shape=[jax.ShapeDtypeStruct(shape, F32) for shape in shapes],
        in_specs=specs,
        out_specs=[pl.BlockSpec(memory_space=pltpu.VMEM)] * len(shapes),
        scratch_shapes=[pltpu.VMEM(shape, F32) for shape in scratch],
        compiler_params=pltpu.CompilerParams(vmem_limit_bytes=limit * MIB),
        interpret=INTERPRET,
    )(*operands)


def both_sides(value, axes):
    count = math.prod(lax.axis_size(axis) for axis in axes)
    low = lax.ppermute(value, axes, [(i, i + 1) for i in range(count - 1)])
    high = lax.ppermute(value, axes, [(i + 1, i) for i in range(count - 1)])
    return low, high


def body(forcing, coefficient):
    count_x, chips = lax.axis_size("gx"), lax.axis_size("chip")
    count_y = 2 * chips
    block = jnp.concatenate([coefficient, forcing], 0)
    low, high = both_sides(block, ("gx",))
    own = jnp.concatenate([low[1:8], coefficient, high[0:7], low[10:16], forcing, high[8:14]], 0)
    low, high = both_sides(own, ("chip", "core"))

    full, half, full1 = (24, 256), (16, 256), (16, 128)
    copies, share = call(
        fine_kernel, 16,
        [(count_x * chips, 4, 128), (16, 8, 128)],
        [(22, *full), (6, 20, *full)] + [(20, *full)] * 4 + [(18, *full), (18, 24, 128)]
        + [(10, *full1), (8, *full1), (6, 8, *full1)] + [(8, *full1)] * 4 + [(4, *full1)],
        low, own, high)

    mine = lax.all_to_all(copies, ("gx", "chip"), 0, 0).reshape(-1, 128)
    other = lax.ppermute(mine, "core", [(0, 1), (1, 0)])

    low1, high1 = both_sides(share, ("gx",))
    own1 = jnp.concatenate([low1[0:6], share[2:6], high1[2:8], low1[8:14], share[10:14], high1[10:16]], 0)
    low1, high1 = both_sides(own1, ("chip", "core"))
    prepared = call(
        prepare_kernel, 16,
        [(6, 16, *full1)] + [(16, *full1)] * 2 + [(6, 16, *half)] + [(16, *half)] * 3,
        [(16, *full1)] * 2 + [(18, *full), (16, *half), (1, *full)],
        low1, own1, high1, low, own, high)

    place = jnp.stack([lax.axis_index("gx"), lax.axis_index(("chip", "core"))]).astype(jnp.int32)
    plane2 = (2, count_y // 2, 128)
    padded = (2 * count_x + 8, *plane2)
    near_e, = call(
        make_coarse_kernel(count_x, count_y), 20,
        [(6, 16, 128)],
        [padded, (6, *padded)] + [padded] * 5
        + [(2 * count_x, *plane2), (6, count_x // 4, *plane2), (count_x // 4, *plane2), (10, *plane2)],
        place, mine, other, scalars=1)

    correction, residual = call(
        post_kernel, 16,
        [forcing.shape, forcing.shape],
        [(16, *full1)] * 3 + [(8, *full1)] + [(16, *half)] * 4,
        near_e, *prepared)
    return correction, residual


def solution(mesh):
    shape = (mesh.shape["gx"], mesh.shape["gy"] // 2, 2)
    mesh = jax.sharding.Mesh(mesh.devices.reshape(shape), ("gx", "chip", "core"))
    spec = P("gx", ("chip", "core"), None)
    return jax.shard_map(body, mesh=mesh, in_specs=(spec, spec), out_specs=(spec, spec), check_vma=False)
```

```python
import math

import jax
import jax.numpy as jnp
from jax import lax
from jax.experimental import pallas as pl
from jax.experimental.pallas import tpu as pltpu
from jax.sharding import PartitionSpec as P

INTERPRET = False
COARSE_STEPS = 8
F32 = jnp.float32
HIGHEST = lax.Precision.HIGHEST
MIB = 1024 * 1024


def step_factors(low_end, steps):
    center, radius = 0.5 * (2.0 + low_end), 0.5 * (2.0 - low_end)
    sigma = center / radius
    ratio = 1.0 / sigma
    factors = [(0.0, 1.0 / center)]
    for _ in range(steps - 1):
        ratio_next = 1.0 / (2.0 * sigma - ratio)
        factors.append((ratio_next * ratio, 2.0 * ratio_next / radius))
        ratio = ratio_next
    return factors


(_, FIRST), (KEEP, ADD) = step_factors(0.4, 2)
COARSE_FACTORS = step_factors(0.02, COARSE_STEPS)


def iota(shape, dim):
    return lax.broadcasted_iota(jnp.int32, shape, dim)


def shifted(value, step, axis):
    return pltpu.roll(value, (-step) % value.shape[axis], axis)


def dot(a, b):
    return jnp.dot(a, b, precision=HIGHEST, preferred_element_type=F32)


def ones_where(condition):
    return jnp.where(condition, 1.0, 0.0).astype(F32)


def blocks(first, last, size, step):
    count = (last - first) // size
    assert first + count * size == last
    if count == 1:
        step(first)
        return

    def one(number, carry):
        step(first + number * size)
        return carry

    lax.fori_loop(0, count, one, 0)


def near(ref, start, size):
    here = ref[pl.ds(start, size)]
    return (ref[pl.ds(start - 1, size)], ref[pl.ds(start + 1, size)],
            shifted(here, -1, 1), shifted(here, 1, 1), shifted(here, -1, 2), shifted(here, 1, 2))


def near_inside(ref, start, size):
    x_low, x_high, y_low, y_high, z_low, z_high = near(ref, start, size)
    lane = iota(z_low.shape, 2)
    z_low = jnp.where(lane == 0, 0.0, z_low)
    z_high = jnp.where(lane == z_low.shape[2] - 1, 0.0, z_high)
    return x_low, x_high, y_low, y_high, z_low, z_high


def coupling(center, around, masked):
    total = 6.0 * center
    for value in around:
        total = total + value
    inside = center > 0.0
    half_inverse = jnp.where(inside, 1.0 / jnp.where(inside, total, 1.0), 0.0)
    couplings = []
    for number, value in enumerate(around):
        c = (center + value) * half_inverse
        couplings.append(jnp.where(value > 0.0, c, 0.0) if number in masked else c)
    return couplings, 2.0 * half_inverse, 0.5 * total


def pick(c_ref, number, where):
    return c_ref.at[number][where] if where else c_ref[number]


def spread(c_ref, where, around):
    total = pick(c_ref, 0, where) * around[0]
    for number in range(1, 6):
        total = total + pick(c_ref, number, where) * around[number]
    return total


PAIRS = ([("k", dx, 7 - dx) for dx in (1, 2, 3)], [("f", dx, 6 - dx) for dx in (1, 2, 3)])
Y_TILES = 28


def pack_x_kernel(k_ref, f_ref, up_ref, down_ref):
    up_ref[0:7] = k_ref[1:8]
    up_ref[7:13] = f_ref[2:8]
    down_ref[0:7] = k_ref[0:7]
    down_ref[7:13] = f_ref[0:6]


def pair_tiles():
    tile = 16
    for pairs in PAIRS:
        for side in ("low", "high"):
            for name, dx, far in pairs:
                yield tile, name, side, dx, far
                tile += 1


def halo_plane(name, side, dx, low_ref, high_ref):
    reach = 7 if name == "k" else 6
    base = 0 if name == "k" else 7
    return low_ref[base + reach - dx] if side == "low" else high_ref[base + dx - 1]


def pack_y_kernel(k_ref, f_ref, low_ref, high_ref, up_ref, down_ref):
    for ref in (up_ref, down_ref):
        ref[0:8] = k_ref[...]
        ref[8:16] = f_ref[...]
    row = iota((8, k_ref.shape[2]), 0)
    for tile, name, side, dx, far in pair_tiles():
        near_plane = halo_plane(name, side, dx, low_ref, high_ref)
        far_plane = halo_plane(name, side, far, low_ref, high_ref)
        up_ref[tile] = jnp.where(row < dx, shifted(far_plane, 8 - dx, 0), near_plane)
        down_ref[tile] = jnp.where(row >= 8 - dx, shifted(far_plane, dx - 8, 0), near_plane)


def unpack(k_ref, f_ref, x_low_ref, x_high_ref, y_low_ref, y_high_ref, k0, f0):
    for to, base, reach, name, ref in ((k0, 0, 7, "k", k_ref), (f0, 8, 6, "f", f_ref)):
        to[reach:reach + 8, 0:8] = y_low_ref[base:base + 8]
        to[reach:reach + 8, 8:16] = ref[...]
        to[reach:reach + 8, 16:24] = y_high_ref[base:base + 8]
        first = 0 if name == "k" else 7
        to[0:reach, 8:16] = x_low_ref[first:first + reach]
        to[reach + 8:2 * reach + 8, 8:16] = x_high_ref[first:first + reach]
        for plane in (0, 2 * reach + 7):
            to[plane, 0:8] = jnp.zeros(ref.shape[1:], F32)
            to[plane, 16:24] = jnp.zeros(ref.shape[1:], F32)
    for tile, name, side, dx, far in pair_tiles():
        to, reach = (k0, 7) if name == "k" else (f0, 6)
        near_plane = reach - dx if side == "low" else reach + 7 + dx
        far_plane = reach - far if side == "low" else reach + 7 + far
        below, above = y_low_ref[tile], y_high_ref[tile]
        to[near_plane, 0:8] = below
        to[near_plane, 16:24] = above
        if far != dx:
            to[far_plane, 0:8] = shifted(below, dx - 8, 0)
            to[far_plane, 16:24] = shifted(above, 8 - dx, 0)


def fine_kernel(k_ref, f_ref, x_low_ref, x_high_ref, y_low_ref, y_high_ref,
                k0, f0, k1, f1, up_ref, down_ref,
                c0, diag0, g0, d0, e0, sums, zsums):
    unpack(k_ref, f_ref, x_low_ref, x_high_ref, y_low_ref, y_high_ref, k0, f0)

    def setup(start):
        at = pl.ds(start, 2)
        couplings, inverse, diagonal = coupling(k0[pl.ds(start + 1, 2)], near_inside(k0, start + 1, 2), (4, 5))
        for number in range(6):
            c0.at[number][at] = couplings[number]
        diag0[at] = diagonal
        scaled = inverse * f0[at]
        g0[at] = scaled
        d0[at] = FIRST * scaled

    blocks(0, 20, 2, setup)

    def second(start):
        at = pl.ds(start, 2)
        here = d0[at]
        scaled = g0[at] - here + spread(c0, (at,), near(d0, start, 2))
        g0[at] = scaled
        e0[at] = KEEP * here + ADD * scaled

    blocks(1, 19, 2, second)

    def left(start):
        at = pl.ds(start, 2)
        rest = diag0[at] * (g0[at] - e0[at] + spread(c0, (at,), near(e0, start, 2)))
        sums[start // 2 - 1] = 0.5 * (rest[0] + rest[1])

    blocks(2, 18, 2, left)
    for index in range(10):
        sums[index + 8] = 0.125 * (k0[2 * index + 1] + k0[2 * index + 2])
    fold = ones_where(iota((256, 128), 0) // 2 == iota((256, 128), 1))
    zsums[...] = dot(sums[...].reshape(18 * 24, 256), fold).reshape(18, 24, 128)

    k1[...] = jnp.zeros_like(k1)
    f1[...] = jnp.zeros_like(f1)
    rows = zsums[:, pl.ds(0, 12, stride=2), :] + zsums[:, pl.ds(1, 12, stride=2), :]
    f1[:, 2:14, :] = rows[0:8]
    k1[:, 2:14, :] = rows[8:18]
    up_ref[0:6] = k1[1:7, 4:12, :]
    up_ref[6:11] = f1[1:6, 4:12, :]
    down_ref[0:6] = k1[3:9, 4:12, :]
    down_ref[6:11] = f1[2:7, 4:12, :]


def next_kernel(k1, f1, copies_ref, c1, diag1, g1, d1, e1, out):
    def setup1(start):
        at = pl.ds(start, 4)
        couplings, inverse, diagonal = coupling(k1[pl.ds(start + 1, 4)], near_inside(k1, start + 1, 4), (4, 5))
        for number in range(6):
            c1.at[number][at] = couplings[number]
        diag1[at] = diagonal
        scaled = inverse * f1[at]
        g1[at] = scaled
        d1[at] = FIRST * scaled

    blocks(0, 8, 4, setup1)
    at = pl.ds(1, 6)
    scaled = g1[at] - d1[at] + spread(c1, (at,), near(d1, 1, 6))
    g1[at] = scaled
    e1[at] = KEEP * d1[at] + ADD * scaled
    at = pl.ds(2, 4)
    rest = diag1[at] * (g1[at] - e1[at] + spread(c1, (at,), near(e1, 2, 4)))
    for half in range(2):
        out[half] = 0.5 * (rest[2 * half] + rest[2 * half + 1])
        out[half + 2] = 0.125 * (k1[2 * half + 3] + k1[2 * half + 4])
    row, lane = iota((128, 256), 0), iota((128, 256), 1)
    fold = ones_where((lane == row // 2) | (lane == 192 + row // 2))
    folded = dot(out[...].reshape(64, 128), fold).reshape(4, 16, 256)
    lines = [folded[number, 6:7, 0:128] + folded[number, 7:8, 0:128]
             + folded[number, 8:9, 128:256] + folded[number, 9:10, 128:256] for number in range(4)]
    payload = jnp.concatenate(lines, 0)

    def copy(start):
        copies_ref[pl.ds(start, 8)] = jnp.broadcast_to(payload[None], (8, 4, 128))

    blocks(0, copies_ref.shape[0], 8, copy)


def near2(ref, start, size):
    here = ref[pl.ds(start, size)]
    below, above = ref[pl.ds(start - 1, size)], ref[pl.ds(start + 1, size)]
    z_low, z_high = shifted(here, -1, 3), shifted(here, 1, 3)
    turned = shifted(here, 64, 3)
    turned0, turned1 = turned[:, 0:1], turned[:, 1:2]
    first = iota(turned0.shape, 3) < 64
    y_high = [jnp.where(first, turned0, turned1), jnp.where(first, turned1, shifted(turned0, 1, 2))]
    y_low = [jnp.where(first, shifted(turned1, -1, 2), turned0), jnp.where(first, turned0, turned1)]
    return below, above, jnp.concatenate(y_low, 1), jnp.concatenate(y_high, 1), z_low, z_high


def near2_inside(ref, start, size):
    x_low, x_high, y_low, y_high, z_low, z_high = near2(ref, start, size)
    core, row, lane = (iota(z_low.shape, dim) for dim in (1, 2, 3))
    last = z_low.shape[2] - 1
    y_low = jnp.where((core == 0) & (row == 0) & (lane < 64), 0.0, y_low)
    y_high = jnp.where((core == 1) & (row == last) & (lane >= 64), 0.0, y_high)
    z_low = jnp.where(lane % 64 == 0, 0.0, z_low)
    z_high = jnp.where(lane % 64 == 63, 0.0, z_high)
    return x_low, x_high, y_low, y_high, z_low, z_high


def near3(value):
    count = value.shape[0]
    before, after = shifted(value[count - 1:], -32, 3), shifted(value[0:1], 32, 3)
    x_low = jnp.concatenate([before, value[:count - 1]], 0) if count > 1 else before
    x_high = jnp.concatenate([value[1:], after], 0) if count > 1 else after
    core0, core1 = value[:, 0:1], value[:, 1:2]
    y_low = jnp.concatenate([shifted(core1, -1, 2), core0], 1)
    y_high = jnp.concatenate([core1, shifted(core0, 1, 2)], 1)
    return x_low, x_high, y_low, y_high, shifted(value, -1, 3), shifted(value, 1, 3)


def near3_inside(value):
    x_low, x_high, y_low, y_high, z_low, z_high = near3(value)
    plane, core, row, lane = (iota(value.shape, dim) for dim in range(4))
    count, rows = value.shape[0], value.shape[2]
    x_low = jnp.where((plane == 0) & (lane < 32), 0.0, x_low)
    x_high = jnp.where((plane == count - 1) & (lane >= 96), 0.0, x_high)
    y_low = jnp.where((core == 0) & (row == 0), 0.0, y_low)
    y_high = jnp.where((core == 1) & (row == rows - 1), 0.0, y_high)
    z_low = jnp.where(lane % 32 == 0, 0.0, z_low)
    z_high = jnp.where(lane % 32 == 31, 0.0, z_high)
    return x_low, x_high, y_low, y_high, z_low, z_high


def make_coarse_kernel(count_x, count_y):
    planes2, rows, count3 = 2 * count_x, count_y // 2, count_x // 4
    size = 8
    line = (2, rows, 128)

    def coarse_kernel(place_ref, mine_ref, other_ref, near_ref,
                      k2, c2, diag2, g2, d2, e2, h2, sums, c3, e3, x0):
        at_x, at_y = place_ref[0], place_ref[1]
        zero = jnp.zeros((4, *line), F32)
        for ends in (pl.ds(0, 4), pl.ds(planes2 + 4, 4)):
            for ref in (k2, g2, d2, e2):
                ref[ends] = zero
            for number in range(6):
                c2.at[number][ends] = zero

        core = at_y % 2

        def load(index):
            for half in range(2):
                start = index * (4 * rows) + half
                to = 2 * index + half + 4
                for ref, side in ((mine_ref, core), (other_ref, 1 - core)):
                    k2[to, side] = ref[pl.ds(start + 2, rows, stride=4), :]
                    e2[to, side] = ref[pl.ds(start, rows, stride=4), :]

        def load_some(start):
            for index in range(4):
                load(start + index)

        blocks(0, count_x, 4, load_some)

        def setup(start):
            at = pl.ds(start, size)
            couplings, inverse, diagonal = coupling(k2[at], near2_inside(k2, start, size), (2, 3, 4, 5))
            for number in range(6):
                c2.at[number][at] = couplings[number]
            diag2[at] = diagonal
            scaled = inverse * e2[at]
            g2[at] = scaled
            d2[at] = FIRST * scaled

        blocks(4, planes2 + 4, size, setup)

        def second(start):
            at = pl.ds(start, size)
            here = d2[at]
            scaled = g2[at] - here + spread(c2, (at,), near2(d2, start, size))
            h2[at] = scaled
            e2[at] = KEEP * here + ADD * scaled

        blocks(4, planes2 + 4, size, second)

        def left(start):
            at = pl.ds(start, size)
            rest = diag2[at] * (h2[at] - e2[at] + spread(c2, (at,), near2(e2, start, size)))
            rest = rest.reshape(size // 2, 2, *line)
            here = k2[at].reshape(size // 2, 2, *line)
            to = (start - 4) // 2
            sums[pl.ds(to, size // 2)] = 0.5 * (rest[:, 0] + rest[:, 1])
            sums[pl.ds(to + count_x, size // 2)] = 0.125 * (here[:, 0] + here[:, 1])

        blocks(4, planes2 + 4, size, left)

        flat = count3 * 2 * rows
        f3 = jnp.zeros((flat, 128), F32)
        k3 = jnp.zeros((flat, 128), F32)
        row, lane = iota((128, 128), 0), iota((128, 128), 1)
        for quarter in range(4):
            fold = ones_where(lane == 32 * quarter + (row % 64) // 2)
            f3 = f3 + dot(sums[pl.ds(quarter * count3, count3)].reshape(flat, 128), fold)
            k3 = k3 + dot(sums[pl.ds(count_x + quarter * count3, count3)].reshape(flat, 128), fold)
        f3 = f3.reshape(count3, *line)
        k3 = k3.reshape(count3, *line)
        couplings, inverse, _ = coupling(k3, near3_inside(k3), (0, 1, 2, 3, 4, 5))
        for number in range(6):
            c3[number] = couplings[number]
        scaled = inverse * f3
        step = COARSE_FACTORS[0][1] * scaled
        total = step
        for keep, add in COARSE_FACTORS[1:]:
            scaled = scaled - step + spread(c3, (), near3(step))
            step = keep * step + add * scaled
            total = total + step
        e3[...] = total

        base = 2 * at_x
        parts = []
        for number in range(5):
            x3 = at_x - 2 + number
            inside = (x3 >= 0) & (x3 < count_x)
            safe = jnp.clip(x3, 0, count_x - 1)
            plane = pltpu.roll(e3[safe % count3].reshape(2 * rows, 128), (128 - 32 * (safe // count3)) % 128, 1)
            parts.append(jnp.where(inside, plane, 0.0))
        unfold = ones_where((row < 32) & ((lane % 64) // 2 == row))
        up = dot(jnp.concatenate(parts, 0), unfold).reshape(5, *line)
        local = pl.ds(base, 10)
        twice = jnp.stack([up, up], 1).reshape(10, *line)
        x0[...] = d2[local] + e2[local] + twice
        inner = pl.ds(base + 1, 8)
        scaled = g2[inner] - x0[1:9] + spread(c2, (inner,), near2(x0, 1, 8))
        h2[0:8] = scaled
        d2[0:8] = FIRST * scaled
        inner = pl.ds(base + 2, 6)
        here = d2[1:7]
        scaled = h2[1:7] - here + spread(c2, (inner,), near2(d2, 1, 6))
        found = x0[2:8] + (1.0 + KEEP) * here + ADD * scaled

        row, lane = iota((128, 256), 0), iota((128, 256), 1)
        widen = ones_where(row == 64 * (lane // 128) + (lane % 128) // 2)
        wide = dot(found.reshape(6 * 2 * rows, 128), widen)
        target, source = iota((16, 2 * rows), 0), iota((16, 2 * rows), 1)
        source = 2 * (source % rows) + source // rows
        inside = (target >= 2) & (target < 14) & (source == at_y - 1 + (target - 2) // 4)
        first = ones_where(inside & ((target - 2) % 4 < 2))
        other = ones_where(inside & ((target - 2) % 4 >= 2))
        for index in range(6):
            block = wide[index * 2 * rows:(index + 1) * 2 * rows]
            near_ref[index] = dot(first, block[:, 0:128]) + dot(other, block[:, 128:256])

    return coarse_kernel


def pack_share_kernel(k1, f1, low_ref, high_ref, out_ref):
    out_ref[0:5] = low_ref[1:6]
    out_ref[5:9] = k1[3:7, 4:12, :]
    out_ref[9:14] = high_ref[0:5]
    out_ref[14:18] = low_ref[7:11]
    out_ref[18:22] = f1[2:6, 4:12, :]
    out_ref[22:26] = high_ref[6:10]


def prepare_kernel(x_low_ref, x_high_ref, y_low_ref, own_ref, y_high_ref, k_ref, f_ref,
                   c1, g1, x1, c0, diag0, g0, x0, k1, f1, d1, d0):
    row = iota((8, 128), 0)

    def join(low, middle, high):
        middle = shifted(middle, 4, 1)
        return jnp.concatenate([jnp.where(row < 6, low, middle), jnp.where(row < 2, middle, high)], 1)

    zero = jnp.zeros((1, 8, 128), F32)
    k1[1:15] = join(y_low_ref[0:14], own_ref[0:14], y_high_ref[0:14])
    f1[2:14] = join(y_low_ref[14:26], own_ref[14:26], y_high_ref[14:26])
    for to, plane, tile in ((k1, 0, x_low_ref[0:1]), (k1, 15, x_high_ref[5:6]),
                            (f1, 1, x_low_ref[6:7]), (f1, 14, x_high_ref[10:11])):
        to[plane:plane + 1] = join(zero, tile, zero)

    def setup1(start):
        at = pl.ds(start, 7)
        couplings, inverse, _ = coupling(k1[at], near_inside(k1, start, 7), (4, 5))
        for number in range(6):
            c1.at[number][at] = couplings[number]
        scaled = inverse * f1[at]
        g1[at] = scaled
        d1[at] = FIRST * scaled

    blocks(1, 15, 7, setup1)

    def guess1(start):
        at = pl.ds(start, 6)
        here = d1[at]
        scaled = g1[at] - here + spread(c1, (at,), near(d1, start, 6))
        x1[at] = (1.0 + KEEP) * here + ADD * scaled

    blocks(2, 14, 6, guess1)

    def setup0(start):
        def cut(value):
            return shifted(value, 4, 1)[:, 0:16]

        at = pl.ds(start, 2)
        couplings, inverse, diagonal = coupling(k_ref[pl.ds(start + 3, 2)], near_inside(k_ref, start + 3, 2), (4, 5))
        for number in range(6):
            c0.at[number][at] = cut(couplings[number])
        diag0[at] = cut(diagonal)
        scaled = cut(inverse * f_ref[pl.ds(start + 2, 2)])
        g0[at] = scaled
        d0[at] = FIRST * scaled

    blocks(0, 16, 2, setup0)

    def guess0(start):
        at = pl.ds(start, 2)
        here = d0[at]
        scaled = g0[at] - here + spread(c0, (at,), near(d0, start, 2))
        x0[at] = (1.0 + KEEP) * here + ADD * scaled

    blocks(1, 15, 2, guess0)


def post_kernel(near_ref, c1, g1, x1, c0, diag0, g0, x0, correction_ref, residual_ref,
                y1, d1, h1, wide, y0, d0, h0, v0):
    up = near_ref[...]
    y1[2:14] = x1[2:14] + jnp.stack([up, up], 1).reshape(12, 16, 128)
    scaled = g1[3:13] - y1[3:13] + spread(c1, (pl.ds(3, 10),), near(y1, 3, 10))
    h1[3:13] = scaled
    d1[3:13] = FIRST * scaled
    here = d1[4:12]
    scaled = h1[4:12] - here + spread(c1, (pl.ds(4, 8),), near(d1, 4, 8))
    found = y1[4:12] + (1.0 + KEEP) * here + ADD * scaled
    wide[:, pl.ds(0, 8, stride=2), :] = found[:, 4:12]
    wide[:, pl.ds(1, 8, stride=2), :] = found[:, 4:12]
    unfold = ones_where(iota((128, 256), 0) == iota((128, 256), 1) // 2)
    up = dot(wide[...].reshape(128, 128), unfold).reshape(8, 16, 256)

    for index in range(1, 15):
        y0[index] = x0[index] + up[index // 2]

    def first0(start):
        at = pl.ds(start, 3)
        scaled = g0[at] - y0[at] + spread(c0, (at,), near(y0, start, 3))
        h0[at] = scaled
        d0[at] = FIRST * scaled

    blocks(2, 14, 3, first0)

    def second0(start):
        at = pl.ds(start, 2)
        here = d0[at]
        scaled = h0[at] - here + spread(c0, (at,), near(d0, start, 2))
        h0[at] = scaled
        v0[at] = KEEP * here + ADD * scaled

    blocks(3, 13, 2, second0)

    def last0(start):
        at, to = pl.ds(start, 2), pl.ds(start - 4, 2)
        here = v0[at]
        correction_ref[to] = (y0[at] + d0[at] + here)[:, 4:12]
        scaled = h0[at] - here + spread(c0, (at,), near(v0, start, 2))
        residual_ref[to] = (diag0[at] * scaled)[:, 4:12]

    blocks(4, 12, 2, last0)


def call(kernel, limit, shapes, scratch, *operands, scalars=0, flops=0):
    specs = [pl.BlockSpec(memory_space=pltpu.SMEM)] * scalars
    specs += [pl.BlockSpec(memory_space=pltpu.VMEM)] * (len(operands) - scalars)
    return pl.pallas_call(
        kernel,
        out_shape=[jax.ShapeDtypeStruct(shape, F32) for shape in shapes],
        in_specs=specs,
        out_specs=[pl.BlockSpec(memory_space=pltpu.VMEM)] * len(shapes),
        scratch_shapes=[pltpu.VMEM(shape, F32) for shape in scratch],
        compiler_params=pltpu.CompilerParams(vmem_limit_bytes=limit * MIB),
        cost_estimate=pl.CostEstimate(flops=flops, bytes_accessed=0, transcendentals=0) if flops else None,
        interpret=INTERPRET,
    )(*operands)


def both_sides(up, down, axes):
    count = math.prod(lax.axis_size(axis) for axis in axes)
    low = lax.ppermute(up, axes, [(i, i + 1) for i in range(count - 1)])
    high = lax.ppermute(down, axes, [(i + 1, i) for i in range(count - 1)])
    return low, high


def body(f, k):
    count_x, chips = lax.axis_size("gx"), lax.axis_size("chip")
    count_y = 2 * chips
    along_x, along_y = ("gx",), ("chip", "core")
    tile, full, half = f.shape[1:], (24, 256), (16, 256)
    tile1, full1 = (8, 128), (16, 128)
    up, down = call(pack_x_kernel, 4, [(13, *tile)] * 2, [], k, f)
    x_low, x_high = both_sides(up, down, along_x)
    up, down = call(pack_y_kernel, 4, [(Y_TILES, *tile)] * 2, [], k, f, x_low, x_high)
    y_low, y_high = both_sides(up, down, along_y)

    k0, f0, k1, f1, up, down = call(
        fine_kernel, 16,
        [(22, *full), (20, *full), (10, *full1), (8, *full1), (11, *tile1), (11, *tile1)],
        [(6, 20, *full)] + [(20, *full)] * 4 + [(18, *full), (18, 24, 128)],
        k, f, x_low, x_high, y_low, y_high)
    x_low, x_high = both_sides(up, down, along_x)
    copies, = call(
        next_kernel, 8,
        [(count_x * chips, 4, 128)],
        [(6, 8, *full1)] + [(8, *full1)] * 4 + [(4, *full1)],
        k1, f1, flops=1500000000)

    mine = lax.all_to_all(copies, ("gx", "chip"), 0, 0).reshape(-1, 128)
    other = lax.ppermute(mine, "core", [(0, 1), (1, 0)])

    own, = call(pack_share_kernel, 4, [(26, *tile1)], [], k1, f1, x_low, x_high)
    y_low, y_high = both_sides(own, own, along_y)
    prepared = call(
        prepare_kernel, 16,
        [(6, 16, *full1)] + [(16, *full1)] * 2 + [(6, 16, *half)] + [(16, *half)] * 3,
        [(16, *full1)] * 3 + [(16, *half)],
        x_low, x_high, y_low, own, y_high, k0, f0, flops=2500000000)

    place = jnp.stack([lax.axis_index("gx"), lax.axis_index(("chip", "core"))]).astype(jnp.int32)
    plane2 = (2, count_y // 2, 128)
    padded = (2 * count_x + 8, *plane2)
    near_e, = call(
        make_coarse_kernel(count_x, count_y), 20,
        [(6, 16, 128)],
        [padded, (6, *padded)] + [padded] * 5
        + [(2 * count_x, *plane2), (6, count_x // 4, *plane2), (count_x // 4, *plane2), (10, *plane2)],
        place, mine, other, scalars=1, flops=6000000000)

    correction, residual = call(
        post_kernel, 16,
        [f.shape, f.shape],
        [(16, *full1)] * 3 + [(8, *full1)] + [(16, *half)] * 4,
        near_e, *prepared)
    return correction, residual


def solution(mesh):
    shape = (mesh.shape["gx"], mesh.shape["gy"] // 2, 2)
    mesh = jax.sharding.Mesh(mesh.devices.reshape(shape), ("gx", "chip", "core"))
    spec = P("gx", ("chip", "core"), None)
    return jax.shard_map(body, mesh=mesh, in_specs=(spec, spec), out_specs=(spec, spec), check_vma=False)
```

```python
import math

import jax
import jax.numpy as jnp
from jax import lax
from jax.experimental import pallas as pl
from jax.experimental.pallas import tpu as pltpu
from jax.sharding import PartitionSpec as P

INTERPRET = False
COARSE_STEPS = 8
F32 = jnp.float32
HIGHEST = lax.Precision.HIGHEST
MIB = 1024 * 1024


def step_factors(low_end, steps):
    center, radius = 0.5 * (2.0 + low_end), 0.5 * (2.0 - low_end)
    sigma = center / radius
    ratio = 1.0 / sigma
    factors = [(0.0, 1.0 / center)]
    for _ in range(steps - 1):
        ratio_next = 1.0 / (2.0 * sigma - ratio)
        factors.append((ratio_next * ratio, 2.0 * ratio_next / radius))
        ratio = ratio_next
    return factors


(_, FIRST), (KEEP, ADD) = step_factors(0.4, 2)
COARSE_FACTORS = step_factors(0.02, COARSE_STEPS)


def iota(shape, dim):
    return lax.broadcasted_iota(jnp.int32, shape, dim)


def shifted(value, step, axis):
    return pltpu.roll(value, (-step) % value.shape[axis], axis)


def dot(a, b):
    return jnp.dot(a, b, precision=HIGHEST, preferred_element_type=F32)


def ones_where(condition):
    return jnp.where(condition, 1.0, 0.0).astype(F32)


def blocks(first, last, size, step):
    count = (last - first) // size
    assert first + count * size == last
    if count == 1:
        step(first)
        return

    def one(number, carry):
        step(first + number * size)
        return carry

    lax.fori_loop(0, count, one, 0)


def near(ref, start, size):
    here = ref[pl.ds(start, size)]
    return (ref[pl.ds(start - 1, size)], ref[pl.ds(start + 1, size)],
            shifted(here, -1, 1), shifted(here, 1, 1), shifted(here, -1, 2), shifted(here, 1, 2))


def near_inside(ref, start, size):
    x_low, x_high, y_low, y_high, z_low, z_high = near(ref, start, size)
    lane = iota(z_low.shape, 2)
    z_low = jnp.where(lane == 0, 0.0, z_low)
    z_high = jnp.where(lane == z_low.shape[2] - 1, 0.0, z_high)
    return x_low, x_high, y_low, y_high, z_low, z_high


def coupling(center, around, masked):
    total = 6.0 * center
    for value in around:
        total = total + value
    inside = center > 0.0
    half_inverse = jnp.where(inside, 1.0 / jnp.where(inside, total, 1.0), 0.0)
    couplings = []
    for number, value in enumerate(around):
        c = (center + value) * half_inverse
        couplings.append(jnp.where(value > 0.0, c, 0.0) if number in masked else c)
    return couplings, 2.0 * half_inverse, 0.5 * total


def pick(c_ref, number, where):
    return c_ref.at[number][where] if where else c_ref[number]


def spread(c_ref, where, around):
    total = pick(c_ref, 0, where) * around[0]
    for number in range(1, 6):
        total = total + pick(c_ref, number, where) * around[number]
    return total


PAIRS = ([("k", dx, 7 - dx) for dx in (1, 2, 3)], [("f", dx, 6 - dx) for dx in (1, 2, 3)])
Y_TILES = 28


def pack_x_kernel(k_ref, f_ref, up_ref, down_ref, own_ref, done):
    pieces = ((k_ref, 1, up_ref, 0, 7), (f_ref, 2, up_ref, 7, 6), (k_ref, 0, down_ref, 0, 7), (f_ref, 0, down_ref, 7, 6),
              (k_ref, 0, own_ref, 0, 8), (f_ref, 0, own_ref, 8, 8))
    copies = [pltpu.make_async_copy(ref.at[pl.ds(first, size)], to.at[pl.ds(place, size)], done.at[number])
              for number, (ref, first, to, place, size) in enumerate(pieces)]
    for copy in copies:
        copy.start()
    for copy in copies:
        copy.wait()


def pair_tiles():
    tile = 16
    for pairs in PAIRS:
        for side in ("low", "high"):
            for name, dx, far in pairs:
                yield tile, name, side, dx, far
                tile += 1


def halo_plane(name, side, dx, low_ref, high_ref):
    reach = 7 if name == "k" else 6
    base = 0 if name == "k" else 7
    return low_ref[base + reach - dx] if side == "low" else high_ref[base + dx - 1]


def pack_y_kernel(own_ref, low_ref, high_ref, up_ref, down_ref):
    for ref in (up_ref, down_ref):
        ref[0:16] = own_ref[...]
    row = iota((8, own_ref.shape[2]), 0)
    for tile, name, side, dx, far in pair_tiles():
        near_plane = halo_plane(name, side, dx, low_ref, high_ref)
        far_plane = halo_plane(name, side, far, low_ref, high_ref)
        up_ref[tile] = jnp.where(row < dx, shifted(far_plane, 8 - dx, 0), near_plane)
        down_ref[tile] = jnp.where(row >= 8 - dx, shifted(far_plane, dx - 8, 0), near_plane)


def unpack(own_ref, x_low_ref, x_high_ref, y_low_ref, y_high_ref, k0, f0):
    for to, base, reach, name in ((k0, 0, 7, "k"), (f0, 8, 6, "f")):
        to[reach:reach + 8, 0:8] = y_low_ref[base:base + 8]
        to[reach:reach + 8, 8:16] = own_ref[base:base + 8]
        to[reach:reach + 8, 16:24] = y_high_ref[base:base + 8]
        first = 0 if name == "k" else 7
        to[0:reach, 8:16] = x_low_ref[first:first + reach]
        to[reach + 8:2 * reach + 8, 8:16] = x_high_ref[first:first + reach]
        for plane in (0, 2 * reach + 7):
            to[plane, 0:8] = jnp.zeros(own_ref.shape[1:], F32)
            to[plane, 16:24] = jnp.zeros(own_ref.shape[1:], F32)
    for tile, name, side, dx, far in pair_tiles():
        to, reach = (k0, 7) if name == "k" else (f0, 6)
        near_plane = reach - dx if side == "low" else reach + 7 + dx
        far_plane = reach - far if side == "low" else reach + 7 + far
        below, above = y_low_ref[tile], y_high_ref[tile]
        to[near_plane, 0:8] = below
        to[near_plane, 16:24] = above
        if far != dx:
            to[far_plane, 0:8] = shifted(below, dx - 8, 0)
            to[far_plane, 16:24] = shifted(above, 8 - dx, 0)


def fine_kernel(own_ref, x_low_ref, x_high_ref, y_low_ref, y_high_ref,
                k0, f0, k1, f1, up_ref, down_ref,
                c0, diag0, g0, d0, e0, sums, zsums):
    unpack(own_ref, x_low_ref, x_high_ref, y_low_ref, y_high_ref, k0, f0)

    def setup(start):
        at = pl.ds(start, 2)
        couplings, inverse, diagonal = coupling(k0[pl.ds(start + 1, 2)], near_inside(k0, start + 1, 2), (4, 5))
        for number in range(6):
            c0.at[number][at] = couplings[number]
        diag0[at] = diagonal
        scaled = inverse * f0[at]
        g0[at] = scaled
        d0[at] = FIRST * scaled

    blocks(0, 20, 2, setup)

    def second(start):
        at = pl.ds(start, 2)
        here = d0[at]
        scaled = g0[at] - here + spread(c0, (at,), near(d0, start, 2))
        g0[at] = scaled
        e0[at] = KEEP * here + ADD * scaled

    blocks(1, 19, 2, second)

    def left(start):
        at = pl.ds(start, 2)
        rest = diag0[at] * (g0[at] - e0[at] + spread(c0, (at,), near(e0, start, 2)))
        sums[start // 2 - 1] = 0.5 * (rest[0] + rest[1])

    blocks(2, 18, 2, left)
    for index in range(10):
        sums[index + 8] = 0.125 * (k0[2 * index + 1] + k0[2 * index + 2])
    fold = ones_where(iota((256, 128), 0) // 2 == iota((256, 128), 1))
    zsums[...] = dot(sums[...].reshape(18 * 24, 256), fold).reshape(18, 24, 128)

    k1[...] = jnp.zeros_like(k1)
    f1[...] = jnp.zeros_like(f1)
    rows = zsums[:, pl.ds(0, 12, stride=2), :] + zsums[:, pl.ds(1, 12, stride=2), :]
    f1[:, 2:14, :] = rows[0:8]
    k1[:, 2:14, :] = rows[8:18]
    up_ref[0:6] = k1[1:7, 4:12, :]
    up_ref[6:11] = f1[1:6, 4:12, :]
    down_ref[0:6] = k1[3:9, 4:12, :]
    down_ref[6:11] = f1[2:7, 4:12, :]


def next_kernel(k1, f1, copies_ref, c1, diag1, g1, d1, e1, out):
    def setup1(start):
        at = pl.ds(start, 4)
        couplings, inverse, diagonal = coupling(k1[pl.ds(start + 1, 4)], near_inside(k1, start + 1, 4), (4, 5))
        for number in range(6):
            c1.at[number][at] = couplings[number]
        diag1[at] = diagonal
        scaled = inverse * f1[at]
        g1[at] = scaled
        d1[at] = FIRST * scaled

    blocks(0, 8, 4, setup1)
    at = pl.ds(1, 6)
    scaled = g1[at] - d1[at] + spread(c1, (at,), near(d1, 1, 6))
    g1[at] = scaled
    e1[at] = KEEP * d1[at] + ADD * scaled
    at = pl.ds(2, 4)
    rest = diag1[at] * (g1[at] - e1[at] + spread(c1, (at,), near(e1, 2, 4)))
    for half in range(2):
        out[half] = 0.5 * (rest[2 * half] + rest[2 * half + 1])
        out[half + 2] = 0.125 * (k1[2 * half + 3] + k1[2 * half + 4])
    row, lane = iota((128, 256), 0), iota((128, 256), 1)
    fold = ones_where((lane == row // 2) | (lane == 192 + row // 2))
    folded = dot(out[...].reshape(64, 128), fold).reshape(4, 16, 256)
    lines = [folded[number, 6:7, 0:128] + folded[number, 7:8, 0:128]
             + folded[number, 8:9, 128:256] + folded[number, 9:10, 128:256] for number in range(4)]
    payload = jnp.concatenate(lines, 0)

    def copy(start):
        copies_ref[pl.ds(start, 8)] = jnp.broadcast_to(payload[None], (8, 4, 128))

    blocks(0, copies_ref.shape[0], 8, copy)


def near2(ref, start, size):
    here = ref[pl.ds(start, size)]
    below, above = ref[pl.ds(start - 1, size)], ref[pl.ds(start + 1, size)]
    z_low, z_high = shifted(here, -1, 3), shifted(here, 1, 3)
    turned = shifted(here, 64, 3)
    turned0, turned1 = turned[:, 0:1], turned[:, 1:2]
    first = iota(turned0.shape, 3) < 64
    y_high = [jnp.where(first, turned0, turned1), jnp.where(first, turned1, shifted(turned0, 1, 2))]
    y_low = [jnp.where(first, shifted(turned1, -1, 2), turned0), jnp.where(first, turned0, turned1)]
    return below, above, jnp.concatenate(y_low, 1), jnp.concatenate(y_high, 1), z_low, z_high


def near2_inside(ref, start, size):
    x_low, x_high, y_low, y_high, z_low, z_high = near2(ref, start, size)
    core, row, lane = (iota(z_low.shape, dim) for dim in (1, 2, 3))
    last = z_low.shape[2] - 1
    y_low = jnp.where((core == 0) & (row == 0) & (lane < 64), 0.0, y_low)
    y_high = jnp.where((core == 1) & (row == last) & (lane >= 64), 0.0, y_high)
    z_low = jnp.where(lane % 64 == 0, 0.0, z_low)
    z_high = jnp.where(lane % 64 == 63, 0.0, z_high)
    return x_low, x_high, y_low, y_high, z_low, z_high


def near3(value):
    count = value.shape[0]
    before, after = shifted(value[count - 1:], -32, 3), shifted(value[0:1], 32, 3)
    x_low = jnp.concatenate([before, value[:count - 1]], 0) if count > 1 else before
    x_high = jnp.concatenate([value[1:], after], 0) if count > 1 else after
    core0, core1 = value[:, 0:1], value[:, 1:2]
    y_low = jnp.concatenate([shifted(core1, -1, 2), core0], 1)
    y_high = jnp.concatenate([core1, shifted(core0, 1, 2)], 1)
    return x_low, x_high, y_low, y_high, shifted(value, -1, 3), shifted(value, 1, 3)


def near3_inside(value):
    x_low, x_high, y_low, y_high, z_low, z_high = near3(value)
    plane, core, row, lane = (iota(value.shape, dim) for dim in range(4))
    count, rows = value.shape[0], value.shape[2]
    x_low = jnp.where((plane == 0) & (lane < 32), 0.0, x_low)
    x_high = jnp.where((plane == count - 1) & (lane >= 96), 0.0, x_high)
    y_low = jnp.where((core == 0) & (row == 0), 0.0, y_low)
    y_high = jnp.where((core == 1) & (row == rows - 1), 0.0, y_high)
    z_low = jnp.where(lane % 32 == 0, 0.0, z_low)
    z_high = jnp.where(lane % 32 == 31, 0.0, z_high)
    return x_low, x_high, y_low, y_high, z_low, z_high


def make_coarse_kernel(count_x, count_y):
    planes2, rows, count3 = 2 * count_x, count_y // 2, count_x // 4
    size = 8
    line = (2, rows, 128)

    def coarse_kernel(place_ref, mine_ref, other_ref, near_ref,
                      k2, c2, diag2, g2, d2, e2, h2, sums, c3, e3, x0):
        at_x, at_y = place_ref[0], place_ref[1]
        zero = jnp.zeros((4, *line), F32)
        for ends in (pl.ds(0, 4), pl.ds(planes2 + 4, 4)):
            for ref in (k2, g2, d2, e2):
                ref[ends] = zero
            for number in range(6):
                c2.at[number][ends] = zero

        core = at_y % 2

        def load(index):
            for half in range(2):
                start = index * (4 * rows) + half
                to = 2 * index + half + 4
                for ref, side in ((mine_ref, core), (other_ref, 1 - core)):
                    k2[to, side] = ref[pl.ds(start + 2, rows, stride=4), :]
                    e2[to, side] = ref[pl.ds(start, rows, stride=4), :]

        def load_some(start):
            for index in range(4):
                load(start + index)

        blocks(0, count_x, 4, load_some)

        def setup(start):
            at = pl.ds(start, size)
            couplings, inverse, diagonal = coupling(k2[at], near2_inside(k2, start, size), (2, 3, 4, 5))
            for number in range(6):
                c2.at[number][at] = couplings[number]
            diag2[at] = diagonal
            scaled = inverse * e2[at]
            g2[at] = scaled
            d2[at] = FIRST * scaled

        blocks(4, planes2 + 4, size, setup)

        def second(start):
            at = pl.ds(start, size)
            here = d2[at]
            scaled = g2[at] - here + spread(c2, (at,), near2(d2, start, size))
            h2[at] = scaled
            e2[at] = KEEP * here + ADD * scaled

        blocks(4, planes2 + 4, size, second)

        def left(start):
            at = pl.ds(start, size)
            rest = diag2[at] * (h2[at] - e2[at] + spread(c2, (at,), near2(e2, start, size)))
            rest = rest.reshape(size // 2, 2, *line)
            here = k2[at].reshape(size // 2, 2, *line)
            to = (start - 4) // 2
            sums[pl.ds(to, size // 2)] = 0.5 * (rest[:, 0] + rest[:, 1])
            sums[pl.ds(to + count_x, size // 2)] = 0.125 * (here[:, 0] + here[:, 1])

        blocks(4, planes2 + 4, size, left)

        flat = count3 * 2 * rows
        f3 = jnp.zeros((flat, 128), F32)
        k3 = jnp.zeros((flat, 128), F32)
        row, lane = iota((128, 128), 0), iota((128, 128), 1)
        for quarter in range(4):
            fold = ones_where(lane == 32 * quarter + (row % 64) // 2)
            f3 = f3 + dot(sums[pl.ds(quarter * count3, count3)].reshape(flat, 128), fold)
            k3 = k3 + dot(sums[pl.ds(count_x + quarter * count3, count3)].reshape(flat, 128), fold)
        f3 = f3.reshape(count3, *line)
        k3 = k3.reshape(count3, *line)
        couplings, inverse, _ = coupling(k3, near3_inside(k3), (0, 1, 2, 3, 4, 5))
        for number in range(6):
            c3[number] = couplings[number]
        scaled = inverse * f3
        step = COARSE_FACTORS[0][1] * scaled
        total = step
        for keep, add in COARSE_FACTORS[1:]:
            scaled = scaled - step + spread(c3, (), near3(step))
            step = keep * step + add * scaled
            total = total + step
        e3[...] = total

        base = 2 * at_x
        parts = []
        for number in range(5):
            x3 = at_x - 2 + number
            inside = (x3 >= 0) & (x3 < count_x)
            safe = jnp.clip(x3, 0, count_x - 1)
            plane = pltpu.roll(e3[safe % count3].reshape(2 * rows, 128), (128 - 32 * (safe // count3)) % 128, 1)
            parts.append(jnp.where(inside, plane, 0.0))
        unfold = ones_where((row < 32) & ((lane % 64) // 2 == row))
        up = dot(jnp.concatenate(parts, 0), unfold).reshape(5, *line)
        local = pl.ds(base, 10)
        twice = jnp.stack([up, up], 1).reshape(10, *line)
        x0[...] = d2[local] + e2[local] + twice
        inner = pl.ds(base + 1, 8)
        scaled = g2[inner] - x0[1:9] + spread(c2, (inner,), near2(x0, 1, 8))
        h2[0:8] = scaled
        d2[0:8] = FIRST * scaled
        inner = pl.ds(base + 2, 6)
        here = d2[1:7]
        scaled = h2[1:7] - here + spread(c2, (inner,), near2(d2, 1, 6))
        found = x0[2:8] + (1.0 + KEEP) * here + ADD * scaled

        row, lane = iota((128, 256), 0), iota((128, 256), 1)
        widen = ones_where(row == 64 * (lane // 128) + (lane % 128) // 2)
        wide = dot(found.reshape(6 * 2 * rows, 128), widen)
        target, source = iota((16, 2 * rows), 0), iota((16, 2 * rows), 1)
        source = 2 * (source % rows) + source // rows
        inside = (target >= 2) & (target < 14) & (source == at_y - 1 + (target - 2) // 4)
        first = ones_where(inside & ((target - 2) % 4 < 2))
        other = ones_where(inside & ((target - 2) % 4 >= 2))
        for index in range(6):
            block = wide[index * 2 * rows:(index + 1) * 2 * rows]
            near_ref[index] = dot(first, block[:, 0:128]) + dot(other, block[:, 128:256])

    return coarse_kernel


def pack_share_kernel(k1, f1, low_ref, high_ref, out_ref):
    out_ref[0:5] = low_ref[1:6]
    out_ref[5:9] = k1[3:7, 4:12, :]
    out_ref[9:14] = high_ref[0:5]
    out_ref[14:18] = low_ref[7:11]
    out_ref[18:22] = f1[2:6, 4:12, :]
    out_ref[22:26] = high_ref[6:10]


def prepare_kernel(k_ref, f_ref, c0, diag0, g0, x0, d0):
    def setup0(start):
        def cut(value):
            return shifted(value, 4, 1)[:, 0:16]

        at = pl.ds(start, 2)
        couplings, inverse, diagonal = coupling(k_ref[pl.ds(start + 3, 2)], near_inside(k_ref, start + 3, 2), (4, 5))
        for number in range(6):
            c0.at[number][at] = cut(couplings[number])
        diag0[at] = cut(diagonal)
        scaled = cut(inverse * f_ref[pl.ds(start + 2, 2)])
        g0[at] = scaled
        d0[at] = FIRST * scaled

    blocks(0, 16, 2, setup0)

    def guess0(start):
        at = pl.ds(start, 2)
        here = d0[at]
        scaled = g0[at] - here + spread(c0, (at,), near(d0, start, 2))
        x0[at] = (1.0 + KEEP) * here + ADD * scaled

    blocks(1, 15, 2, guess0)


def gate_kernel(*refs):
    pass


def post_kernel(near_ref, x_low_ref, x_high_ref, y_low_ref, own_ref, y_high_ref, c0, diag0, g0, x0,
                correction_ref, residual_ref,
                k1, f1, c1, g1, x1, y1, d1, h1, wide, y0, d0, h0, v0):
    row = iota((8, 128), 0)

    def join(low, middle, high):
        middle = shifted(middle, 4, 1)
        return jnp.concatenate([jnp.where(row < 6, low, middle), jnp.where(row < 2, middle, high)], 1)

    zero = jnp.zeros((1, 8, 128), F32)
    k1[1:15] = join(y_low_ref[0:14], own_ref[0:14], y_high_ref[0:14])
    f1[2:14] = join(y_low_ref[14:26], own_ref[14:26], y_high_ref[14:26])
    for to, plane, tile in ((k1, 0, x_low_ref[0:1]), (k1, 15, x_high_ref[5:6]),
                            (f1, 1, x_low_ref[6:7]), (f1, 14, x_high_ref[10:11])):
        to[plane:plane + 1] = join(zero, tile, zero)

    def setup1(start):
        at = pl.ds(start, 7)
        couplings, inverse, _ = coupling(k1[at], near_inside(k1, start, 7), (4, 5))
        for number in range(6):
            c1.at[number][at] = couplings[number]
        scaled = inverse * f1[at]
        g1[at] = scaled
        d1[at] = FIRST * scaled

    blocks(1, 15, 7, setup1)

    def guess1(start):
        at = pl.ds(start, 6)
        here = d1[at]
        scaled = g1[at] - here + spread(c1, (at,), near(d1, start, 6))
        x1[at] = (1.0 + KEEP) * here + ADD * scaled

    blocks(2, 14, 6, guess1)

    up = near_ref[...]
    y1[2:14] = x1[2:14] + jnp.stack([up, up], 1).reshape(12, 16, 128)
    scaled = g1[3:13] - y1[3:13] + spread(c1, (pl.ds(3, 10),), near(y1, 3, 10))
    h1[3:13] = scaled
    d1[3:13] = FIRST * scaled
    here = d1[4:12]
    scaled = h1[4:12] - here + spread(c1, (pl.ds(4, 8),), near(d1, 4, 8))
    found = y1[4:12] + (1.0 + KEEP) * here + ADD * scaled
    wide[:, pl.ds(0, 8, stride=2), :] = found[:, 4:12]
    wide[:, pl.ds(1, 8, stride=2), :] = found[:, 4:12]
    unfold = ones_where(iota((128, 256), 0) == iota((128, 256), 1) // 2)
    up = dot(wide[...].reshape(128, 128), unfold).reshape(8, 16, 256)

    for index in range(1, 15):
        y0[index] = x0[index] + up[index // 2]

    def first0(start):
        at = pl.ds(start, 3)
        scaled = g0[at] - y0[at] + spread(c0, (at,), near(y0, start, 3))
        h0[at] = scaled
        d0[at] = FIRST * scaled

    blocks(2, 14, 3, first0)

    def second0(start):
        at = pl.ds(start, 2)
        here = d0[at]
        scaled = h0[at] - here + spread(c0, (at,), near(d0, start, 2))
        h0[at] = scaled
        v0[at] = KEEP * here + ADD * scaled

    blocks(3, 13, 2, second0)

    def last0(start):
        at, to = pl.ds(start, 2), pl.ds(start - 4, 2)
        here = v0[at]
        correction_ref[to] = (y0[at] + d0[at] + here)[:, 4:12]
        scaled = h0[at] - here + spread(c0, (at,), near(v0, start, 2))
        residual_ref[to] = (diag0[at] * scaled)[:, 4:12]

    blocks(4, 12, 2, last0)


def call(kernel, limit, shapes, scratch, *operands, scalars=0, flops=0):
    specs = [pl.BlockSpec(memory_space=pltpu.SMEM)] * scalars
    specs += [pl.BlockSpec(memory_space=pltpu.VMEM)] * (len(operands) - scalars)
    return pl.pallas_call(
        kernel,
        out_shape=[jax.ShapeDtypeStruct(shape, F32) for shape in shapes],
        in_specs=specs,
        out_specs=[pl.BlockSpec(memory_space=pltpu.VMEM)] * len(shapes),
        scratch_shapes=[pltpu.VMEM(shape, F32) for shape in scratch],
        compiler_params=pltpu.CompilerParams(vmem_limit_bytes=limit * MIB),
        cost_estimate=pl.CostEstimate(flops=flops, bytes_accessed=0, transcendentals=0) if flops else None,
        interpret=INTERPRET,
    )(*operands)


def both_sides(up, down, axes):
    count = math.prod(lax.axis_size(axis) for axis in axes)
    low = lax.ppermute(up, axes, [(i, i + 1) for i in range(count - 1)])
    high = lax.ppermute(down, axes, [(i + 1, i) for i in range(count - 1)])
    return low, high


def body(f, k):
    count_x, chips = lax.axis_size("gx"), lax.axis_size("chip")
    count_y = 2 * chips
    along_x, along_y = ("gx",), ("chip", "core")
    tile, full, half = f.shape[1:], (24, 256), (16, 256)
    tile1, full1 = (8, 128), (16, 128)
    up, down, own = pl.pallas_call(
        pack_x_kernel,
        out_shape=[jax.ShapeDtypeStruct((planes, *tile), F32) for planes in (13, 13, 16)],
        in_specs=[pl.BlockSpec(memory_space=pltpu.HBM)] * 2,
        out_specs=[pl.BlockSpec(memory_space=pltpu.VMEM)] * 3,
        scratch_shapes=[pltpu.SemaphoreType.DMA((6,))],
        compiler_params=pltpu.CompilerParams(vmem_limit_bytes=4 * MIB),
        interpret=INTERPRET,
    )(k, f)
    x_low, x_high = both_sides(up, down, along_x)
    up, down = call(pack_y_kernel, 4, [(Y_TILES, *tile)] * 2, [], own, x_low, x_high)
    y_low, y_high = both_sides(up, down, along_y)

    k0, f0, k1, f1, up, down = call(
        fine_kernel, 16,
        [(22, *full), (20, *full), (10, *full1), (8, *full1), (11, *tile1), (11, *tile1)],
        [(6, 20, *full)] + [(20, *full)] * 4 + [(18, *full), (18, 24, 128)],
        own, x_low, x_high, y_low, y_high)
    x_low, x_high = both_sides(up, down, along_x)
    copies, = call(
        next_kernel, 8,
        [(count_x * chips, 4, 128)],
        [(6, 8, *full1)] + [(8, *full1)] * 4 + [(4, *full1)],
        k1, f1)

    prepared = call(
        prepare_kernel, 16,
        [(6, 16, *half)] + [(16, *half)] * 3,
        [(16, *half)],
        k0, f0)

    mine = lax.all_to_all(copies, ("gx", "chip"), 0, 0).reshape(-1, 128)
    mine = pl.pallas_call(
        gate_kernel,
        out_shape=jax.ShapeDtypeStruct(mine.shape, F32),
        in_specs=[pl.BlockSpec(memory_space=pl.ANY)] * 4,
        out_specs=pl.BlockSpec(memory_space=pl.ANY),
        input_output_aliases={0: 0},
        interpret=INTERPRET,
    )(mine, x_low, x_high, prepared[0])
    other = lax.ppermute(mine, "core", [(0, 1), (1, 0)])

    own, = call(pack_share_kernel, 4, [(26, *tile1)], [], k1, f1, x_low, x_high)
    y_low, y_high = both_sides(own, own, along_y)

    place = jnp.stack([lax.axis_index("gx"), lax.axis_index(("chip", "core"))]).astype(jnp.int32)
    plane2 = (2, count_y // 2, 128)
    padded = (2 * count_x + 8, *plane2)
    near_e, = call(
        make_coarse_kernel(count_x, count_y), 20,
        [(6, 16, 128)],
        [padded, (6, *padded)] + [padded] * 5
        + [(2 * count_x, *plane2), (6, count_x // 4, *plane2), (count_x // 4, *plane2), (10, *plane2)],
        place, mine, other, scalars=1, flops=6000000000)

    correction, residual = call(
        post_kernel, 16,
        [f.shape, f.shape],
        [(16, *full1)] * 2 + [(6, 16, *full1)] + [(16, *full1)] * 5 + [(8, *full1)] + [(16, *half)] * 4,
        near_e, x_low, x_high, y_low, own, y_high, *prepared)
    return correction, residual


def solution(mesh):
    shape = (mesh.shape["gx"], mesh.shape["gy"] // 2, 2)
    mesh = jax.sharding.Mesh(mesh.devices.reshape(shape), ("gx", "chip", "core"))
    spec = P("gx", ("chip", "core"), None)
    return jax.shard_map(body, mesh=mesh, in_specs=(spec, spec), out_specs=(spec, spec), check_vma=False)
```

```python
import math

import jax
import jax.numpy as jnp
from jax import lax
from jax.experimental import pallas as pl
from jax.experimental.pallas import tpu as pltpu
from jax.sharding import PartitionSpec as P

INTERPRET = False
COARSE_STEPS = 8
F32 = jnp.float32
HIGHEST = lax.Precision.HIGHEST
MIB = 1024 * 1024


def step_factors(low_end, steps):
    center, radius = 0.5 * (2.0 + low_end), 0.5 * (2.0 - low_end)
    sigma = center / radius
    ratio = 1.0 / sigma
    factors = [(0.0, 1.0 / center)]
    for _ in range(steps - 1):
        ratio_next = 1.0 / (2.0 * sigma - ratio)
        factors.append((ratio_next * ratio, 2.0 * ratio_next / radius))
        ratio = ratio_next
    return factors


(_, FIRST), (KEEP, ADD) = step_factors(0.4, 2)
COARSE_FACTORS = step_factors(0.02, COARSE_STEPS)


def iota(shape, dim):
    return lax.broadcasted_iota(jnp.int32, shape, dim)


def shifted(value, step, axis):
    return pltpu.roll(value, (-step) % value.shape[axis], axis)


def dot(a, b):
    return jnp.dot(a, b, precision=HIGHEST, preferred_element_type=F32)


def ones_where(condition):
    return jnp.where(condition, 1.0, 0.0).astype(F32)


def blocks(first, last, size, step):
    count = (last - first) // size
    assert first + count * size == last
    if count == 1:
        step(first)
        return

    def one(number, carry):
        step(first + number * size)
        return carry

    lax.fori_loop(0, count, one, 0)


def near(ref, start, size):
    here = ref[pl.ds(start, size)]
    return (ref[pl.ds(start - 1, size)], ref[pl.ds(start + 1, size)],
            shifted(here, -1, 1), shifted(here, 1, 1), shifted(here, -1, 2), shifted(here, 1, 2))


def near_inside(ref, start, size):
    x_low, x_high, y_low, y_high, z_low, z_high = near(ref, start, size)
    lane = iota(z_low.shape, 2)
    z_low = jnp.where(lane == 0, 0.0, z_low)
    z_high = jnp.where(lane == z_low.shape[2] - 1, 0.0, z_high)
    return x_low, x_high, y_low, y_high, z_low, z_high


def coupling(center, around, masked):
    total = 6.0 * center
    for value in around:
        total = total + value
    inside = center > 0.0
    half_inverse = jnp.where(inside, 1.0 / jnp.where(inside, total, 1.0), 0.0)
    couplings = []
    for number, value in enumerate(around):
        c = (center + value) * half_inverse
        couplings.append(jnp.where(value > 0.0, c, 0.0) if number in masked else c)
    return couplings, 2.0 * half_inverse, 0.5 * total


def pick(c_ref, number, where):
    return c_ref.at[number][where] if where else c_ref[number]


def spread(c_ref, where, around):
    total = pick(c_ref, 0, where) * around[0]
    for number in range(1, 6):
        total = total + pick(c_ref, number, where) * around[number]
    return total


PAIRS = ([("k", dx, 7 - dx) for dx in (1, 2, 3)], [("f", dx, 6 - dx) for dx in (1, 2, 3)])
Y_TILES = 28


def pack_x_kernel(k_ref, f_ref, up_ref, down_ref, own_ref, done):
    pieces = ((k_ref, 1, up_ref, 0, 7), (f_ref, 2, up_ref, 7, 6), (k_ref, 0, down_ref, 0, 7), (f_ref, 0, down_ref, 7, 6),
              (k_ref, 0, own_ref, 0, 8), (f_ref, 0, own_ref, 8, 8))
    copies = [pltpu.make_async_copy(ref.at[pl.ds(first, size)], to.at[pl.ds(place, size)], done.at[number])
              for number, (ref, first, to, place, size) in enumerate(pieces)]
    for copy in copies:
        copy.start()
    for copy in copies:
        copy.wait()


def pair_tiles():
    tile = 16
    for pairs in PAIRS:
        for side in ("low", "high"):
            for name, dx, far in pairs:
                yield tile, name, side, dx, far
                tile += 1


def halo_plane(name, side, dx, low_ref, high_ref):
    reach = 7 if name == "k" else 6
    base = 0 if name == "k" else 7
    return low_ref[base + reach - dx] if side == "low" else high_ref[base + dx - 1]


def pack_y_kernel(own_ref, low_ref, high_ref, up_ref, down_ref):
    for ref in (up_ref, down_ref):
        ref[0:16] = own_ref[...]
    row = iota((8, own_ref.shape[2]), 0)
    for tile, name, side, dx, far in pair_tiles():
        near_plane = halo_plane(name, side, dx, low_ref, high_ref)
        far_plane = halo_plane(name, side, far, low_ref, high_ref)
        up_ref[tile] = jnp.where(row < dx, shifted(far_plane, 8 - dx, 0), near_plane)
        down_ref[tile] = jnp.where(row >= 8 - dx, shifted(far_plane, dx - 8, 0), near_plane)


def unpack(own_ref, x_low_ref, x_high_ref, y_low_ref, y_high_ref, k0, f0):
    for to, base, reach, name in ((k0, 0, 7, "k"), (f0, 8, 6, "f")):
        to[reach:reach + 8, 0:8] = y_low_ref[base:base + 8]
        to[reach:reach + 8, 8:16] = own_ref[base:base + 8]
        to[reach:reach + 8, 16:24] = y_high_ref[base:base + 8]
        first = 0 if name == "k" else 7
        to[0:reach, 8:16] = x_low_ref[first:first + reach]
        to[reach + 8:2 * reach + 8, 8:16] = x_high_ref[first:first + reach]
        for plane in (0, 2 * reach + 7):
            to[plane, 0:8] = jnp.zeros(own_ref.shape[1:], F32)
            to[plane, 16:24] = jnp.zeros(own_ref.shape[1:], F32)
    for tile, name, side, dx, far in pair_tiles():
        to, reach = (k0, 7) if name == "k" else (f0, 6)
        near_plane = reach - dx if side == "low" else reach + 7 + dx
        far_plane = reach - far if side == "low" else reach + 7 + far
        below, above = y_low_ref[tile], y_high_ref[tile]
        to[near_plane, 0:8] = below
        to[near_plane, 16:24] = above
        if far != dx:
            to[far_plane, 0:8] = shifted(below, dx - 8, 0)
            to[far_plane, 16:24] = shifted(above, 8 - dx, 0)


def fine_kernel(own_ref, x_low_ref, x_high_ref, y_low_ref, y_high_ref,
                k0, f0, k1, f1, up_ref, down_ref, side_ref,
                c0, diag0, g0, d0, e0, sums, zsums):
    unpack(own_ref, x_low_ref, x_high_ref, y_low_ref, y_high_ref, k0, f0)

    def setup(start):
        at = pl.ds(start, 2)
        couplings, inverse, diagonal = coupling(k0[pl.ds(start + 1, 2)], near_inside(k0, start + 1, 2), (4, 5))
        for number in range(6):
            c0.at[number][at] = couplings[number]
        diag0[at] = diagonal
        scaled = inverse * f0[at]
        g0[at] = scaled
        d0[at] = FIRST * scaled

    blocks(0, 20, 2, setup)

    def second(start):
        at = pl.ds(start, 2)
        here = d0[at]
        scaled = g0[at] - here + spread(c0, (at,), near(d0, start, 2))
        g0[at] = scaled
        e0[at] = KEEP * here + ADD * scaled

    blocks(1, 19, 2, second)

    def left(start):
        at = pl.ds(start, 2)
        rest = diag0[at] * (g0[at] - e0[at] + spread(c0, (at,), near(e0, start, 2)))
        sums[start // 2 - 1] = 0.5 * (rest[0] + rest[1])

    blocks(2, 18, 2, left)
    for index in range(10):
        sums[index + 8] = 0.125 * (k0[2 * index + 1] + k0[2 * index + 2])
    fold = ones_where(iota((256, 128), 0) // 2 == iota((256, 128), 1))
    zsums[...] = dot(sums[...].reshape(18 * 24, 256), fold).reshape(18, 24, 128)

    k1[...] = jnp.zeros_like(k1)
    f1[...] = jnp.zeros_like(f1)
    rows = zsums[:, pl.ds(0, 12, stride=2), :] + zsums[:, pl.ds(1, 12, stride=2), :]
    f1[:, 2:14, :] = rows[0:8]
    k1[:, 2:14, :] = rows[8:18]
    up_ref[0:6] = k1[1:7, 4:12, :]
    up_ref[6:11] = f1[1:6, 4:12, :]
    down_ref[0:6] = k1[3:9, 4:12, :]
    down_ref[6:11] = f1[2:7, 4:12, :]
    side_ref[0:10] = k1[:, 4:12, :]
    side_ref[10:18] = f1[:, 4:12, :]


def next_kernel(k1, f1, copies_ref, c1, diag1, g1, d1, e1, out):
    def setup1(start):
        at = pl.ds(start, 4)
        couplings, inverse, diagonal = coupling(k1[pl.ds(start + 1, 4)], near_inside(k1, start + 1, 4), (4, 5))
        for number in range(6):
            c1.at[number][at] = couplings[number]
        diag1[at] = diagonal
        scaled = inverse * f1[at]
        g1[at] = scaled
        d1[at] = FIRST * scaled

    blocks(0, 8, 4, setup1)
    at = pl.ds(1, 6)
    scaled = g1[at] - d1[at] + spread(c1, (at,), near(d1, 1, 6))
    g1[at] = scaled
    e1[at] = KEEP * d1[at] + ADD * scaled
    at = pl.ds(2, 4)
    rest = diag1[at] * (g1[at] - e1[at] + spread(c1, (at,), near(e1, 2, 4)))
    for half in range(2):
        out[half] = 0.5 * (rest[2 * half] + rest[2 * half + 1])
        out[half + 2] = 0.125 * (k1[2 * half + 3] + k1[2 * half + 4])
    row, lane = iota((128, 256), 0), iota((128, 256), 1)
    fold = ones_where((lane == row // 2) | (lane == 192 + row // 2))
    folded = dot(out[...].reshape(64, 128), fold).reshape(4, 16, 256)
    lines = [folded[number, 6:7, 0:128] + folded[number, 7:8, 0:128]
             + folded[number, 8:9, 128:256] + folded[number, 9:10, 128:256] for number in range(4)]
    payload = jnp.concatenate(lines, 0)

    def copy(start):
        copies_ref[pl.ds(start, 8)] = jnp.broadcast_to(payload[None], (8, 4, 128))

    blocks(0, copies_ref.shape[0], 8, copy)


def near2(ref, start, size):
    here = ref[pl.ds(start, size)]
    below, above = ref[pl.ds(start - 1, size)], ref[pl.ds(start + 1, size)]
    z_low, z_high = shifted(here, -1, 3), shifted(here, 1, 3)
    turned = shifted(here, 64, 3)
    turned0, turned1 = turned[:, 0:1], turned[:, 1:2]
    first = iota(turned0.shape, 3) < 64
    y_high = [jnp.where(first, turned0, turned1), jnp.where(first, turned1, shifted(turned0, 1, 2))]
    y_low = [jnp.where(first, shifted(turned1, -1, 2), turned0), jnp.where(first, turned0, turned1)]
    return below, above, jnp.concatenate(y_low, 1), jnp.concatenate(y_high, 1), z_low, z_high


def near2_inside(ref, start, size):
    x_low, x_high, y_low, y_high, z_low, z_high = near2(ref, start, size)
    core, row, lane = (iota(z_low.shape, dim) for dim in (1, 2, 3))
    last = z_low.shape[2] - 1
    y_low = jnp.where((core == 0) & (row == 0) & (lane < 64), 0.0, y_low)
    y_high = jnp.where((core == 1) & (row == last) & (lane >= 64), 0.0, y_high)
    z_low = jnp.where(lane % 64 == 0, 0.0, z_low)
    z_high = jnp.where(lane % 64 == 63, 0.0, z_high)
    return x_low, x_high, y_low, y_high, z_low, z_high


def near3(value):
    count = value.shape[0]
    before, after = shifted(value[count - 1:], -32, 3), shifted(value[0:1], 32, 3)
    x_low = jnp.concatenate([before, value[:count - 1]], 0) if count > 1 else before
    x_high = jnp.concatenate([value[1:], after], 0) if count > 1 else after
    core0, core1 = value[:, 0:1], value[:, 1:2]
    y_low = jnp.concatenate([shifted(core1, -1, 2), core0], 1)
    y_high = jnp.concatenate([core1, shifted(core0, 1, 2)], 1)
    return x_low, x_high, y_low, y_high, shifted(value, -1, 3), shifted(value, 1, 3)


def near3_inside(value):
    x_low, x_high, y_low, y_high, z_low, z_high = near3(value)
    plane, core, row, lane = (iota(value.shape, dim) for dim in range(4))
    count, rows = value.shape[0], value.shape[2]
    x_low = jnp.where((plane == 0) & (lane < 32), 0.0, x_low)
    x_high = jnp.where((plane == count - 1) & (lane >= 96), 0.0, x_high)
    y_low = jnp.where((core == 0) & (row == 0), 0.0, y_low)
    y_high = jnp.where((core == 1) & (row == rows - 1), 0.0, y_high)
    z_low = jnp.where(lane % 32 == 0, 0.0, z_low)
    z_high = jnp.where(lane % 32 == 31, 0.0, z_high)
    return x_low, x_high, y_low, y_high, z_low, z_high


def make_coarse_kernel(count_x, count_y):
    planes2, rows, count3 = 2 * count_x, count_y // 2, count_x // 4
    size = 8
    line = (2, rows, 128)

    def coarse_kernel(place_ref, mine_ref, other_ref, near_ref,
                      k2, c2, diag2, g2, d2, e2, h2, sums, c3, e3, x0):
        at_x, at_y = place_ref[0], place_ref[1]
        zero = jnp.zeros((4, *line), F32)
        for ends in (pl.ds(0, 4), pl.ds(planes2 + 4, 4)):
            for ref in (k2, g2, d2, e2):
                ref[ends] = zero
            for number in range(6):
                c2.at[number][ends] = zero

        core = at_y % 2

        def load(index):
            for half in range(2):
                start = index * (4 * rows) + half
                to = 2 * index + half + 4
                for ref, side in ((mine_ref, core), (other_ref, 1 - core)):
                    k2[to, side] = ref[pl.ds(start + 2, rows, stride=4), :]
                    e2[to, side] = ref[pl.ds(start, rows, stride=4), :]

        def load_some(start):
            for index in range(4):
                load(start + index)

        blocks(0, count_x, 4, load_some)

        def setup(start):
            at = pl.ds(start, size)
            couplings, inverse, diagonal = coupling(k2[at], near2_inside(k2, start, size), (2, 3, 4, 5))
            for number in range(6):
                c2.at[number][at] = couplings[number]
            diag2[at] = diagonal
            scaled = inverse * e2[at]
            g2[at] = scaled
            d2[at] = FIRST * scaled

        blocks(4, planes2 + 4, size, setup)

        def second(start):
            at = pl.ds(start, size)
            here = d2[at]
            scaled = g2[at] - here + spread(c2, (at,), near2(d2, start, size))
            h2[at] = scaled
            e2[at] = KEEP * here + ADD * scaled

        blocks(4, planes2 + 4, size, second)

        def left(start):
            at = pl.ds(start, size)
            rest = diag2[at] * (h2[at] - e2[at] + spread(c2, (at,), near2(e2, start, size)))
            rest = rest.reshape(size // 2, 2, *line)
            here = k2[at].reshape(size // 2, 2, *line)
            to = (start - 4) // 2
            sums[pl.ds(to, size // 2)] = 0.5 * (rest[:, 0] + rest[:, 1])
            sums[pl.ds(to + count_x, size // 2)] = 0.125 * (here[:, 0] + here[:, 1])

        blocks(4, planes2 + 4, size, left)

        flat = count3 * 2 * rows
        f3 = jnp.zeros((flat, 128), F32)
        k3 = jnp.zeros((flat, 128), F32)
        row, lane = iota((128, 128), 0), iota((128, 128), 1)
        for quarter in range(4):
            fold = ones_where(lane == 32 * quarter + (row % 64) // 2)
            f3 = f3 + dot(sums[pl.ds(quarter * count3, count3)].reshape(flat, 128), fold)
            k3 = k3 + dot(sums[pl.ds(count_x + quarter * count3, count3)].reshape(flat, 128), fold)
        f3 = f3.reshape(count3, *line)
        k3 = k3.reshape(count3, *line)
        couplings, inverse, _ = coupling(k3, near3_inside(k3), (0, 1, 2, 3, 4, 5))
        for number in range(6):
            c3[number] = couplings[number]
        scaled = inverse * f3
        step = COARSE_FACTORS[0][1] * scaled
        total = step
        for keep, add in COARSE_FACTORS[1:]:
            scaled = scaled - step + spread(c3, (), near3(step))
            step = keep * step + add * scaled
            total = total + step
        e3[...] = total

        base = 2 * at_x
        parts = []
        for number in range(5):
            x3 = at_x - 2 + number
            inside = (x3 >= 0) & (x3 < count_x)
            safe = jnp.clip(x3, 0, count_x - 1)
            plane = pltpu.roll(e3[safe % count3].reshape(2 * rows, 128), (128 - 32 * (safe // count3)) % 128, 1)
            parts.append(jnp.where(inside, plane, 0.0))
        unfold = ones_where((row < 32) & ((lane % 64) // 2 == row))
        up = dot(jnp.concatenate(parts, 0), unfold).reshape(5, *line)
        local = pl.ds(base, 10)
        twice = jnp.stack([up, up], 1).reshape(10, *line)
        x0[...] = d2[local] + e2[local] + twice
        inner = pl.ds(base + 1, 8)
        scaled = g2[inner] - x0[1:9] + spread(c2, (inner,), near2(x0, 1, 8))
        h2[0:8] = scaled
        d2[0:8] = FIRST * scaled
        inner = pl.ds(base + 2, 6)
        here = d2[1:7]
        scaled = h2[1:7] - here + spread(c2, (inner,), near2(d2, 1, 6))
        found = x0[2:8] + (1.0 + KEEP) * here + ADD * scaled

        row, lane = iota((128, 256), 0), iota((128, 256), 1)
        widen = ones_where(row == 64 * (lane // 128) + (lane % 128) // 2)
        wide = dot(found.reshape(6 * 2 * rows, 128), widen)
        target, source = iota((16, 2 * rows), 0), iota((16, 2 * rows), 1)
        source = 2 * (source % rows) + source // rows
        inside = (target >= 2) & (target < 14) & (source == at_y - 1 + (target - 2) // 4)
        first = ones_where(inside & ((target - 2) % 4 < 2))
        other = ones_where(inside & ((target - 2) % 4 >= 2))
        for index in range(6):
            block = wide[index * 2 * rows:(index + 1) * 2 * rows]
            near_ref[index] = dot(first, block[:, 0:128]) + dot(other, block[:, 128:256])

    return coarse_kernel


def prepare_kernel(k_ref, f_ref, c0, diag0, g0, x0, d0):
    def setup0(start):
        def cut(value):
            return shifted(value, 4, 1)[:, 0:16]

        at = pl.ds(start, 2)
        couplings, inverse, diagonal = coupling(k_ref[pl.ds(start + 3, 2)], near_inside(k_ref, start + 3, 2), (4, 5))
        for number in range(6):
            c0.at[number][at] = cut(couplings[number])
        diag0[at] = cut(diagonal)
        scaled = cut(inverse * f_ref[pl.ds(start + 2, 2)])
        g0[at] = scaled
        d0[at] = FIRST * scaled

    blocks(0, 16, 2, setup0)

    def guess0(start):
        at = pl.ds(start, 2)
        here = d0[at]
        scaled = g0[at] - here + spread(c0, (at,), near(d0, start, 2))
        x0[at] = (1.0 + KEEP) * here + ADD * scaled

    blocks(1, 15, 2, guess0)


def gate_kernel(*refs):
    pass


def post_kernel(near_ref, k_ref, f_ref, x_low_ref, x_high_ref, y_low_ref, y_high_ref, c0, diag0, g0, x0,
                correction_ref, residual_ref,
                k1, f1, c1, g1, x1, y1, d1, h1, wide, y0, d0, h0, v0):
    row = iota((8, 128), 0)

    def join(low, middle, high):
        middle = shifted(middle, 4, 1)
        return jnp.concatenate([jnp.where(row < 6, low, middle), jnp.where(row < 2, middle, high)], 1)

    def alone(tiles):
        tiles = shifted(tiles, 4, 1)
        return jnp.concatenate([tiles, tiles], 1)

    middle = jnp.concatenate([x_low_ref[3:6], k_ref[3:7, 4:12, :], x_high_ref[0:3]], 0)
    k1[0:3] = alone(x_low_ref[0:3])
    k1[3:13] = join(y_low_ref[0:10], middle, y_high_ref[0:10])
    k1[13:16] = alone(x_high_ref[3:6])
    middle = jnp.concatenate([x_low_ref[9:11], f_ref[2:6, 4:12, :], x_high_ref[6:8]], 0)
    f1[1:4] = alone(x_low_ref[6:9])
    f1[4:12] = join(y_low_ref[10:18], middle, y_high_ref[10:18])
    f1[12:15] = alone(x_high_ref[8:11])

    def setup1(start):
        at = pl.ds(start, 7)
        couplings, inverse, _ = coupling(k1[at], near_inside(k1, start, 7), (4, 5))
        for number in range(6):
            c1.at[number][at] = couplings[number]
        scaled = inverse * f1[at]
        g1[at] = scaled
        d1[at] = FIRST * scaled

    blocks(1, 15, 7, setup1)

    def guess1(start):
        at = pl.ds(start, 6)
        here = d1[at]
        scaled = g1[at] - here + spread(c1, (at,), near(d1, start, 6))
        x1[at] = (1.0 + KEEP) * here + ADD * scaled

    blocks(2, 14, 6, guess1)

    up = near_ref[...]
    y1[2:14] = x1[2:14] + jnp.stack([up, up], 1).reshape(12, 16, 128)
    scaled = g1[3:13] - y1[3:13] + spread(c1, (pl.ds(3, 10),), near(y1, 3, 10))
    h1[3:13] = scaled
    d1[3:13] = FIRST * scaled
    here = d1[4:12]
    scaled = h1[4:12] - here + spread(c1, (pl.ds(4, 8),), near(d1, 4, 8))
    found = y1[4:12] + (1.0 + KEEP) * here + ADD * scaled
    wide[:, pl.ds(0, 8, stride=2), :] = found[:, 4:12]
    wide[:, pl.ds(1, 8, stride=2), :] = found[:, 4:12]
    unfold = ones_where(iota((128, 256), 0) == iota((128, 256), 1) // 2)
    up = dot(wide[...].reshape(128, 128), unfold).reshape(8, 16, 256)

    for index in range(1, 15):
        y0[index] = x0[index] + up[index // 2]

    def first0(start):
        at = pl.ds(start, 3)
        scaled = g0[at] - y0[at] + spread(c0, (at,), near(y0, start, 3))
        h0[at] = scaled
        d0[at] = FIRST * scaled

    blocks(2, 14, 3, first0)

    def second0(start):
        at = pl.ds(start, 2)
        here = d0[at]
        scaled = h0[at] - here + spread(c0, (at,), near(d0, start, 2))
        h0[at] = scaled
        v0[at] = KEEP * here + ADD * scaled

    blocks(3, 13, 2, second0)

    def last0(start):
        at, to = pl.ds(start, 2), pl.ds(start - 4, 2)
        here = v0[at]
        correction_ref[to] = (y0[at] + d0[at] + here)[:, 4:12]
        scaled = h0[at] - here + spread(c0, (at,), near(v0, start, 2))
        residual_ref[to] = (diag0[at] * scaled)[:, 4:12]

    blocks(4, 12, 2, last0)


def call(kernel, limit, shapes, scratch, *operands, scalars=0, flops=0):
    specs = [pl.BlockSpec(memory_space=pltpu.SMEM)] * scalars
    specs += [pl.BlockSpec(memory_space=pltpu.VMEM)] * (len(operands) - scalars)
    return pl.pallas_call(
        kernel,
        out_shape=[jax.ShapeDtypeStruct(shape, F32) for shape in shapes],
        in_specs=specs,
        out_specs=[pl.BlockSpec(memory_space=pltpu.VMEM)] * len(shapes),
        scratch_shapes=[pltpu.VMEM(shape, F32) for shape in scratch],
        compiler_params=pltpu.CompilerParams(vmem_limit_bytes=limit * MIB),
        cost_estimate=pl.CostEstimate(flops=flops, bytes_accessed=0, transcendentals=0) if flops else None,
        interpret=INTERPRET,
    )(*operands)


def both_sides(up, down, axes):
    count = math.prod(lax.axis_size(axis) for axis in axes)
    low = lax.ppermute(up, axes, [(i, i + 1) for i in range(count - 1)])
    high = lax.ppermute(down, axes, [(i + 1, i) for i in range(count - 1)])
    return low, high


def body(f, k):
    count_x, chips = lax.axis_size("gx"), lax.axis_size("chip")
    count_y = 2 * chips
    along_x, along_y = ("gx",), ("chip", "core")
    tile, full, half = f.shape[1:], (24, 256), (16, 256)
    tile1, full1 = (8, 128), (16, 128)
    up, down, own = pl.pallas_call(
        pack_x_kernel,
        out_shape=[jax.ShapeDtypeStruct((planes, *tile), F32) for planes in (13, 13, 16)],
        in_specs=[pl.BlockSpec(memory_space=pltpu.HBM)] * 2,
        out_specs=[pl.BlockSpec(memory_space=pltpu.HBM)] * 3,
        scratch_shapes=[pltpu.SemaphoreType.DMA((6,))],
        compiler_params=pltpu.CompilerParams(vmem_limit_bytes=60 * MIB),
        interpret=INTERPRET,
    )(k, f)
    x_low, x_high = both_sides(up, down, along_x)
    packed, down = call(pack_y_kernel, 4, [(Y_TILES, *tile)] * 2, [], own, x_low, x_high)
    y_low, y_high = both_sides(packed, down, along_y)

    k0, f0, k1, f1, up, down, side = call(
        fine_kernel, 16,
        [(22, *full), (20, *full), (10, *full1), (8, *full1), (11, *tile1), (11, *tile1), (18, *tile1)],
        [(6, 20, *full)] + [(20, *full)] * 4 + [(18, *full), (18, 24, 128)],
        packed, x_low, x_high, y_low, y_high)
    x_low, x_high = both_sides(up, down, along_x)
    y_low, y_high = both_sides(side, side, along_y)
    copies, = call(
        next_kernel, 8,
        [(count_x * chips, 4, 128)],
        [(6, 8, *full1)] + [(8, *full1)] * 4 + [(4, *full1)],
        k1, f1)

    prepared = call(
        prepare_kernel, 16,
        [(6, 16, *half)] + [(16, *half)] * 3,
        [(16, *half)],
        k0, f0)

    mine = lax.all_to_all(copies, ("gx", "chip"), 0, 0).reshape(-1, 128)
    waited = (mine, x_low, x_high, y_low, y_high, prepared[0])
    mine = pl.pallas_call(
        gate_kernel,
        out_shape=jax.ShapeDtypeStruct(mine.shape, F32),
        in_specs=[pl.BlockSpec(memory_space=pltpu.VMEM)] * len(waited),
        out_specs=pl.BlockSpec(memory_space=pltpu.VMEM),
        input_output_aliases={0: 0},
        compiler_params=pltpu.CompilerParams(vmem_limit_bytes=4 * MIB),
        interpret=INTERPRET,
    )(*waited)
    other = lax.ppermute(mine, "core", [(0, 1), (1, 0)])

    place = jnp.stack([lax.axis_index("gx"), lax.axis_index(("chip", "core"))]).astype(jnp.int32)
    plane2 = (2, count_y // 2, 128)
    padded = (2 * count_x + 8, *plane2)
    near_e, = call(
        make_coarse_kernel(count_x, count_y), 20,
        [(6, 16, 128)],
        [padded, (6, *padded)] + [padded] * 5
        + [(2 * count_x, *plane2), (6, count_x // 4, *plane2), (count_x // 4, *plane2), (10, *plane2)],
        place, mine, other, scalars=1, flops=6000000000)

    correction, residual = call(
        post_kernel, 16,
        [f.shape, f.shape],
        [(16, *full1)] * 2 + [(6, 16, *full1)] + [(16, *full1)] * 5 + [(8, *full1)] + [(16, *half)] * 4,
        near_e, k1, f1, x_low, x_high, y_low, y_high, *prepared)
    return correction, residual


def solution(mesh):
    shape = (mesh.shape["gx"], mesh.shape["gy"] // 2, 2)
    mesh = jax.sharding.Mesh(mesh.devices.reshape(shape), ("gx", "chip", "core"))
    spec = P("gx", ("chip", "core"), None)
    return jax.shard_map(body, mesh=mesh, in_specs=(spec, spec), out_specs=(spec, spec), check_vma=False)
```

```python
import math

import jax
import jax.numpy as jnp
from jax import lax
from jax.experimental import pallas as pl
from jax.experimental.pallas import tpu as pltpu
from jax.sharding import PartitionSpec as P

INTERPRET = False
COARSE_STEPS = 8
F32 = jnp.float32
MIB = 1024 * 1024


def step_factors(low_end, steps):
    center, radius = 0.5 * (2.0 + low_end), 0.5 * (2.0 - low_end)
    sigma = center / radius
    ratio = 1.0 / sigma
    factors = [(0.0, 1.0 / center)]
    for _ in range(steps - 1):
        ratio_next = 1.0 / (2.0 * sigma - ratio)
        factors.append((ratio_next * ratio, 2.0 * ratio_next / radius))
        ratio = ratio_next
    return factors


(_, FIRST), (KEEP, ADD) = step_factors(0.4, 2)
COARSE_FACTORS = step_factors(0.02, COARSE_STEPS)


def iota(shape, dim):
    return lax.broadcasted_iota(jnp.int32, shape, dim)


def shifted(value, step, axis):
    return pltpu.roll(value, (-step) % value.shape[axis], axis)


def parts_of(value):
    parts = []
    for _ in range(3):
        part = value.astype(jnp.bfloat16)
        parts.append(part)
        value = value - part.astype(F32)
    return parts


def ones_where(condition):
    return jnp.where(condition, 1.0, 0.0).astype(jnp.bfloat16)


def dot(a, ones):
    rows = a.shape[0]
    out = jnp.dot(jnp.concatenate(parts_of(a), 0), ones, preferred_element_type=F32)
    return out[0:rows] + out[rows:2 * rows] + out[2 * rows:]


def dot_left(ones, a):
    columns = a.shape[1]
    out = jnp.dot(ones, jnp.concatenate(parts_of(a), 1), preferred_element_type=F32)
    return out[:, 0:columns] + out[:, columns:2 * columns] + out[:, 2 * columns:]


def blocks(first, last, size, step):
    count = (last - first) // size
    assert first + count * size == last
    if count == 1:
        step(first)
        return

    def one(number, carry):
        step(first + number * size)
        return carry

    lax.fori_loop(0, count, one, 0)


def near(ref, start, size):
    here = ref[pl.ds(start, size)]
    return (ref[pl.ds(start - 1, size)], ref[pl.ds(start + 1, size)],
            shifted(here, -1, 1), shifted(here, 1, 1), shifted(here, -1, 2), shifted(here, 1, 2))


def near_inside(ref, start, size):
    x_low, x_high, y_low, y_high, z_low, z_high = near(ref, start, size)
    lane = iota(z_low.shape, 2)
    z_low = jnp.where(lane == 0, 0.0, z_low)
    z_high = jnp.where(lane == z_low.shape[2] - 1, 0.0, z_high)
    return x_low, x_high, y_low, y_high, z_low, z_high


def coupling(center, around, masked):
    total = 6.0 * center
    for value in around:
        total = total + value
    inside = center > 0.0
    half_inverse = jnp.where(inside, 1.0 / jnp.where(inside, total, 1.0), 0.0)
    couplings = []
    for number, value in enumerate(around):
        c = (center + value) * half_inverse
        couplings.append(jnp.where(value > 0.0, c, 0.0) if number in masked else c)
    return couplings, 2.0 * half_inverse, 0.5 * total


def pick(c_ref, number, where):
    return c_ref.at[number][where] if where else c_ref[number]


def spread(c_ref, where, around):
    total = pick(c_ref, 0, where) * around[0]
    for number in range(1, 6):
        total = total + pick(c_ref, number, where) * around[number]
    return total


PAIRS = ([("k", dx, 7 - dx) for dx in (1, 2, 3)], [("f", dx, 6 - dx) for dx in (1, 2, 3)])
Y_TILES = 28


def pack_x_kernel(k_ref, f_ref, up_ref, down_ref, own_ref, done):
    pieces = ((k_ref, 1, up_ref, 0, 7), (f_ref, 2, up_ref, 7, 6), (k_ref, 0, down_ref, 0, 7), (f_ref, 0, down_ref, 7, 6),
              (k_ref, 0, own_ref, 0, 8), (f_ref, 0, own_ref, 8, 8))
    copies = [pltpu.make_async_copy(ref.at[pl.ds(first, size)], to.at[pl.ds(place, size)], done.at[number])
              for number, (ref, first, to, place, size) in enumerate(pieces)]
    for copy in copies:
        copy.start()
    for copy in copies:
        copy.wait()


def pair_tiles():
    tile = 16
    for pairs in PAIRS:
        for side in ("low", "high"):
            for name, dx, far in pairs:
                yield tile, name, side, dx, far
                tile += 1


def halo_plane(name, side, dx, low_ref, high_ref):
    reach = 7 if name == "k" else 6
    base = 0 if name == "k" else 7
    return low_ref[base + reach - dx] if side == "low" else high_ref[base + dx - 1]


def pack_y_kernel(core_ref, own_ref, low_ref, high_ref, sibling_ref, next_ref):
    first_core = core_ref[0] == 0
    for ref in (sibling_ref, next_ref):
        ref[0:16] = own_ref[...]
    row = iota((8, own_ref.shape[2]), 0)
    for tile, name, side, dx, far in pair_tiles():
        near_plane = halo_plane(name, side, dx, low_ref, high_ref)
        far_plane = halo_plane(name, side, far, low_ref, high_ref)
        up = jnp.where(row < dx, shifted(far_plane, 8 - dx, 0), near_plane)
        down = jnp.where(row >= 8 - dx, shifted(far_plane, dx - 8, 0), near_plane)
        sibling_ref[tile] = jnp.where(first_core, up, down)
        next_ref[tile] = jnp.where(first_core, down, up)


def unpack(first_core, own_ref, x_low_ref, x_high_ref, sibling_ref, next_ref, k0, f0):
    def below(tiles):
        return jnp.where(first_core, next_ref[tiles], sibling_ref[tiles])

    def above(tiles):
        return jnp.where(first_core, sibling_ref[tiles], next_ref[tiles])

    for to, base, reach, name in ((k0, 0, 7, "k"), (f0, 8, 6, "f")):
        tiles = pl.ds(base, 8)
        to[reach:reach + 8, 0:8] = below(tiles)
        to[reach:reach + 8, 8:16] = own_ref[tiles]
        to[reach:reach + 8, 16:24] = above(tiles)
        first = 0 if name == "k" else 7
        to[0:reach, 8:16] = x_low_ref[first:first + reach]
        to[reach + 8:2 * reach + 8, 8:16] = x_high_ref[first:first + reach]
        for plane in (0, 2 * reach + 7):
            to[plane, 0:8] = jnp.zeros(own_ref.shape[1:], F32)
            to[plane, 16:24] = jnp.zeros(own_ref.shape[1:], F32)
    for tile, name, side, dx, far in pair_tiles():
        to, reach = (k0, 7) if name == "k" else (f0, 6)
        near_plane = reach - dx if side == "low" else reach + 7 + dx
        far_plane = reach - far if side == "low" else reach + 7 + far
        low, high = below(tile), above(tile)
        to[near_plane, 0:8] = low
        to[near_plane, 16:24] = high
        if far != dx:
            to[far_plane, 0:8] = shifted(low, dx - 8, 0)
            to[far_plane, 16:24] = shifted(high, 8 - dx, 0)


def fine_kernel(core_ref, own_ref, x_low_ref, x_high_ref, sibling_ref, next_ref,
                k0, f0, k1, f1, up_ref, down_ref, side_ref,
                c0, diag0, g0, d0, e0, sums, zsums):
    unpack(core_ref[0] == 0, own_ref, x_low_ref, x_high_ref, sibling_ref, next_ref, k0, f0)

    def setup(start):
        at = pl.ds(start, 2)
        couplings, inverse, diagonal = coupling(k0[pl.ds(start + 1, 2)], near_inside(k0, start + 1, 2), (4, 5))
        for number in range(6):
            c0.at[number][at] = couplings[number]
        diag0[at] = diagonal
        scaled = inverse * f0[at]
        g0[at] = scaled
        d0[at] = FIRST * scaled

    blocks(0, 20, 2, setup)

    def second(start):
        at = pl.ds(start, 2)
        here = d0[at]
        scaled = g0[at] - here + spread(c0, (at,), near(d0, start, 2))
        g0[at] = scaled
        e0[at] = KEEP * here + ADD * scaled

    blocks(1, 19, 2, second)

    def left(start):
        at = pl.ds(start, 2)
        rest = diag0[at] * (g0[at] - e0[at] + spread(c0, (at,), near(e0, start, 2)))
        sums[start // 2 - 1] = 0.5 * (rest[0] + rest[1])

    blocks(2, 18, 2, left)
    for index in range(10):
        sums[index + 8] = 0.125 * (k0[2 * index + 1] + k0[2 * index + 2])
    fold = ones_where(iota((256, 128), 0) // 2 == iota((256, 128), 1))
    zsums[...] = dot(sums[...].reshape(18 * 24, 256), fold).reshape(18, 24, 128)

    k1[...] = jnp.zeros_like(k1)
    f1[...] = jnp.zeros_like(f1)
    rows = zsums[:, pl.ds(0, 12, stride=2), :] + zsums[:, pl.ds(1, 12, stride=2), :]
    f1[:, 2:14, :] = rows[0:8]
    k1[:, 2:14, :] = rows[8:18]
    up_ref[0:6] = k1[1:7, 4:12, :]
    up_ref[6:11] = f1[1:6, 4:12, :]
    down_ref[0:6] = k1[3:9, 4:12, :]
    down_ref[6:11] = f1[2:7, 4:12, :]
    side_ref[0:10] = k1[:, 4:12, :]
    side_ref[10:18] = f1[:, 4:12, :]


def next_kernel(k1, f1, copies_ref, c1, diag1, g1, d1, e1, out):
    def setup1(start):
        at = pl.ds(start, 4)
        couplings, inverse, diagonal = coupling(k1[pl.ds(start + 1, 4)], near_inside(k1, start + 1, 4), (4, 5))
        for number in range(6):
            c1.at[number][at] = couplings[number]
        diag1[at] = diagonal
        scaled = inverse * f1[at]
        g1[at] = scaled
        d1[at] = FIRST * scaled

    blocks(0, 8, 4, setup1)
    at = pl.ds(1, 6)
    scaled = g1[at] - d1[at] + spread(c1, (at,), near(d1, 1, 6))
    g1[at] = scaled
    e1[at] = KEEP * d1[at] + ADD * scaled
    at = pl.ds(2, 4)
    rest = diag1[at] * (g1[at] - e1[at] + spread(c1, (at,), near(e1, 2, 4)))
    for half in range(2):
        out[half] = 0.5 * (rest[2 * half] + rest[2 * half + 1])
        out[half + 2] = 0.125 * (k1[2 * half + 3] + k1[2 * half + 4])
    row, lane = iota((128, 256), 0), iota((128, 256), 1)
    fold = ones_where((lane == row // 2) | (lane == 192 + row // 2))
    folded = dot(out[...].reshape(64, 128), fold).reshape(4, 16, 256)
    lines = [folded[number, 6:7, 0:128] + folded[number, 7:8, 0:128]
             + folded[number, 8:9, 128:256] + folded[number, 9:10, 128:256] for number in range(4)]
    payload = jnp.concatenate(lines, 0)

    def copy(start):
        copies_ref[pl.ds(start, 8)] = jnp.broadcast_to(payload[None], (8, 4, 128))

    blocks(0, copies_ref.shape[0], 8, copy)


def near2(ref, start, size):
    here = ref[pl.ds(start, size)]
    below, above = ref[pl.ds(start - 1, size)], ref[pl.ds(start + 1, size)]
    z_low, z_high = shifted(here, -1, 3), shifted(here, 1, 3)
    turned = shifted(here, 64, 3)
    turned0, turned1 = turned[:, 0:1], turned[:, 1:2]
    first = iota(turned0.shape, 3) < 64
    y_high = [jnp.where(first, turned0, turned1), jnp.where(first, turned1, shifted(turned0, 1, 2))]
    y_low = [jnp.where(first, shifted(turned1, -1, 2), turned0), jnp.where(first, turned0, turned1)]
    return below, above, jnp.concatenate(y_low, 1), jnp.concatenate(y_high, 1), z_low, z_high


def near2_inside(ref, start, size):
    x_low, x_high, y_low, y_high, z_low, z_high = near2(ref, start, size)
    core, row, lane = (iota(z_low.shape, dim) for dim in (1, 2, 3))
    last = z_low.shape[2] - 1
    y_low = jnp.where((core == 0) & (row == 0) & (lane < 64), 0.0, y_low)
    y_high = jnp.where((core == 1) & (row == last) & (lane >= 64), 0.0, y_high)
    z_low = jnp.where(lane % 64 == 0, 0.0, z_low)
    z_high = jnp.where(lane % 64 == 63, 0.0, z_high)
    return x_low, x_high, y_low, y_high, z_low, z_high


def near3(value):
    count = value.shape[0]
    before, after = shifted(value[count - 1:], -32, 3), shifted(value[0:1], 32, 3)
    x_low = jnp.concatenate([before, value[:count - 1]], 0) if count > 1 else before
    x_high = jnp.concatenate([value[1:], after], 0) if count > 1 else after
    core0, core1 = value[:, 0:1], value[:, 1:2]
    y_low = jnp.concatenate([shifted(core1, -1, 2), core0], 1)
    y_high = jnp.concatenate([core1, shifted(core0, 1, 2)], 1)
    return x_low, x_high, y_low, y_high, shifted(value, -1, 3), shifted(value, 1, 3)


def near3_inside(value):
    x_low, x_high, y_low, y_high, z_low, z_high = near3(value)
    plane, core, row, lane = (iota(value.shape, dim) for dim in range(4))
    count, rows = value.shape[0], value.shape[2]
    x_low = jnp.where((plane == 0) & (lane < 32), 0.0, x_low)
    x_high = jnp.where((plane == count - 1) & (lane >= 96), 0.0, x_high)
    y_low = jnp.where((core == 0) & (row == 0), 0.0, y_low)
    y_high = jnp.where((core == 1) & (row == rows - 1), 0.0, y_high)
    z_low = jnp.where(lane % 32 == 0, 0.0, z_low)
    z_high = jnp.where(lane % 32 == 31, 0.0, z_high)
    return x_low, x_high, y_low, y_high, z_low, z_high


def make_coarse_kernel(count_x, count_y):
    planes2, rows, count3 = 2 * count_x, count_y // 2, count_x // 4
    size = 8
    line = (2, rows, 128)

    def coarse_kernel(place_ref, mine_ref, other_ref, near_ref,
                      k2, c2, diag2, g2, d2, e2, h2, sums, c3, e3, x0):
        at_x, at_y = place_ref[0], place_ref[1]
        zero = jnp.zeros((4, *line), F32)
        for ends in (pl.ds(0, 4), pl.ds(planes2 + 4, 4)):
            for ref in (k2, g2, d2, e2):
                ref[ends] = zero
            for number in range(6):
                c2.at[number][ends] = zero

        core = at_y % 2

        def load(index):
            for half in range(2):
                start = index * (4 * rows) + half
                to = 2 * index + half + 4
                for ref, side in ((mine_ref, core), (other_ref, 1 - core)):
                    k2[to, side] = ref[pl.ds(start + 2, rows, stride=4), :]
                    e2[to, side] = ref[pl.ds(start, rows, stride=4), :]

        def load_some(start):
            for index in range(4):
                load(start + index)

        blocks(0, count_x, 4, load_some)

        def setup(start):
            at = pl.ds(start, size)
            couplings, inverse, diagonal = coupling(k2[at], near2_inside(k2, start, size), (2, 3, 4, 5))
            for number in range(6):
                c2.at[number][at] = couplings[number]
            diag2[at] = diagonal
            scaled = inverse * e2[at]
            g2[at] = scaled
            d2[at] = FIRST * scaled

        blocks(4, planes2 + 4, size, setup)

        def second(start):
            at = pl.ds(start, size)
            here = d2[at]
            scaled = g2[at] - here + spread(c2, (at,), near2(d2, start, size))
            h2[at] = scaled
            e2[at] = KEEP * here + ADD * scaled

        blocks(4, planes2 + 4, size, second)

        def left(start):
            at = pl.ds(start, size)
            rest = diag2[at] * (h2[at] - e2[at] + spread(c2, (at,), near2(e2, start, size)))
            rest = rest.reshape(size // 2, 2, *line)
            here = k2[at].reshape(size // 2, 2, *line)
            to = (start - 4) // 2
            sums[pl.ds(to, size // 2)] = 0.5 * (rest[:, 0] + rest[:, 1])
            sums[pl.ds(to + count_x, size // 2)] = 0.125 * (here[:, 0] + here[:, 1])

        blocks(4, planes2 + 4, size, left)

        flat = count3 * 2 * rows
        row, lane = iota((512, 128), 0), iota((512, 128), 1)
        fold = ones_where(lane == 32 * (row // 128) + (row % 64) // 2)
        quarters = [jnp.concatenate([sums[pl.ds(first + quarter * count3, count3)].reshape(flat, 128)
                                     for first in (0, count_x)], 0) for quarter in range(4)]
        folded = dot(jnp.concatenate(quarters, 1), fold)
        f3 = folded[0:flat].reshape(count3, *line)
        k3 = folded[flat:].reshape(count3, *line)
        couplings, inverse, _ = coupling(k3, near3_inside(k3), (0, 1, 2, 3, 4, 5))
        for number in range(6):
            c3[number] = couplings[number]
        scaled = inverse * f3
        step = COARSE_FACTORS[0][1] * scaled
        total = step
        for keep, add in COARSE_FACTORS[1:]:
            scaled = scaled - step + spread(c3, (), near3(step))
            step = keep * step + add * scaled
            total = total + step
        e3[...] = total

        base = 2 * at_x
        parts = []
        for number in range(5):
            x3 = at_x - 2 + number
            inside = (x3 >= 0) & (x3 < count_x)
            safe = jnp.clip(x3, 0, count_x - 1)
            plane = pltpu.roll(e3[safe % count3].reshape(2 * rows, 128), (128 - 32 * (safe // count3)) % 128, 1)
            parts.append(jnp.where(inside, plane, 0.0))
        row, lane = iota((128, 128), 0), iota((128, 128), 1)
        unfold = ones_where((row < 32) & ((lane % 64) // 2 == row))
        up = dot(jnp.concatenate(parts, 0), unfold).reshape(5, *line)
        local = pl.ds(base, 10)
        twice = jnp.stack([up, up], 1).reshape(10, *line)
        x0[...] = d2[local] + e2[local] + twice
        inner = pl.ds(base + 1, 8)
        scaled = g2[inner] - x0[1:9] + spread(c2, (inner,), near2(x0, 1, 8))
        h2[0:8] = scaled
        d2[0:8] = FIRST * scaled
        inner = pl.ds(base + 2, 6)
        here = d2[1:7]
        scaled = h2[1:7] - here + spread(c2, (inner,), near2(d2, 1, 6))
        found = x0[2:8] + (1.0 + KEEP) * here + ADD * scaled

        row, lane = iota((128, 256), 0), iota((128, 256), 1)
        widen = ones_where(row == 64 * (lane // 128) + (lane % 128) // 2)
        wide = dot(found.reshape(6 * 2 * rows, 128), widen)
        target, source = iota((16, 4 * rows), 0), iota((16, 4 * rows), 1)
        half, source = source // (2 * rows), source % (2 * rows)
        source = 2 * (source % rows) + source // rows
        inside = (target >= 2) & (target < 14) & (source == at_y - 1 + (target - 2) // 4)
        spread_rows = ones_where(inside & (((target - 2) % 4) // 2 == half))
        both = [jnp.concatenate([wide[2 * rows * index:2 * rows * (index + 1), 128 * half:128 * half + 128]
                                 for index in range(6)], 1) for half in range(2)]
        near_e = dot_left(spread_rows, jnp.concatenate(both, 0))
        for index in range(6):
            near_ref[index] = near_e[:, 128 * index:128 * index + 128]

    return coarse_kernel


def prepare_kernel(k_ref, f_ref, c0, diag0, g0, x0, d0):
    def setup0(start):
        def cut(value):
            return shifted(value, 4, 1)[:, 0:16]

        at = pl.ds(start, 2)
        couplings, inverse, diagonal = coupling(k_ref[pl.ds(start + 3, 2)], near_inside(k_ref, start + 3, 2), (4, 5))
        for number in range(6):
            c0.at[number][at] = cut(couplings[number])
        diag0[at] = cut(diagonal)
        scaled = cut(inverse * f_ref[pl.ds(start + 2, 2)])
        g0[at] = scaled
        d0[at] = FIRST * scaled

    blocks(0, 16, 2, setup0)

    def guess0(start):
        at = pl.ds(start, 2)
        here = d0[at]
        scaled = g0[at] - here + spread(c0, (at,), near(d0, start, 2))
        x0[at] = (1.0 + KEEP) * here + ADD * scaled

    blocks(1, 15, 2, guess0)


def gate_kernel(*refs):
    pass


def prepare1_kernel(k_ref, f_ref, x_low_ref, x_high_ref, y_low_ref, y_high_ref, after_ref, c1, g1, x1, k1, f1, d1):
    row = iota((8, 128), 0)

    def join(low, middle, high):
        middle = shifted(middle, 4, 1)
        return jnp.concatenate([jnp.where(row < 6, low, middle), jnp.where(row < 2, middle, high)], 1)

    def alone(tiles):
        tiles = shifted(tiles, 4, 1)
        return jnp.concatenate([tiles, tiles], 1)

    middle = jnp.concatenate([x_low_ref[3:6], k_ref[3:7, 4:12, :], x_high_ref[0:3]], 0)
    k1[0:3] = alone(x_low_ref[0:3])
    k1[3:13] = join(y_low_ref[0:10], middle, y_high_ref[0:10])
    k1[13:16] = alone(x_high_ref[3:6])
    middle = jnp.concatenate([x_low_ref[9:11], f_ref[2:6, 4:12, :], x_high_ref[6:8]], 0)
    f1[1:4] = alone(x_low_ref[6:9])
    f1[4:12] = join(y_low_ref[10:18], middle, y_high_ref[10:18])
    f1[12:15] = alone(x_high_ref[8:11])

    def setup1(start):
        at = pl.ds(start, 7)
        couplings, inverse, _ = coupling(k1[at], near_inside(k1, start, 7), (4, 5))
        for number in range(6):
            c1.at[number][at] = couplings[number]
        scaled = inverse * f1[at]
        g1[at] = scaled
        d1[at] = FIRST * scaled

    blocks(1, 15, 7, setup1)

    def guess1(start):
        at = pl.ds(start, 6)
        here = d1[at]
        scaled = g1[at] - here + spread(c1, (at,), near(d1, start, 6))
        x1[at] = (1.0 + KEEP) * here + ADD * scaled

    blocks(2, 14, 6, guess1)

def post_kernel(near_ref, c1, g1, x1, c0, diag0, g0, x0, correction_ref, residual_ref,
                y1, d1, h1, wide, y0, d0, h0, v0):
    up = near_ref[...]
    y1[2:14] = x1[2:14] + jnp.stack([up, up], 1).reshape(12, 16, 128)
    scaled = g1[3:13] - y1[3:13] + spread(c1, (pl.ds(3, 10),), near(y1, 3, 10))
    h1[3:13] = scaled
    d1[3:13] = FIRST * scaled
    here = d1[4:12]
    scaled = h1[4:12] - here + spread(c1, (pl.ds(4, 8),), near(d1, 4, 8))
    found = y1[4:12] + (1.0 + KEEP) * here + ADD * scaled
    wide[:, pl.ds(0, 8, stride=2), :] = found[:, 4:12]
    wide[:, pl.ds(1, 8, stride=2), :] = found[:, 4:12]
    unfold = ones_where(iota((128, 256), 0) == iota((128, 256), 1) // 2)
    up = dot(wide[...].reshape(128, 128), unfold).reshape(8, 16, 256)

    for index in range(1, 15):
        y0[index] = x0[index] + up[index // 2]

    def first0(start):
        at = pl.ds(start, 3)
        scaled = g0[at] - y0[at] + spread(c0, (at,), near(y0, start, 3))
        h0[at] = scaled
        d0[at] = FIRST * scaled

    blocks(2, 14, 3, first0)

    def second0(start):
        at = pl.ds(start, 2)
        here = d0[at]
        scaled = h0[at] - here + spread(c0, (at,), near(d0, start, 2))
        h0[at] = scaled
        v0[at] = KEEP * here + ADD * scaled

    blocks(3, 13, 2, second0)

    def last0(start):
        at, to = pl.ds(start, 2), pl.ds(start - 4, 2)
        here = v0[at]
        correction_ref[to] = (y0[at] + d0[at] + here)[:, 4:12]
        scaled = h0[at] - here + spread(c0, (at,), near(v0, start, 2))
        residual_ref[to] = (diag0[at] * scaled)[:, 4:12]

    blocks(4, 12, 2, last0)


def call(kernel, limit, shapes, scratch, *operands, scalars=0, flops=0):
    specs = [pl.BlockSpec(memory_space=pltpu.SMEM)] * scalars
    specs += [pl.BlockSpec(memory_space=pltpu.VMEM)] * (len(operands) - scalars)
    return pl.pallas_call(
        kernel,
        out_shape=[jax.ShapeDtypeStruct(shape, F32) for shape in shapes],
        in_specs=specs,
        out_specs=[pl.BlockSpec(memory_space=pltpu.VMEM)] * len(shapes),
        scratch_shapes=[pltpu.VMEM(shape, F32) for shape in scratch],
        compiler_params=pltpu.CompilerParams(vmem_limit_bytes=limit * MIB),
        cost_estimate=pl.CostEstimate(flops=flops, bytes_accessed=0, transcendentals=0) if flops else None,
        interpret=INTERPRET,
    )(*operands)


def both_sides(up, down, axes):
    count = math.prod(lax.axis_size(axis) for axis in axes)
    low = lax.ppermute(up, axes, [(i, i + 1) for i in range(count - 1)])
    high = lax.ppermute(down, axes, [(i + 1, i) for i in range(count - 1)])
    return low, high


def body(f, k):
    count_x, chips = lax.axis_size("gx"), lax.axis_size("chip")
    count_y = 2 * chips
    along_x, along_y = ("gx",), ("chip", "core")
    tile, full, half = f.shape[1:], (24, 256), (16, 256)
    tile1, full1 = (8, 128), (16, 128)
    up, down, own = pl.pallas_call(
        pack_x_kernel,
        out_shape=[jax.ShapeDtypeStruct((planes, *tile), F32) for planes in (13, 13, 16)],
        in_specs=[pl.BlockSpec(memory_space=pltpu.HBM)] * 2,
        out_specs=[pl.BlockSpec(memory_space=pltpu.VMEM)] * 3,
        scratch_shapes=[pltpu.SemaphoreType.DMA((6,))],
        compiler_params=pltpu.CompilerParams(vmem_limit_bytes=4 * MIB),
        interpret=INTERPRET,
    )(k, f)
    x_low, x_high = both_sides(up, down, along_x)
    core = lax.axis_index("core").astype(jnp.int32).reshape(1)
    packed, outer = call(pack_y_kernel, 4, [(Y_TILES, *tile)] * 2, [], core, own, x_low, x_high, scalars=1)
    sibling = lax.ppermute(packed, "core", [(0, 1), (1, 0)])
    after = lax.ppermute(outer, along_y, [pair for i in range(1, count_y - 1, 2) for pair in ((i, i + 1), (i + 1, i))])

    k0, f0, k1, f1, up, down, side = call(
        fine_kernel, 16,
        [(22, *full), (20, *full), (10, *full1), (8, *full1), (11, *tile1), (11, *tile1), (18, *tile1)],
        [(6, 20, *full)] + [(20, *full)] * 4 + [(18, *full), (18, 24, 128)],
        core, packed, x_low, x_high, sibling, after, scalars=1)
    x_low, x_high = both_sides(up, down, along_x)
    y_low, y_high = both_sides(side, side, along_y)
    copies, = call(
        next_kernel, 8,
        [(count_x * chips, 4, 128)],
        [(6, 8, *full1)] + [(8, *full1)] * 4 + [(4, *full1)],
        k1, f1)

    prepared = call(
        prepare_kernel, 16,
        [(6, 16, *half)] + [(16, *half)] * 3,
        [(16, *half)],
        k0, f0)

    mine = lax.all_to_all(copies, ("gx", "chip"), 0, 0).reshape(-1, 128)
    waited = (mine, x_low, x_high, y_low, y_high, prepared[0])
    mine = pl.pallas_call(
        gate_kernel,
        out_shape=jax.ShapeDtypeStruct(mine.shape, F32),
        in_specs=[pl.BlockSpec(memory_space=pltpu.VMEM)] * len(waited),
        out_specs=pl.BlockSpec(memory_space=pltpu.VMEM),
        input_output_aliases={0: 0},
        compiler_params=pltpu.CompilerParams(vmem_limit_bytes=4 * MIB),
        interpret=INTERPRET,
    )(*waited)
    other = lax.ppermute(mine, "core", [(0, 1), (1, 0)])

    prepared1 = call(
        prepare1_kernel, 8,
        [(6, 16, *full1)] + [(16, *full1)] * 2,
        [(16, *full1)] * 3,
        k1, f1, x_low, x_high, y_low, y_high, mine)

    place = jnp.stack([lax.axis_index("gx"), lax.axis_index(("chip", "core"))]).astype(jnp.int32)
    plane2 = (2, count_y // 2, 128)
    padded = (2 * count_x + 8, *plane2)
    near_e, = call(
        make_coarse_kernel(count_x, count_y), 20,
        [(6, 16, 128)],
        [padded, (6, *padded)] + [padded] * 5
        + [(2 * count_x, *plane2), (6, count_x // 4, *plane2), (count_x // 4, *plane2), (10, *plane2)],
        place, mine, other, scalars=1, flops=6000000000)

    correction, residual = call(
        post_kernel, 16,
        [f.shape, f.shape],
        [(16, *full1)] * 3 + [(8, *full1)] + [(16, *half)] * 4,
        near_e, *prepared1, *prepared)
    return correction, residual


def solution(mesh):
    shape = (mesh.shape["gx"], mesh.shape["gy"] // 2, 2)
    mesh = jax.sharding.Mesh(mesh.devices.reshape(shape), ("gx", "chip", "core"))
    spec = P("gx", ("chip", "core"), None)
    return jax.shard_map(body, mesh=mesh, in_specs=(spec, spec), out_specs=(spec, spec), check_vma=False)
```

```python
import math

import jax
import jax.numpy as jnp
from jax import lax
from jax.experimental import pallas as pl
from jax.experimental.pallas import tpu as pltpu
from jax.sharding import PartitionSpec as P

INTERPRET = False
COARSE_STEPS = 8
F32 = jnp.float32
MIB = 1024 * 1024


def step_factors(low_end, steps):
    center, radius = 0.5 * (2.0 + low_end), 0.5 * (2.0 - low_end)
    sigma = center / radius
    ratio = 1.0 / sigma
    factors = [(0.0, 1.0 / center)]
    for _ in range(steps - 1):
        ratio_next = 1.0 / (2.0 * sigma - ratio)
        factors.append((ratio_next * ratio, 2.0 * ratio_next / radius))
        ratio = ratio_next
    return factors


(_, FIRST), (KEEP, ADD) = step_factors(0.4, 2)
COARSE_FACTORS = step_factors(0.02, COARSE_STEPS)


def iota(shape, dim):
    return lax.broadcasted_iota(jnp.int32, shape, dim)


def shifted(value, step, axis):
    return pltpu.roll(value, (-step) % value.shape[axis], axis)


def parts_of(value):
    parts = []
    for _ in range(3):
        part = value.astype(jnp.bfloat16)
        parts.append(part)
        value = value - part.astype(F32)
    return parts


def ones_where(condition):
    return jnp.where(condition, 1.0, 0.0).astype(jnp.bfloat16)


def dot(a, ones):
    rows = a.shape[0]
    out = jnp.dot(jnp.concatenate(parts_of(a), 0), ones, preferred_element_type=F32)
    return out[0:rows] + out[rows:2 * rows] + out[2 * rows:]


def dot_left(ones, a):
    columns = a.shape[1]
    out = jnp.dot(ones, jnp.concatenate(parts_of(a), 1), preferred_element_type=F32)
    return out[:, 0:columns] + out[:, columns:2 * columns] + out[:, 2 * columns:]


def blocks(first, last, size, step):
    count = (last - first) // size
    assert first + count * size == last
    if count == 1:
        step(first)
        return

    def one(number, carry):
        step(first + number * size)
        return carry

    lax.fori_loop(0, count, one, 0)


def near(ref, start, size):
    here = ref[pl.ds(start, size)]
    return (ref[pl.ds(start - 1, size)], ref[pl.ds(start + 1, size)],
            shifted(here, -1, 1), shifted(here, 1, 1), shifted(here, -1, 2), shifted(here, 1, 2))


def near_inside(ref, start, size):
    x_low, x_high, y_low, y_high, z_low, z_high = near(ref, start, size)
    lane = iota(z_low.shape, 2)
    z_low = jnp.where(lane == 0, 0.0, z_low)
    z_high = jnp.where(lane == z_low.shape[2] - 1, 0.0, z_high)
    return x_low, x_high, y_low, y_high, z_low, z_high


def coupling(center, around, masked):
    total = 6.0 * center
    for value in around:
        total = total + value
    inside = center > 0.0
    half_inverse = jnp.where(inside, 1.0 / jnp.where(inside, total, 1.0), 0.0)
    couplings = []
    for number, value in enumerate(around):
        c = (center + value) * half_inverse
        couplings.append(jnp.where(value > 0.0, c, 0.0) if number in masked else c)
    return couplings, 2.0 * half_inverse, 0.5 * total


def pick(c_ref, number, where):
    return c_ref.at[number][where] if where else c_ref[number]


def spread(c_ref, where, around):
    total = pick(c_ref, 0, where) * around[0]
    for number in range(1, 6):
        total = total + pick(c_ref, number, where) * around[number]
    return total


PAIRS = ([("k", dx, 7 - dx) for dx in (1, 2, 3)], [("f", dx, 6 - dx) for dx in (1, 2, 3)])
Y_TILES = 28


def pack_x_kernel(core_ref, k_ref, f_ref, one_ref, two_ref, own_ref, done):
    core = core_ref[0]
    pieces = ((k_ref, 1 - core, one_ref, 0, 7), (f_ref, 2 - 2 * core, one_ref, 7, 6),
              (k_ref, core, two_ref, 0, 7), (f_ref, 2 * core, two_ref, 7, 6),
              (k_ref, 0, own_ref, 0, 8), (f_ref, 0, own_ref, 8, 8))
    copies = [pltpu.make_async_copy(ref.at[pl.ds(first, size)], to.at[pl.ds(place, size)], done.at[number])
              for number, (ref, first, to, place, size) in enumerate(pieces)]
    for copy in copies:
        copy.start()
    for copy in copies:
        copy.wait()


def chosen(first_core, one_ref, two_ref):
    def low(at):
        return jnp.where(first_core, one_ref[at], two_ref[at])

    def high(at):
        return jnp.where(first_core, two_ref[at], one_ref[at])

    return low, high


def pair_tiles():
    tile = 16
    for pairs in PAIRS:
        for side in ("low", "high"):
            for name, dx, far in pairs:
                yield tile, name, side, dx, far
                tile += 1


def halo_plane(name, side, dx, x_low, x_high):
    reach = 7 if name == "k" else 6
    base = 0 if name == "k" else 7
    return x_low(base + reach - dx) if side == "low" else x_high(base + dx - 1)


def pack_y_kernel(core_ref, own_ref, x_one_ref, x_two_ref, sibling_ref, next_ref):
    first_core = core_ref[0] == 0
    x_low, x_high = chosen(first_core, x_one_ref, x_two_ref)
    for ref in (sibling_ref, next_ref):
        ref[0:16] = own_ref[...]
    row = iota((8, own_ref.shape[2]), 0)
    for tile, name, side, dx, far in pair_tiles():
        near_plane = halo_plane(name, side, dx, x_low, x_high)
        far_plane = halo_plane(name, side, far, x_low, x_high)
        up = jnp.where(row < dx, shifted(far_plane, 8 - dx, 0), near_plane)
        down = jnp.where(row >= 8 - dx, shifted(far_plane, dx - 8, 0), near_plane)
        sibling_ref[tile] = jnp.where(first_core, up, down)
        next_ref[tile] = jnp.where(first_core, down, up)


def unpack(first_core, own_ref, x_one_ref, x_two_ref, sibling_ref, next_ref, k0, f0):
    x_low, x_high = chosen(first_core, x_one_ref, x_two_ref)
    below, above = chosen(first_core, next_ref, sibling_ref)
    for to, base, reach, name in ((k0, 0, 7, "k"), (f0, 8, 6, "f")):
        tiles = pl.ds(base, 8)
        to[reach:reach + 8, 0:8] = below(tiles)
        to[reach:reach + 8, 8:16] = own_ref[tiles]
        to[reach:reach + 8, 16:24] = above(tiles)
        first = 0 if name == "k" else 7
        to[0:reach, 8:16] = x_low(pl.ds(first, reach))
        to[reach + 8:2 * reach + 8, 8:16] = x_high(pl.ds(first, reach))
        for plane in (0, 2 * reach + 7):
            to[plane, 0:8] = jnp.zeros(own_ref.shape[1:], F32)
            to[plane, 16:24] = jnp.zeros(own_ref.shape[1:], F32)
    for tile, name, side, dx, far in pair_tiles():
        to, reach = (k0, 7) if name == "k" else (f0, 6)
        near_plane = reach - dx if side == "low" else reach + 7 + dx
        far_plane = reach - far if side == "low" else reach + 7 + far
        low, high = below(tile), above(tile)
        to[near_plane, 0:8] = low
        to[near_plane, 16:24] = high
        if far != dx:
            to[far_plane, 0:8] = shifted(low, dx - 8, 0)
            to[far_plane, 16:24] = shifted(high, 8 - dx, 0)


def fine_kernel(core_ref, own_ref, x_one_ref, x_two_ref, sibling_ref, next_ref,
                k0, f0, k1, f1, up_ref, down_ref, side_ref,
                c0, diag0, g0, d0, e0, sums, zsums):
    unpack(core_ref[0] == 0, own_ref, x_one_ref, x_two_ref, sibling_ref, next_ref, k0, f0)

    def setup(start):
        at = pl.ds(start, 2)
        couplings, inverse, diagonal = coupling(k0[pl.ds(start + 1, 2)], near_inside(k0, start + 1, 2), (4, 5))
        for number in range(6):
            c0.at[number][at] = couplings[number]
        diag0[at] = diagonal
        scaled = inverse * f0[at]
        g0[at] = scaled
        d0[at] = FIRST * scaled

    blocks(0, 20, 2, setup)

    def second(start):
        at = pl.ds(start, 2)
        here = d0[at]
        scaled = g0[at] - here + spread(c0, (at,), near(d0, start, 2))
        g0[at] = scaled
        e0[at] = KEEP * here + ADD * scaled

    blocks(1, 19, 2, second)

    def left(start):
        at = pl.ds(start, 2)
        rest = diag0[at] * (g0[at] - e0[at] + spread(c0, (at,), near(e0, start, 2)))
        sums[start // 2 - 1] = 0.5 * (rest[0] + rest[1])

    blocks(2, 18, 2, left)
    for index in range(10):
        sums[index + 8] = 0.125 * (k0[2 * index + 1] + k0[2 * index + 2])
    fold = ones_where(iota((256, 128), 0) // 2 == iota((256, 128), 1))
    zsums[...] = dot(sums[...].reshape(18 * 24, 256), fold).reshape(18, 24, 128)

    k1[...] = jnp.zeros_like(k1)
    f1[...] = jnp.zeros_like(f1)
    rows = zsums[:, pl.ds(0, 12, stride=2), :] + zsums[:, pl.ds(1, 12, stride=2), :]
    f1[:, 2:14, :] = rows[0:8]
    k1[:, 2:14, :] = rows[8:18]
    up_ref[0:6] = k1[1:7, 4:12, :]
    up_ref[6:11] = f1[1:6, 4:12, :]
    down_ref[0:6] = k1[3:9, 4:12, :]
    down_ref[6:11] = f1[2:7, 4:12, :]
    side_ref[0:10] = k1[:, 4:12, :]
    side_ref[10:18] = f1[:, 4:12, :]


def next_kernel(k1, f1, copies_ref, c1, diag1, g1, d1, e1, out):
    def setup1(start):
        at = pl.ds(start, 4)
        couplings, inverse, diagonal = coupling(k1[pl.ds(start + 1, 4)], near_inside(k1, start + 1, 4), (4, 5))
        for number in range(6):
            c1.at[number][at] = couplings[number]
        diag1[at] = diagonal
        scaled = inverse * f1[at]
        g1[at] = scaled
        d1[at] = FIRST * scaled

    blocks(0, 8, 4, setup1)
    at = pl.ds(1, 6)
    scaled = g1[at] - d1[at] + spread(c1, (at,), near(d1, 1, 6))
    g1[at] = scaled
    e1[at] = KEEP * d1[at] + ADD * scaled
    at = pl.ds(2, 4)
    rest = diag1[at] * (g1[at] - e1[at] + spread(c1, (at,), near(e1, 2, 4)))
    for half in range(2):
        out[half] = 0.5 * (rest[2 * half] + rest[2 * half + 1])
        out[half + 2] = 0.125 * (k1[2 * half + 3] + k1[2 * half + 4])
    row, lane = iota((128, 256), 0), iota((128, 256), 1)
    fold = ones_where((lane == row // 2) | (lane == 192 + row // 2))
    folded = dot(out[...].reshape(64, 128), fold).reshape(4, 16, 256)
    lines = [folded[number, 6:7, 0:128] + folded[number, 7:8, 0:128]
             + folded[number, 8:9, 128:256] + folded[number, 9:10, 128:256] for number in range(4)]
    payload = jnp.concatenate(lines, 0)

    copies_ref[...] = jnp.broadcast_to(payload[None], copies_ref.shape)


def near2(ref, start, size):
    here = ref[pl.ds(start, size)]
    below, above = ref[pl.ds(start - 1, size)], ref[pl.ds(start + 1, size)]
    z_low, z_high = shifted(here, -1, 3), shifted(here, 1, 3)
    turned = shifted(here, 64, 3)
    turned0, turned1 = turned[:, 0:1], turned[:, 1:2]
    first = iota(turned0.shape, 3) < 64
    y_high = [jnp.where(first, turned0, turned1), jnp.where(first, turned1, shifted(turned0, 1, 2))]
    y_low = [jnp.where(first, shifted(turned1, -1, 2), turned0), jnp.where(first, turned0, turned1)]
    return below, above, jnp.concatenate(y_low, 1), jnp.concatenate(y_high, 1), z_low, z_high


def near2_inside(ref, start, size):
    x_low, x_high, y_low, y_high, z_low, z_high = near2(ref, start, size)
    core, row, lane = (iota(z_low.shape, dim) for dim in (1, 2, 3))
    last = z_low.shape[2] - 1
    y_low = jnp.where((core == 0) & (row == 0) & (lane < 64), 0.0, y_low)
    y_high = jnp.where((core == 1) & (row == last) & (lane >= 64), 0.0, y_high)
    z_low = jnp.where(lane % 64 == 0, 0.0, z_low)
    z_high = jnp.where(lane % 64 == 63, 0.0, z_high)
    return x_low, x_high, y_low, y_high, z_low, z_high


def near3(value):
    count = value.shape[0]
    before, after = shifted(value[count - 1:], -32, 3), shifted(value[0:1], 32, 3)
    x_low = jnp.concatenate([before, value[:count - 1]], 0) if count > 1 else before
    x_high = jnp.concatenate([value[1:], after], 0) if count > 1 else after
    core0, core1 = value[:, 0:1], value[:, 1:2]
    y_low = jnp.concatenate([shifted(core1, -1, 2), core0], 1)
    y_high = jnp.concatenate([core1, shifted(core0, 1, 2)], 1)
    return x_low, x_high, y_low, y_high, shifted(value, -1, 3), shifted(value, 1, 3)


def near3_inside(value):
    x_low, x_high, y_low, y_high, z_low, z_high = near3(value)
    plane, core, row, lane = (iota(value.shape, dim) for dim in range(4))
    count, rows = value.shape[0], value.shape[2]
    x_low = jnp.where((plane == 0) & (lane < 32), 0.0, x_low)
    x_high = jnp.where((plane == count - 1) & (lane >= 96), 0.0, x_high)
    y_low = jnp.where((core == 0) & (row == 0), 0.0, y_low)
    y_high = jnp.where((core == 1) & (row == rows - 1), 0.0, y_high)
    z_low = jnp.where(lane % 32 == 0, 0.0, z_low)
    z_high = jnp.where(lane % 32 == 31, 0.0, z_high)
    return x_low, x_high, y_low, y_high, z_low, z_high


def make_coarse_kernel(count_x, count_y):
    planes2, rows, count3 = 2 * count_x, count_y // 2, count_x // 4
    size = 4
    line = (2, rows, 128)

    def coarse_kernel(place_ref, mine_ref, other_ref, near_ref,
                      k2, c2, diag2, g2, d2, e2, h2, sums, c3, e3, x0):
        at_x, at_y = place_ref[0], place_ref[1]
        zero = jnp.zeros((4, *line), F32)
        for ends in (pl.ds(0, 4), pl.ds(planes2 + 4, 4)):
            for ref in (k2, g2, d2, e2):
                ref[ends] = zero
            for number in range(6):
                c2.at[number][ends] = zero

        core = at_y % 2

        def load(index):
            for half in range(2):
                start = index * (4 * rows) + half
                to = 2 * index + half + 4
                for ref, side in ((mine_ref, core), (other_ref, 1 - core)):
                    k2[to, side] = ref[pl.ds(start + 2, rows, stride=4), :]
                    e2[to, side] = ref[pl.ds(start, rows, stride=4), :]

        def load_some(start):
            for index in range(4):
                load(start + index)

        blocks(0, count_x, 4, load_some)

        def setup(start):
            at = pl.ds(start, size)
            couplings, inverse, diagonal = coupling(k2[at], near2_inside(k2, start, size), (2, 3, 4, 5))
            for number in range(6):
                c2.at[number][at] = couplings[number]
            diag2[at] = diagonal
            scaled = inverse * e2[at]
            g2[at] = scaled
            d2[at] = FIRST * scaled

        blocks(4, planes2 + 4, size, setup)

        def second(start):
            at = pl.ds(start, size)
            here = d2[at]
            scaled = g2[at] - here + spread(c2, (at,), near2(d2, start, size))
            h2[at] = scaled
            e2[at] = KEEP * here + ADD * scaled

        blocks(4, planes2 + 4, size, second)

        def left(start):
            at = pl.ds(start, size)
            rest = diag2[at] * (h2[at] - e2[at] + spread(c2, (at,), near2(e2, start, size)))
            rest = rest.reshape(size // 2, 2, *line)
            here = k2[at].reshape(size // 2, 2, *line)
            to = (start - 4) // 2
            sums[pl.ds(to, size // 2)] = 0.5 * (rest[:, 0] + rest[:, 1])
            sums[pl.ds(to + count_x, size // 2)] = 0.125 * (here[:, 0] + here[:, 1])

        blocks(4, planes2 + 4, size, left)

        flat = count3 * 2 * rows
        row, lane = iota((512, 128), 0), iota((512, 128), 1)
        fold = ones_where(lane == 32 * (row // 128) + (row % 64) // 2)
        quarters = [jnp.concatenate([sums[pl.ds(first + quarter * count3, count3)].reshape(flat, 128)
                                     for first in (0, count_x)], 0) for quarter in range(4)]
        folded = dot(jnp.concatenate(quarters, 1), fold)
        f3 = folded[0:flat].reshape(count3, *line)
        k3 = folded[flat:].reshape(count3, *line)
        couplings, inverse, _ = coupling(k3, near3_inside(k3), (0, 1, 2, 3, 4, 5))
        for number in range(6):
            c3[number] = couplings[number]
        scaled = inverse * f3
        step = COARSE_FACTORS[0][1] * scaled
        total = step
        for keep, add in COARSE_FACTORS[1:]:
            scaled = scaled - step + spread(c3, (), near3(step))
            step = keep * step + add * scaled
            total = total + step
        e3[...] = total

        base = 2 * at_x
        parts = []
        for number in range(5):
            x3 = at_x - 2 + number
            inside = (x3 >= 0) & (x3 < count_x)
            safe = jnp.clip(x3, 0, count_x - 1)
            plane = pltpu.roll(e3[safe % count3].reshape(2 * rows, 128), (128 - 32 * (safe // count3)) % 128, 1)
            parts.append(jnp.where(inside, plane, 0.0))
        row, lane = iota((128, 128), 0), iota((128, 128), 1)
        unfold = ones_where((row < 32) & ((lane % 64) // 2 == row))
        up = dot(jnp.concatenate(parts, 0), unfold).reshape(5, *line)
        local = pl.ds(base, 10)
        twice = jnp.stack([up, up], 1).reshape(10, *line)
        x0[...] = d2[local] + e2[local] + twice
        inner = pl.ds(base + 1, 8)
        scaled = g2[inner] - x0[1:9] + spread(c2, (inner,), near2(x0, 1, 8))
        h2[0:8] = scaled
        d2[0:8] = FIRST * scaled
        inner = pl.ds(base + 2, 6)
        here = d2[1:7]
        scaled = h2[1:7] - here + spread(c2, (inner,), near2(d2, 1, 6))
        found = x0[2:8] + (1.0 + KEEP) * here + ADD * scaled

        row, lane = iota((128, 256), 0), iota((128, 256), 1)
        widen = ones_where(row == 64 * (lane // 128) + (lane % 128) // 2)
        wide = dot(found.reshape(6 * 2 * rows, 128), widen)
        target, source = iota((16, 4 * rows), 0), iota((16, 4 * rows), 1)
        half, source = source // (2 * rows), source % (2 * rows)
        source = 2 * (source % rows) + source // rows
        inside = (target >= 2) & (target < 14) & (source == at_y - 1 + (target - 2) // 4)
        spread_rows = ones_where(inside & (((target - 2) % 4) // 2 == half))
        both = [jnp.concatenate([wide[2 * rows * index:2 * rows * (index + 1), 128 * half:128 * half + 128]
                                 for index in range(6)], 1) for half in range(2)]
        near_e = dot_left(spread_rows, jnp.concatenate(both, 0))
        for index in range(6):
            near_ref[index] = near_e[:, 128 * index:128 * index + 128]

    return coarse_kernel


def prepare_kernel(k_ref, f_ref, c0, diag0, g0, x0, d0):
    def setup0(start):
        def cut(value):
            return shifted(value, 4, 1)[:, 0:16]

        at = pl.ds(start, 2)
        couplings, inverse, diagonal = coupling(k_ref[pl.ds(start + 3, 2)], near_inside(k_ref, start + 3, 2), (4, 5))
        for number in range(6):
            c0.at[number][at] = cut(couplings[number])
        diag0[at] = cut(diagonal)
        scaled = cut(inverse * f_ref[pl.ds(start + 2, 2)])
        g0[at] = scaled
        d0[at] = FIRST * scaled

    blocks(0, 16, 2, setup0)

    def guess0(start):
        at = pl.ds(start, 2)
        here = d0[at]
        scaled = g0[at] - here + spread(c0, (at,), near(d0, start, 2))
        x0[at] = (1.0 + KEEP) * here + ADD * scaled

    blocks(1, 15, 2, guess0)


def gate_kernel(*refs):
    pass


def prepare1_kernel(k_ref, f_ref, x_low_ref, x_high_ref, y_low_ref, y_high_ref, after_ref, c1, g1, x1, k1, f1, d1):
    row = iota((8, 128), 0)

    def join(low, middle, high):
        middle = shifted(middle, 4, 1)
        return jnp.concatenate([jnp.where(row < 6, low, middle), jnp.where(row < 2, middle, high)], 1)

    def alone(tiles):
        tiles = shifted(tiles, 4, 1)
        return jnp.concatenate([tiles, tiles], 1)

    middle = jnp.concatenate([x_low_ref[3:6], k_ref[3:7, 4:12, :], x_high_ref[0:3]], 0)
    k1[0:3] = alone(x_low_ref[0:3])
    k1[3:13] = join(y_low_ref[0:10], middle, y_high_ref[0:10])
    k1[13:16] = alone(x_high_ref[3:6])
    middle = jnp.concatenate([x_low_ref[9:11], f_ref[2:6, 4:12, :], x_high_ref[6:8]], 0)
    f1[1:4] = alone(x_low_ref[6:9])
    f1[4:12] = join(y_low_ref[10:18], middle, y_high_ref[10:18])
    f1[12:15] = alone(x_high_ref[8:11])

    def setup1(start):
        at = pl.ds(start, 7)
        couplings, inverse, _ = coupling(k1[at], near_inside(k1, start, 7), (4, 5))
        for number in range(6):
            c1.at[number][at] = couplings[number]
        scaled = inverse * f1[at]
        g1[at] = scaled
        d1[at] = FIRST * scaled

    blocks(1, 15, 7, setup1)

    def guess1(start):
        at = pl.ds(start, 6)
        here = d1[at]
        scaled = g1[at] - here + spread(c1, (at,), near(d1, start, 6))
        x1[at] = (1.0 + KEEP) * here + ADD * scaled

    blocks(2, 14, 6, guess1)

def post_kernel(near_ref, c1, g1, x1, c0, diag0, g0, x0, correction_ref, residual_ref,
                y1, d1, h1, wide, y0, d0, h0, v0):
    up = near_ref[...]
    y1[2:14] = x1[2:14] + jnp.stack([up, up], 1).reshape(12, 16, 128)
    scaled = g1[3:13] - y1[3:13] + spread(c1, (pl.ds(3, 10),), near(y1, 3, 10))
    h1[3:13] = scaled
    d1[3:13] = FIRST * scaled
    here = d1[4:12]
    scaled = h1[4:12] - here + spread(c1, (pl.ds(4, 8),), near(d1, 4, 8))
    found = y1[4:12] + (1.0 + KEEP) * here + ADD * scaled
    wide[:, pl.ds(0, 8, stride=2), :] = found[:, 4:12]
    wide[:, pl.ds(1, 8, stride=2), :] = found[:, 4:12]
    unfold = ones_where(iota((128, 256), 0) == iota((128, 256), 1) // 2)
    up = dot(wide[...].reshape(128, 128), unfold).reshape(8, 16, 256)

    for index in range(1, 15):
        y0[index] = x0[index] + up[index // 2]

    def first0(start):
        at = pl.ds(start, 3)
        scaled = g0[at] - y0[at] + spread(c0, (at,), near(y0, start, 3))
        h0[at] = scaled
        d0[at] = FIRST * scaled

    blocks(2, 14, 3, first0)

    def second0(start):
        at = pl.ds(start, 2)
        here = d0[at]
        scaled = h0[at] - here + spread(c0, (at,), near(d0, start, 2))
        h0[at] = scaled
        v0[at] = KEEP * here + ADD * scaled

    blocks(3, 13, 2, second0)

    def last0(start):
        at, to = pl.ds(start, 2), pl.ds(start - 4, 2)
        here = v0[at]
        correction_ref[to] = (y0[at] + d0[at] + here)[:, 4:12]
        scaled = h0[at] - here + spread(c0, (at,), near(v0, start, 2))
        residual_ref[to] = (diag0[at] * scaled)[:, 4:12]

    blocks(4, 12, 2, last0)


def call(kernel, limit, shapes, scratch, *operands, scalars=0, flops=0):
    specs = [pl.BlockSpec(memory_space=pltpu.SMEM)] * scalars
    specs += [pl.BlockSpec(memory_space=pltpu.VMEM)] * (len(operands) - scalars)
    return pl.pallas_call(
        kernel,
        out_shape=[jax.ShapeDtypeStruct(shape, F32) for shape in shapes],
        in_specs=specs,
        out_specs=[pl.BlockSpec(memory_space=pltpu.VMEM)] * len(shapes),
        scratch_shapes=[pltpu.VMEM(shape, F32) for shape in scratch],
        compiler_params=pltpu.CompilerParams(vmem_limit_bytes=limit * MIB),
        cost_estimate=pl.CostEstimate(flops=flops, bytes_accessed=0, transcendentals=0) if flops else None,
        interpret=INTERPRET,
    )(*operands)


def both_sides(up, down, axes):
    count = math.prod(lax.axis_size(axis) for axis in axes)
    low = lax.ppermute(up, axes, [(i, i + 1) for i in range(count - 1)])
    high = lax.ppermute(down, axes, [(i + 1, i) for i in range(count - 1)])
    return low, high


def body(f, k):
    count_x, chips = lax.axis_size("gx"), lax.axis_size("chip")
    count_y = 2 * chips
    along_x, along_y = ("gx",), ("chip", "core")
    tile, full, half = f.shape[1:], (24, 256), (16, 256)
    tile1, full1 = (8, 128), (16, 128)
    core = lax.axis_index("core").astype(jnp.int32).reshape(1)
    one, two, own = pl.pallas_call(
        pack_x_kernel,
        out_shape=[jax.ShapeDtypeStruct((planes, *tile), F32) for planes in (13, 13, 16)],
        in_specs=[pl.BlockSpec(memory_space=pltpu.SMEM)] + [pl.BlockSpec(memory_space=pltpu.HBM)] * 2,
        out_specs=[pl.BlockSpec(memory_space=pltpu.VMEM)] * 3,
        scratch_shapes=[pltpu.SemaphoreType.DMA((6,))],
        compiler_params=pltpu.CompilerParams(vmem_limit_bytes=4 * MIB),
        interpret=INTERPRET,
    )(core, k, f)
    route = [(2 * i, 2 * i + 2) for i in range(count_x - 1)] + [(2 * i + 3, 2 * i + 1) for i in range(count_x - 1)]
    one = lax.ppermute(one, ("gx", "core"), route)
    two = lax.ppermute(two, ("gx", "core"), [(to, source) for source, to in route])
    packed, outer = call(pack_y_kernel, 4, [(Y_TILES, *tile)] * 2, [], core, own, one, two, scalars=1)
    sibling = lax.ppermute(packed, "core", [(0, 1), (1, 0)])
    after = lax.ppermute(outer, along_y, [pair for i in range(1, count_y - 1, 2) for pair in ((i, i + 1), (i + 1, i))])

    k0, f0, k1, f1, up, down, side = call(
        fine_kernel, 16,
        [(22, *full), (20, *full), (10, *full1), (8, *full1), (11, *tile1), (11, *tile1), (18, *tile1)],
        [(6, 20, *full)] + [(20, *full)] * 4 + [(18, *full), (18, 24, 128)],
        core, packed, one, two, sibling, after, scalars=1)
    x_low, x_high = both_sides(up, down, along_x)
    y_low, y_high = both_sides(side, side, along_y)
    copies, = call(
        next_kernel, 8,
        [(chips, 4, 128)],
        [(6, 8, *full1)] + [(8, *full1)] * 4 + [(4, *full1)],
        k1, f1)

    prepared = call(
        prepare_kernel, 16,
        [(6, 16, *half)] + [(16, *half)] * 3,
        [(16, *half)],
        k0, f0)

    line = lax.all_to_all(copies, "chip", 0, 0).reshape(-1, 128)
    copies = jnp.broadcast_to(line[None], (count_x, *line.shape))
    mine = lax.all_to_all(copies, "gx", 0, 0).reshape(-1, 128)
    waited = (mine, x_low, x_high, y_low, y_high, prepared[0])
    mine = pl.pallas_call(
        gate_kernel,
        out_shape=jax.ShapeDtypeStruct(mine.shape, F32),
        in_specs=[pl.BlockSpec(memory_space=pltpu.VMEM)] * len(waited),
        out_specs=pl.BlockSpec(memory_space=pltpu.VMEM),
        input_output_aliases={0: 0},
        compiler_params=pltpu.CompilerParams(vmem_limit_bytes=4 * MIB),
        interpret=INTERPRET,
    )(*waited)
    other = lax.ppermute(mine, "core", [(0, 1), (1, 0)])

    prepared1 = call(
        prepare1_kernel, 8,
        [(6, 16, *full1)] + [(16, *full1)] * 2,
        [(16, *full1)] * 3,
        k1, f1, x_low, x_high, y_low, y_high, mine)

    place = jnp.stack([lax.axis_index("gx"), lax.axis_index(("chip", "core"))]).astype(jnp.int32)
    plane2 = (2, count_y // 2, 128)
    padded = (2 * count_x + 8, *plane2)
    near_e, = call(
        make_coarse_kernel(count_x, count_y), 20,
        [(6, 16, 128)],
        [padded, (6, *padded)] + [padded] * 5
        + [(2 * count_x, *plane2), (6, count_x // 4, *plane2), (count_x // 4, *plane2), (10, *plane2)],
        place, mine, other, scalars=1, flops=6000000000)

    correction, residual = call(
        post_kernel, 16,
        [f.shape, f.shape],
        [(16, *full1)] * 3 + [(8, *full1)] + [(16, *half)] * 4,
        near_e, *prepared1, *prepared)
    return correction, residual


def solution(mesh):
    shape = (mesh.shape["gx"], mesh.shape["gy"] // 2, 2)
    mesh = jax.sharding.Mesh(mesh.devices.reshape(shape), ("gx", "chip", "core"))
    spec = P("gx", ("chip", "core"), None)
    return jax.shard_map(body, mesh=mesh, in_specs=(spec, spec), out_specs=(spec, spec), check_vma=False)
```

```python
import math

import jax
import jax.numpy as jnp
from jax import lax
from jax.experimental import pallas as pl
from jax.experimental.pallas import tpu as pltpu
from jax.sharding import PartitionSpec as P

INTERPRET = False
COARSE_STEPS = 8
F32 = jnp.float32
MIB = 1024 * 1024


def step_factors(low_end, steps):
    center, radius = 0.5 * (2.0 + low_end), 0.5 * (2.0 - low_end)
    sigma = center / radius
    ratio = 1.0 / sigma
    factors = [(0.0, 1.0 / center)]
    for _ in range(steps - 1):
        ratio_next = 1.0 / (2.0 * sigma - ratio)
        factors.append((ratio_next * ratio, 2.0 * ratio_next / radius))
        ratio = ratio_next
    return factors


(_, FIRST), (KEEP, ADD) = step_factors(0.4, 2)
COARSE_FACTORS = step_factors(0.02, COARSE_STEPS)


def iota(shape, dim):
    return lax.broadcasted_iota(jnp.int32, shape, dim)


def shifted(value, step, axis):
    return pltpu.roll(value, (-step) % value.shape[axis], axis)


def parts_of(value):
    parts = []
    for _ in range(3):
        part = value.astype(jnp.bfloat16)
        parts.append(part)
        value = value - part.astype(F32)
    return parts


def ones_where(condition):
    return jnp.where(condition, 1.0, 0.0).astype(jnp.bfloat16)


def dot(a, ones):
    rows = a.shape[0]
    out = jnp.dot(jnp.concatenate(parts_of(a), 0), ones, preferred_element_type=F32)
    return out[0:rows] + out[rows:2 * rows] + out[2 * rows:]


def dot_left(ones, a):
    columns = a.shape[1]
    out = jnp.dot(ones, jnp.concatenate(parts_of(a), 1), preferred_element_type=F32)
    return out[:, 0:columns] + out[:, columns:2 * columns] + out[:, 2 * columns:]


def blocks(first, last, size, step):
    count = (last - first) // size
    assert first + count * size == last
    if count == 1:
        step(first)
        return

    def one(number, carry):
        step(first + number * size)
        return carry

    lax.fori_loop(0, count, one, 0)


def near(ref, start, size):
    here = ref[pl.ds(start, size)]
    return (ref[pl.ds(start - 1, size)], ref[pl.ds(start + 1, size)],
            shifted(here, -1, 1), shifted(here, 1, 1), shifted(here, -1, 2), shifted(here, 1, 2))


def near_inside(ref, start, size):
    x_low, x_high, y_low, y_high, z_low, z_high = near(ref, start, size)
    lane = iota(z_low.shape, 2)
    z_low = jnp.where(lane == 0, 0.0, z_low)
    z_high = jnp.where(lane == z_low.shape[2] - 1, 0.0, z_high)
    return x_low, x_high, y_low, y_high, z_low, z_high


def coupling(center, around, masked):
    total = 6.0 * center
    for value in around:
        total = total + value
    inside = center > 0.0
    half_inverse = jnp.where(inside, 1.0 / jnp.where(inside, total, 1.0), 0.0)
    couplings = []
    for number, value in enumerate(around):
        c = (center + value) * half_inverse
        couplings.append(jnp.where(value > 0.0, c, 0.0) if number in masked else c)
    return couplings, 2.0 * half_inverse, 0.5 * total


def pick(c_ref, number, where):
    return c_ref.at[number][where] if where else c_ref[number]


def spread(c_ref, where, around):
    total = pick(c_ref, 0, where) * around[0]
    for number in range(1, 6):
        total = total + pick(c_ref, number, where) * around[number]
    return total


def face_sums(k_ref, start, size):
    center = k_ref[pl.ds(start, size)]
    around = near_inside(k_ref, start, size)
    total = 6.0 * center
    for value in around:
        total = total + value
    inside = center > 0.0
    half_inverse = jnp.where(inside, 1.0 / jnp.where(inside, total, 1.0), 0.0)
    return (center + around[1], center + around[3], jnp.where(around[5] > 0.0, center + around[5], 0.0), half_inverse)


def spread_faces(w_ref, v_ref, start, size):
    at = pl.ds(start, size)
    here, along_y, along_z = v_ref[at], w_ref.at[1][at], w_ref.at[2][at]
    total = w_ref.at[0][at] * v_ref[pl.ds(start + 1, size)]
    total = total + w_ref.at[0][pl.ds(start - 1, size)] * v_ref[pl.ds(start - 1, size)]
    total = total + along_y * shifted(here, 1, 1) + shifted(along_y * here, -1, 1)
    total = total + along_z * shifted(here, 1, 2) + shifted(along_z * here, -1, 2)
    return w_ref.at[3][at] * total


PAIRS = ([("k", dx, 7 - dx) for dx in (1, 2, 3)], [("f", dx, 6 - dx) for dx in (1, 2, 3)])
Y_TILES = 28


def pack_x_kernel(core_ref, k_ref, f_ref, one_ref, two_ref, own_ref, done):
    core = core_ref[0]
    pieces = ((k_ref, 1 - core, one_ref, 0, 7), (f_ref, 2 - 2 * core, one_ref, 7, 6),
              (k_ref, core, two_ref, 0, 7), (f_ref, 2 * core, two_ref, 7, 6),
              (k_ref, 0, own_ref, 0, 8), (f_ref, 0, own_ref, 8, 8))
    copies = [pltpu.make_async_copy(ref.at[pl.ds(first, size)], to.at[pl.ds(place, size)], done.at[number])
              for number, (ref, first, to, place, size) in enumerate(pieces)]
    for copy in copies:
        copy.start()
    for copy in copies:
        copy.wait()


def chosen(first_core, one_ref, two_ref):
    def low(at):
        return jnp.where(first_core, one_ref[at], two_ref[at])

    def high(at):
        return jnp.where(first_core, two_ref[at], one_ref[at])

    return low, high


def pair_tiles():
    tile = 16
    for pairs in PAIRS:
        for side in ("low", "high"):
            for name, dx, far in pairs:
                yield tile, name, side, dx, far
                tile += 1


def halo_plane(name, side, dx, x_low, x_high):
    reach = 7 if name == "k" else 6
    base = 0 if name == "k" else 7
    return x_low(base + reach - dx) if side == "low" else x_high(base + dx - 1)


def pack_y_kernel(core_ref, own_ref, x_one_ref, x_two_ref, sibling_ref, next_ref):
    first_core = core_ref[0] == 0
    x_low, x_high = chosen(first_core, x_one_ref, x_two_ref)
    for ref in (sibling_ref, next_ref):
        ref[0:16] = own_ref[...]
    row = iota((8, own_ref.shape[2]), 0)
    for tile, name, side, dx, far in pair_tiles():
        near_plane = halo_plane(name, side, dx, x_low, x_high)
        far_plane = halo_plane(name, side, far, x_low, x_high)
        up = jnp.where(row < dx, shifted(far_plane, 8 - dx, 0), near_plane)
        down = jnp.where(row >= 8 - dx, shifted(far_plane, dx - 8, 0), near_plane)
        sibling_ref[tile] = jnp.where(first_core, up, down)
        next_ref[tile] = jnp.where(first_core, down, up)


def unpack(first_core, own_ref, x_one_ref, x_two_ref, sibling_ref, next_ref, k0, f0):
    x_low, x_high = chosen(first_core, x_one_ref, x_two_ref)
    below, above = chosen(first_core, next_ref, sibling_ref)
    for to, base, reach, name in ((k0, 0, 7, "k"), (f0, 8, 6, "f")):
        tiles = pl.ds(base, 8)
        to[reach:reach + 8, 0:8] = below(tiles)
        to[reach:reach + 8, 8:16] = own_ref[tiles]
        to[reach:reach + 8, 16:24] = above(tiles)
        first = 0 if name == "k" else 7
        to[0:reach, 8:16] = x_low(pl.ds(first, reach))
        to[reach + 8:2 * reach + 8, 8:16] = x_high(pl.ds(first, reach))
        for plane in (0, 2 * reach + 7):
            to[plane, 0:8] = jnp.zeros(own_ref.shape[1:], F32)
            to[plane, 16:24] = jnp.zeros(own_ref.shape[1:], F32)
    for tile, name, side, dx, far in pair_tiles():
        to, reach = (k0, 7) if name == "k" else (f0, 6)
        near_plane = reach - dx if side == "low" else reach + 7 + dx
        far_plane = reach - far if side == "low" else reach + 7 + far
        low, high = below(tile), above(tile)
        to[near_plane, 0:8] = low
        to[near_plane, 16:24] = high
        if far != dx:
            to[far_plane, 0:8] = shifted(low, dx - 8, 0)
            to[far_plane, 16:24] = shifted(high, 8 - dx, 0)


def fine_kernel(core_ref, own_ref, x_one_ref, x_two_ref, sibling_ref, next_ref,
                k0, f0, k1, f1, up_ref, down_ref, side_ref,
                c0, diag0, g0, d0, e0, sums, zsums):
    unpack(core_ref[0] == 0, own_ref, x_one_ref, x_two_ref, sibling_ref, next_ref, k0, f0)

    def setup(start):
        at = pl.ds(start, 4)
        couplings, inverse, diagonal = coupling(k0[pl.ds(start + 1, 4)], near_inside(k0, start + 1, 4), (4, 5))
        for number in range(6):
            c0.at[number][at] = couplings[number]
        diag0[at] = diagonal
        scaled = inverse * f0[at]
        g0[at] = scaled
        d0[at] = FIRST * scaled

    blocks(0, 20, 4, setup)

    def second(start):
        at = pl.ds(start, 6)
        here = d0[at]
        scaled = g0[at] - here + spread(c0, (at,), near(d0, start, 6))
        g0[at] = scaled
        e0[at] = KEEP * here + ADD * scaled

    blocks(1, 19, 6, second)

    def left(start):
        at = pl.ds(start, 4)
        rest = diag0[at] * (g0[at] - e0[at] + spread(c0, (at,), near(e0, start, 4)))
        sums[start // 2 - 1] = 0.5 * (rest[0] + rest[1])
        sums[start // 2] = 0.5 * (rest[2] + rest[3])

    blocks(2, 18, 4, left)
    for index in range(10):
        sums[index + 8] = 0.125 * (k0[2 * index + 1] + k0[2 * index + 2])
    fold = ones_where(iota((256, 128), 0) // 2 == iota((256, 128), 1))
    zsums[...] = dot(sums[...].reshape(18 * 24, 256), fold).reshape(18, 24, 128)

    k1[...] = jnp.zeros_like(k1)
    f1[...] = jnp.zeros_like(f1)
    rows = zsums[:, pl.ds(0, 12, stride=2), :] + zsums[:, pl.ds(1, 12, stride=2), :]
    f1[:, 2:14, :] = rows[0:8]
    k1[:, 2:14, :] = rows[8:18]
    up_ref[0:6] = k1[1:7, 4:12, :]
    up_ref[6:11] = f1[1:6, 4:12, :]
    down_ref[0:6] = k1[3:9, 4:12, :]
    down_ref[6:11] = f1[2:7, 4:12, :]
    side_ref[0:10] = k1[:, 4:12, :]
    side_ref[10:18] = f1[:, 4:12, :]


def next_kernel(k1, f1, copies_ref, c1, diag1, g1, d1, e1, out):
    def setup1(start):
        at = pl.ds(start, 4)
        couplings, inverse, diagonal = coupling(k1[pl.ds(start + 1, 4)], near_inside(k1, start + 1, 4), (4, 5))
        for number in range(6):
            c1.at[number][at] = couplings[number]
        diag1[at] = diagonal
        scaled = inverse * f1[at]
        g1[at] = scaled
        d1[at] = FIRST * scaled

    blocks(0, 8, 4, setup1)
    at = pl.ds(1, 6)
    scaled = g1[at] - d1[at] + spread(c1, (at,), near(d1, 1, 6))
    g1[at] = scaled
    e1[at] = KEEP * d1[at] + ADD * scaled
    at = pl.ds(2, 4)
    rest = diag1[at] * (g1[at] - e1[at] + spread(c1, (at,), near(e1, 2, 4)))
    for half in range(2):
        out[half] = 0.5 * (rest[2 * half] + rest[2 * half + 1])
        out[half + 2] = 0.125 * (k1[2 * half + 3] + k1[2 * half + 4])
    row, lane = iota((128, 256), 0), iota((128, 256), 1)
    fold = ones_where((lane == row // 2) | (lane == 192 + row // 2))
    folded = dot(out[...].reshape(64, 128), fold).reshape(4, 16, 256)
    lines = [folded[number, 6:7, 0:128] + folded[number, 7:8, 0:128]
             + folded[number, 8:9, 128:256] + folded[number, 9:10, 128:256] for number in range(4)]
    payload = jnp.concatenate(lines, 0)

    copies_ref[...] = jnp.broadcast_to(payload[None], copies_ref.shape)


def near2(ref, start, size):
    here = ref[pl.ds(start, size)]
    below, above = ref[pl.ds(start - 1, size)], ref[pl.ds(start + 1, size)]
    z_low, z_high = shifted(here, -1, 3), shifted(here, 1, 3)
    turned = shifted(here, 64, 3)
    turned0, turned1 = turned[:, 0:1], turned[:, 1:2]
    first = iota(turned0.shape, 3) < 64
    y_high = [jnp.where(first, turned0, turned1), jnp.where(first, turned1, shifted(turned0, 1, 2))]
    y_low = [jnp.where(first, shifted(turned1, -1, 2), turned0), jnp.where(first, turned0, turned1)]
    return below, above, jnp.concatenate(y_low, 1), jnp.concatenate(y_high, 1), z_low, z_high


def near2_inside(ref, start, size):
    x_low, x_high, y_low, y_high, z_low, z_high = near2(ref, start, size)
    core, row, lane = (iota(z_low.shape, dim) for dim in (1, 2, 3))
    last = z_low.shape[2] - 1
    y_low = jnp.where((core == 0) & (row == 0) & (lane < 64), 0.0, y_low)
    y_high = jnp.where((core == 1) & (row == last) & (lane >= 64), 0.0, y_high)
    z_low = jnp.where(lane % 64 == 0, 0.0, z_low)
    z_high = jnp.where(lane % 64 == 63, 0.0, z_high)
    return x_low, x_high, y_low, y_high, z_low, z_high


def near3(value):
    count = value.shape[0]
    before, after = shifted(value[count - 1:], -32, 3), shifted(value[0:1], 32, 3)
    x_low = jnp.concatenate([before, value[:count - 1]], 0) if count > 1 else before
    x_high = jnp.concatenate([value[1:], after], 0) if count > 1 else after
    core0, core1 = value[:, 0:1], value[:, 1:2]
    y_low = jnp.concatenate([shifted(core1, -1, 2), core0], 1)
    y_high = jnp.concatenate([core1, shifted(core0, 1, 2)], 1)
    return x_low, x_high, y_low, y_high, shifted(value, -1, 3), shifted(value, 1, 3)


def near3_inside(value):
    x_low, x_high, y_low, y_high, z_low, z_high = near3(value)
    plane, core, row, lane = (iota(value.shape, dim) for dim in range(4))
    count, rows = value.shape[0], value.shape[2]
    x_low = jnp.where((plane == 0) & (lane < 32), 0.0, x_low)
    x_high = jnp.where((plane == count - 1) & (lane >= 96), 0.0, x_high)
    y_low = jnp.where((core == 0) & (row == 0), 0.0, y_low)
    y_high = jnp.where((core == 1) & (row == rows - 1), 0.0, y_high)
    z_low = jnp.where(lane % 32 == 0, 0.0, z_low)
    z_high = jnp.where(lane % 32 == 31, 0.0, z_high)
    return x_low, x_high, y_low, y_high, z_low, z_high


def make_coarse_kernel(count_x, count_y):
    planes2, rows, count3 = 2 * count_x, count_y // 2, count_x // 4
    size = 16
    line = (2, rows, 128)

    def coarse_kernel(place_ref, mine_ref, other_ref, near_ref,
                      k2, c2, diag2, g2, d2, e2, h2, sums, c3, e3, x0):
        at_x, at_y = place_ref[0], place_ref[1]
        zero = jnp.zeros((4, *line), F32)
        for ends in (pl.ds(0, 4), pl.ds(planes2 + 4, 4)):
            for ref in (k2, g2, d2, e2):
                ref[ends] = zero
            for number in range(6):
                c2.at[number][ends] = zero

        core = at_y % 2

        def load(index):
            for half in range(2):
                start = index * (4 * rows) + half
                to = 2 * index + half + 4
                for ref, side in ((mine_ref, core), (other_ref, 1 - core)):
                    k2[to, side] = ref[pl.ds(start + 2, rows, stride=4), :]
                    e2[to, side] = ref[pl.ds(start, rows, stride=4), :]

        def load_some(start):
            for index in range(4):
                load(start + index)

        blocks(0, count_x, 4, load_some)

        def setup(start):
            at = pl.ds(start, size)
            couplings, inverse, diagonal = coupling(k2[at], near2_inside(k2, start, size), (2, 3, 4, 5))
            for number in range(6):
                c2.at[number][at] = couplings[number]
            diag2[at] = diagonal
            scaled = inverse * e2[at]
            g2[at] = scaled
            d2[at] = FIRST * scaled

        blocks(4, planes2 + 4, size, setup)

        def second(start):
            at = pl.ds(start, size)
            here = d2[at]
            scaled = g2[at] - here + spread(c2, (at,), near2(d2, start, size))
            h2[at] = scaled
            e2[at] = KEEP * here + ADD * scaled

        blocks(4, planes2 + 4, size, second)

        def left(start):
            at = pl.ds(start, size)
            rest = diag2[at] * (h2[at] - e2[at] + spread(c2, (at,), near2(e2, start, size)))
            rest = rest.reshape(size // 2, 2, *line)
            here = k2[at].reshape(size // 2, 2, *line)
            to = (start - 4) // 2
            sums[pl.ds(to, size // 2)] = 0.5 * (rest[:, 0] + rest[:, 1])
            sums[pl.ds(to + count_x, size // 2)] = 0.125 * (here[:, 0] + here[:, 1])

        blocks(4, planes2 + 4, size, left)

        flat = count3 * 2 * rows
        row, lane = iota((512, 128), 0), iota((512, 128), 1)
        fold = ones_where(lane == 32 * (row // 128) + (row % 64) // 2)
        quarters = [jnp.concatenate([sums[pl.ds(first + quarter * count3, count3)].reshape(flat, 128)
                                     for first in (0, count_x)], 0) for quarter in range(4)]
        folded = dot(jnp.concatenate(quarters, 1), fold)
        f3 = folded[0:flat].reshape(count3, *line)
        k3 = folded[flat:].reshape(count3, *line)
        couplings, inverse, _ = coupling(k3, near3_inside(k3), (0, 1, 2, 3, 4, 5))
        for number in range(6):
            c3[number] = couplings[number]
        scaled = inverse * f3
        step = COARSE_FACTORS[0][1] * scaled
        total = step
        for keep, add in COARSE_FACTORS[1:]:
            scaled = scaled - step + spread(c3, (), near3(step))
            step = keep * step + add * scaled
            total = total + step
        e3[...] = total

        base = 2 * at_x
        parts = []
        for number in range(5):
            x3 = at_x - 2 + number
            inside = (x3 >= 0) & (x3 < count_x)
            safe = jnp.clip(x3, 0, count_x - 1)
            plane = pltpu.roll(e3[safe % count3].reshape(2 * rows, 128), (128 - 32 * (safe // count3)) % 128, 1)
            parts.append(jnp.where(inside, plane, 0.0))
        row, lane = iota((128, 128), 0), iota((128, 128), 1)
        unfold = ones_where((row < 32) & ((lane % 64) // 2 == row))
        up = dot(jnp.concatenate(parts, 0), unfold).reshape(5, *line)
        local = pl.ds(base, 10)
        twice = jnp.stack([up, up], 1).reshape(10, *line)
        x0[...] = d2[local] + e2[local] + twice
        inner = pl.ds(base + 1, 8)
        scaled = g2[inner] - x0[1:9] + spread(c2, (inner,), near2(x0, 1, 8))
        h2[0:8] = scaled
        d2[0:8] = FIRST * scaled
        inner = pl.ds(base + 2, 6)
        here = d2[1:7]
        scaled = h2[1:7] - here + spread(c2, (inner,), near2(d2, 1, 6))
        found = x0[2:8] + (1.0 + KEEP) * here + ADD * scaled

        row, lane = iota((128, 256), 0), iota((128, 256), 1)
        widen = ones_where(row == 64 * (lane // 128) + (lane % 128) // 2)
        wide = dot(found.reshape(6 * 2 * rows, 128), widen)
        target, source = iota((16, 4 * rows), 0), iota((16, 4 * rows), 1)
        half, source = source // (2 * rows), source % (2 * rows)
        source = 2 * (source % rows) + source // rows
        inside = (target >= 2) & (target < 14) & (source == at_y - 1 + (target - 2) // 4)
        spread_rows = ones_where(inside & (((target - 2) % 4) // 2 == half))
        both = [jnp.concatenate([wide[2 * rows * index:2 * rows * (index + 1), 128 * half:128 * half + 128]
                                 for index in range(6)], 1) for half in range(2)]
        near_e = dot_left(spread_rows, jnp.concatenate(both, 0))
        for index in range(6):
            near_ref[index] = near_e[:, 128 * index:128 * index + 128]

    return coarse_kernel


def prepare_kernel(k_ref, f_ref, after_ref, w0, g0, x0, d0):
    def cut(value):
        return shifted(value, 4, 1)[:, 0:16]

    def setup0(start):
        at = pl.ds(start, 4)
        faces = face_sums(k_ref, start + 3, 4)
        for number in range(4):
            w0.at[number][at] = cut(faces[number])
        scaled = cut(2.0 * faces[3] * f_ref[pl.ds(start + 2, 4)])
        g0[at] = scaled
        d0[at] = FIRST * scaled

    blocks(0, 16, 4, setup0)

    def guess0(start):
        at = pl.ds(start, 7)
        here = d0[at]
        scaled = g0[at] - here + spread_faces(w0, d0, start, 7)
        x0[at] = (1.0 + KEEP) * here + ADD * scaled

    blocks(1, 15, 7, guess0)


def gate_kernel(*refs):
    pass


def prepare1_kernel(k_ref, f_ref, x_low_ref, x_high_ref, y_low_ref, y_high_ref, after_ref, w1, g1, x1, k1, f1, d1):
    row = iota((8, 128), 0)

    def join(low, middle, high):
        middle = shifted(middle, 4, 1)
        return jnp.concatenate([jnp.where(row < 6, low, middle), jnp.where(row < 2, middle, high)], 1)

    def alone(tiles):
        tiles = shifted(tiles, 4, 1)
        return jnp.concatenate([tiles, tiles], 1)

    middle = jnp.concatenate([x_low_ref[3:6], k_ref[3:7, 4:12, :], x_high_ref[0:3]], 0)
    k1[0:3] = alone(x_low_ref[0:3])
    k1[3:13] = join(y_low_ref[0:10], middle, y_high_ref[0:10])
    k1[13:16] = alone(x_high_ref[3:6])
    middle = jnp.concatenate([x_low_ref[9:11], f_ref[2:6, 4:12, :], x_high_ref[6:8]], 0)
    f1[1:4] = alone(x_low_ref[6:9])
    f1[4:12] = join(y_low_ref[10:18], middle, y_high_ref[10:18])
    f1[12:15] = alone(x_high_ref[8:11])

    def setup1(start):
        at = pl.ds(start, 7)
        faces = face_sums(k1, start, 7)
        for number in range(4):
            w1.at[number][at] = faces[number]
        scaled = 2.0 * faces[3] * f1[at]
        g1[at] = scaled
        d1[at] = FIRST * scaled

    blocks(1, 15, 7, setup1)
    at = pl.ds(2, 12)
    here = d1[at]
    scaled = g1[at] - here + spread_faces(w1, d1, 2, 12)
    x1[at] = (1.0 + KEEP) * here + ADD * scaled


def post_kernel(near_ref, w1, g1, x1, w0, g0, x0, correction_ref, residual_ref,
                y1, d1, h1, wide, y0, d0, h0, v0):
    up = near_ref[...]
    y1[2:14] = x1[2:14] + jnp.stack([up, up], 1).reshape(12, 16, 128)
    scaled = g1[3:13] - y1[3:13] + spread_faces(w1, y1, 3, 10)
    h1[3:13] = scaled
    d1[3:13] = FIRST * scaled
    here = d1[4:12]
    scaled = h1[4:12] - here + spread_faces(w1, d1, 4, 8)
    found = y1[4:12] + (1.0 + KEEP) * here + ADD * scaled
    wide[:, pl.ds(0, 8, stride=2), :] = found[:, 4:12]
    wide[:, pl.ds(1, 8, stride=2), :] = found[:, 4:12]
    unfold = ones_where(iota((128, 256), 0) == iota((128, 256), 1) // 2)
    up = dot(wide[...].reshape(128, 128), unfold).reshape(8, 16, 256)

    for index in range(1, 15):
        y0[index] = x0[index] + up[index // 2]

    def first0(start):
        at = pl.ds(start, 6)
        scaled = g0[at] - y0[at] + spread_faces(w0, y0, start, 6)
        h0[at] = scaled
        d0[at] = FIRST * scaled

    blocks(2, 14, 6, first0)

    def second0(start):
        at = pl.ds(start, 5)
        here = d0[at]
        scaled = h0[at] - here + spread_faces(w0, d0, start, 5)
        h0[at] = scaled
        v0[at] = KEEP * here + ADD * scaled

    blocks(3, 13, 5, second0)

    def last0(start):
        at, to = pl.ds(start, 4), pl.ds(start - 4, 4)
        here = v0[at]
        correction_ref[to] = (y0[at] + d0[at] + here)[:, 4:12]
        scaled = h0[at] - here + spread_faces(w0, v0, start, 4)
        residual_ref[to] = scaled[:, 4:12] * (0.5 / w0.at[3][at][:, 4:12])

    blocks(4, 12, 4, last0)


def call(kernel, limit, shapes, scratch, *operands, scalars=0, flops=0):
    specs = [pl.BlockSpec(memory_space=pltpu.SMEM)] * scalars
    specs += [pl.BlockSpec(memory_space=pltpu.VMEM)] * (len(operands) - scalars)
    return pl.pallas_call(
        kernel,
        out_shape=[jax.ShapeDtypeStruct(shape, F32) for shape in shapes],
        in_specs=specs,
        out_specs=[pl.BlockSpec(memory_space=pltpu.VMEM)] * len(shapes),
        scratch_shapes=[pltpu.VMEM(shape, F32) for shape in scratch],
        compiler_params=pltpu.CompilerParams(vmem_limit_bytes=limit * MIB),
        cost_estimate=pl.CostEstimate(flops=flops, bytes_accessed=0, transcendentals=0) if flops else None,
        interpret=INTERPRET,
    )(*operands)


def both_sides(up, down, axes):
    count = math.prod(lax.axis_size(axis) for axis in axes)
    low = lax.ppermute(up, axes, [(i, i + 1) for i in range(count - 1)])
    high = lax.ppermute(down, axes, [(i + 1, i) for i in range(count - 1)])
    return low, high


def body(f, k):
    count_x, chips = lax.axis_size("gx"), lax.axis_size("chip")
    count_y = 2 * chips
    along_x, along_y = ("gx",), ("chip", "core")
    tile, full, half = f.shape[1:], (24, 256), (16, 256)
    tile1, full1 = (8, 128), (16, 128)
    core = lax.axis_index("core").astype(jnp.int32).reshape(1)
    one, two, own = pl.pallas_call(
        pack_x_kernel,
        out_shape=[jax.ShapeDtypeStruct((planes, *tile), F32) for planes in (13, 13, 16)],
        in_specs=[pl.BlockSpec(memory_space=pltpu.SMEM)] + [pl.BlockSpec(memory_space=pltpu.HBM)] * 2,
        out_specs=[pl.BlockSpec(memory_space=pltpu.VMEM)] * 3,
        scratch_shapes=[pltpu.SemaphoreType.DMA((6,))],
        compiler_params=pltpu.CompilerParams(vmem_limit_bytes=4 * MIB),
        interpret=INTERPRET,
    )(core, k, f)
    route = [(2 * i, 2 * i + 2) for i in range(count_x - 1)] + [(2 * i + 3, 2 * i + 1) for i in range(count_x - 1)]
    one = lax.ppermute(one, ("gx", "core"), route)
    two = lax.ppermute(two, ("gx", "core"), [(to, source) for source, to in route])
    packed, outer = call(pack_y_kernel, 4, [(Y_TILES, *tile)] * 2, [], core, own, one, two, scalars=1)
    sibling = lax.ppermute(packed, "core", [(0, 1), (1, 0)])
    after = lax.ppermute(outer, along_y, [pair for i in range(1, count_y - 1, 2) for pair in ((i, i + 1), (i + 1, i))])

    k0, f0, k1, f1, up, down, side = call(
        fine_kernel, 16,
        [(22, *full), (20, *full), (10, *full1), (8, *full1), (11, *tile1), (11, *tile1), (18, *tile1)],
        [(6, 20, *full)] + [(20, *full)] * 4 + [(18, *full), (18, 24, 128)],
        core, packed, one, two, sibling, after, scalars=1)
    x_low, x_high = both_sides(up, down, along_x)
    y_low, y_high = both_sides(side, side, along_y)
    copies, = call(
        next_kernel, 8,
        [(chips, 4, 128)],
        [(6, 8, *full1)] + [(8, *full1)] * 4 + [(4, *full1)],
        k1, f1)

    line = lax.all_to_all(copies, "chip", 0, 0).reshape(-1, 128)
    copies = jnp.broadcast_to(line[None], (count_x, *line.shape))
    mine = lax.all_to_all(copies, "gx", 0, 0).reshape(-1, 128)
    waited = (mine, x_low, x_high, y_low, y_high)
    mine = pl.pallas_call(
        gate_kernel,
        out_shape=jax.ShapeDtypeStruct(mine.shape, F32),
        in_specs=[pl.BlockSpec(memory_space=pltpu.VMEM)] * len(waited),
        out_specs=pl.BlockSpec(memory_space=pltpu.VMEM),
        input_output_aliases={0: 0},
        compiler_params=pltpu.CompilerParams(vmem_limit_bytes=4 * MIB),
        interpret=INTERPRET,
    )(*waited)
    other = lax.ppermute(mine, "core", [(0, 1), (1, 0)])

    prepared = call(
        prepare_kernel, 16,
        [(4, 16, *half)] + [(16, *half)] * 2,
        [(16, *half)],
        k0, f0, mine)
    prepared1 = call(
        prepare1_kernel, 8,
        [(4, 16, *full1)] + [(16, *full1)] * 2,
        [(16, *full1)] * 3,
        k1, f1, x_low, x_high, y_low, y_high, mine)

    place = jnp.stack([lax.axis_index("gx"), lax.axis_index(("chip", "core"))]).astype(jnp.int32)
    plane2 = (2, count_y // 2, 128)
    padded = (2 * count_x + 8, *plane2)
    near_e, = call(
        make_coarse_kernel(count_x, count_y), 20,
        [(6, 16, 128)],
        [padded, (6, *padded)] + [padded] * 5
        + [(2 * count_x, *plane2), (6, count_x // 4, *plane2), (count_x // 4, *plane2), (10, *plane2)],
        place, mine, other, scalars=1, flops=6000000000)

    correction, residual = call(
        post_kernel, 16,
        [f.shape, f.shape],
        [(16, *full1)] * 3 + [(8, *full1)] + [(16, *half)] * 4,
        near_e, *prepared1, *prepared)
    return correction, residual


def solution(mesh):
    shape = (mesh.shape["gx"], mesh.shape["gy"] // 2, 2)
    mesh = jax.sharding.Mesh(mesh.devices.reshape(shape), ("gx", "chip", "core"))
    spec = P("gx", ("chip", "core"), None)
    return jax.shard_map(body, mesh=mesh, in_specs=(spec, spec), out_specs=(spec, spec), check_vma=False)
```

```python
import math

import jax
import jax.numpy as jnp
from jax import lax
from jax.experimental import pallas as pl
from jax.experimental.pallas import tpu as pltpu
from jax.sharding import PartitionSpec as P

INTERPRET = False
COARSE_STEPS = 8
F32 = jnp.float32
MIB = 1024 * 1024


def step_factors(low_end, steps):
    center, radius = 0.5 * (2.0 + low_end), 0.5 * (2.0 - low_end)
    sigma = center / radius
    ratio = 1.0 / sigma
    factors = [(0.0, 1.0 / center)]
    for _ in range(steps - 1):
        ratio_next = 1.0 / (2.0 * sigma - ratio)
        factors.append((ratio_next * ratio, 2.0 * ratio_next / radius))
        ratio = ratio_next
    return factors


(_, FIRST), (KEEP, ADD) = step_factors(0.4, 2)
COARSE_FACTORS = step_factors(0.02, COARSE_STEPS)


def iota(shape, dim):
    return lax.broadcasted_iota(jnp.int32, shape, dim)


def shifted(value, step, axis):
    return pltpu.roll(value, (-step) % value.shape[axis], axis)


def parts_of(value):
    parts = []
    for _ in range(3):
        part = value.astype(jnp.bfloat16)
        parts.append(part)
        value = value - part.astype(F32)
    return parts


def ones_where(condition):
    return jnp.where(condition, 1.0, 0.0).astype(jnp.bfloat16)


def dot(a, ones):
    rows = a.shape[0]
    out = jnp.dot(jnp.concatenate(parts_of(a), 0), ones, preferred_element_type=F32)
    return out[0:rows] + out[rows:2 * rows] + out[2 * rows:]


def dot_left(ones, a):
    columns = a.shape[1]
    out = jnp.dot(ones, jnp.concatenate(parts_of(a), 1), preferred_element_type=F32)
    return out[:, 0:columns] + out[:, columns:2 * columns] + out[:, 2 * columns:]


def blocks(first, last, size, step):
    count = (last - first) // size
    assert first + count * size == last
    if count == 1:
        step(first)
        return

    def one(number, carry):
        step(first + number * size)
        return carry

    lax.fori_loop(0, count, one, 0)


def near(ref, start, size):
    here = ref[pl.ds(start, size)]
    return (ref[pl.ds(start - 1, size)], ref[pl.ds(start + 1, size)],
            shifted(here, -1, 1), shifted(here, 1, 1), shifted(here, -1, 2), shifted(here, 1, 2))


def near_inside(ref, start, size):
    x_low, x_high, y_low, y_high, z_low, z_high = near(ref, start, size)
    lane = iota(z_low.shape, 2)
    z_low = jnp.where(lane == 0, 0.0, z_low)
    z_high = jnp.where(lane == z_low.shape[2] - 1, 0.0, z_high)
    return x_low, x_high, y_low, y_high, z_low, z_high


def coupling(center, around, masked):
    total = 6.0 * center
    for value in around:
        total = total + value
    inside = center > 0.0
    half_inverse = jnp.where(inside, 1.0 / jnp.where(inside, total, 1.0), 0.0)
    couplings = []
    for number, value in enumerate(around):
        c = (center + value) * half_inverse
        couplings.append(jnp.where(value > 0.0, c, 0.0) if number in masked else c)
    return couplings, 2.0 * half_inverse, 0.5 * total


def pick(c_ref, number, where):
    return c_ref.at[number][where] if where else c_ref[number]


def spread(c_ref, where, around):
    total = pick(c_ref, 0, where) * around[0]
    for number in range(1, 6):
        total = total + pick(c_ref, number, where) * around[number]
    return total


def face_sums(k_ref, start, size):
    center = k_ref[pl.ds(start, size)]
    around = near_inside(k_ref, start, size)
    total = 6.0 * center
    for value in around:
        total = total + value
    inside = center > 0.0
    half_inverse = jnp.where(inside, 1.0 / jnp.where(inside, total, 1.0), 0.0)
    return (center + around[1], center + around[3], jnp.where(around[5] > 0.0, center + around[5], 0.0), half_inverse)


def spread_faces(w_ref, v_ref, start, size):
    at = pl.ds(start, size)
    here, along_y, along_z = v_ref[at], w_ref.at[1][at], w_ref.at[2][at]
    total = w_ref.at[0][at] * v_ref[pl.ds(start + 1, size)]
    total = total + w_ref.at[0][pl.ds(start - 1, size)] * v_ref[pl.ds(start - 1, size)]
    total = total + along_y * shifted(here, 1, 1) + shifted(along_y * here, -1, 1)
    total = total + along_z * shifted(here, 1, 2) + shifted(along_z * here, -1, 2)
    return w_ref.at[3][at] * total


PAIRS = ([("k", dx, 7 - dx) for dx in (1, 2, 3)], [("f", dx, 6 - dx) for dx in (1, 2, 3)])
Y_TILES = 28


def pack_x_kernel(core_ref, k_ref, f_ref, one_ref, two_ref, own_ref, done):
    core = core_ref[0]
    pieces = ((k_ref, 1 - core, one_ref, 0, 7), (f_ref, 2 - 2 * core, one_ref, 7, 6),
              (k_ref, core, two_ref, 0, 7), (f_ref, 2 * core, two_ref, 7, 6),
              (k_ref, 0, own_ref, 0, 8), (f_ref, 0, own_ref, 8, 8))
    copies = [pltpu.make_async_copy(ref.at[pl.ds(first, size)], to.at[pl.ds(place, size)], done.at[number])
              for number, (ref, first, to, place, size) in enumerate(pieces)]
    for copy in copies:
        copy.start()
    for copy in copies:
        copy.wait()


def chosen(first_core, one_ref, two_ref):
    def low(at):
        return jnp.where(first_core, one_ref[at], two_ref[at])

    def high(at):
        return jnp.where(first_core, two_ref[at], one_ref[at])

    return low, high


def pair_tiles():
    tile = 16
    for pairs in PAIRS:
        for side in ("low", "high"):
            for name, dx, far in pairs:
                yield tile, name, side, dx, far
                tile += 1


def halo_plane(name, side, dx, x_low, x_high):
    reach = 7 if name == "k" else 6
    base = 0 if name == "k" else 7
    return x_low(base + reach - dx) if side == "low" else x_high(base + dx - 1)


def pack_y_kernel(core_ref, own_ref, x_one_ref, x_two_ref, sibling_ref, next_ref):
    first_core = core_ref[0] == 0
    x_low, x_high = chosen(first_core, x_one_ref, x_two_ref)
    for ref in (sibling_ref, next_ref):
        ref[0:16] = own_ref[...]
    row = iota((8, own_ref.shape[2]), 0)
    for tile, name, side, dx, far in pair_tiles():
        near_plane = halo_plane(name, side, dx, x_low, x_high)
        far_plane = halo_plane(name, side, far, x_low, x_high)
        up = jnp.where(row < dx, shifted(far_plane, 8 - dx, 0), near_plane)
        down = jnp.where(row >= 8 - dx, shifted(far_plane, dx - 8, 0), near_plane)
        sibling_ref[tile] = jnp.where(first_core, up, down)
        next_ref[tile] = jnp.where(first_core, down, up)


def unpack(first_core, own_ref, x_one_ref, x_two_ref, sibling_ref, next_ref, k0, f0):
    x_low, x_high = chosen(first_core, x_one_ref, x_two_ref)
    below, above = chosen(first_core, next_ref, sibling_ref)
    for to, base, reach, name in ((k0, 0, 7, "k"), (f0, 8, 6, "f")):
        tiles = pl.ds(base, 8)
        to[reach:reach + 8, 0:8] = below(tiles)
        to[reach:reach + 8, 8:16] = own_ref[tiles]
        to[reach:reach + 8, 16:24] = above(tiles)
        first = 0 if name == "k" else 7
        to[0:reach, 8:16] = x_low(pl.ds(first, reach))
        to[reach + 8:2 * reach + 8, 8:16] = x_high(pl.ds(first, reach))
        for plane in (0, 2 * reach + 7):
            to[plane, 0:8] = jnp.zeros(own_ref.shape[1:], F32)
            to[plane, 16:24] = jnp.zeros(own_ref.shape[1:], F32)
    for tile, name, side, dx, far in pair_tiles():
        to, reach = (k0, 7) if name == "k" else (f0, 6)
        near_plane = reach - dx if side == "low" else reach + 7 + dx
        far_plane = reach - far if side == "low" else reach + 7 + far
        low, high = below(tile), above(tile)
        to[near_plane, 0:8] = low
        to[near_plane, 16:24] = high
        if far != dx:
            to[far_plane, 0:8] = shifted(low, dx - 8, 0)
            to[far_plane, 16:24] = shifted(high, 8 - dx, 0)


def fine_kernel(core_ref, own_ref, x_one_ref, x_two_ref, sibling_ref, next_ref,
                k0, f0, k1, f1, up_ref, down_ref, side_ref,
                c0, diag0, g0, d0, e0, sums, zsums):
    unpack(core_ref[0] == 0, own_ref, x_one_ref, x_two_ref, sibling_ref, next_ref, k0, f0)

    def setup(start):
        at = pl.ds(start, 4)
        couplings, inverse, diagonal = coupling(k0[pl.ds(start + 1, 4)], near_inside(k0, start + 1, 4), (4, 5))
        for number in range(6):
            c0.at[number][at] = couplings[number]
        diag0[at] = diagonal
        scaled = inverse * f0[at]
        g0[at] = scaled
        d0[at] = FIRST * scaled

    blocks(0, 20, 4, setup)

    def second(start):
        at = pl.ds(start, 6)
        here = d0[at]
        scaled = g0[at] - here + spread(c0, (at,), near(d0, start, 6))
        g0[at] = scaled
        e0[at] = KEEP * here + ADD * scaled

    blocks(1, 19, 6, second)

    def left(start):
        at = pl.ds(start, 4)
        rest = diag0[at] * (g0[at] - e0[at] + spread(c0, (at,), near(e0, start, 4)))
        sums[start // 2 - 1] = 0.5 * (rest[0] + rest[1])
        sums[start // 2] = 0.5 * (rest[2] + rest[3])

    blocks(2, 18, 4, left)
    for index in range(10):
        sums[index + 8] = 0.125 * (k0[2 * index + 1] + k0[2 * index + 2])
    fold = ones_where(iota((256, 128), 0) // 2 == iota((256, 128), 1))
    zsums[...] = dot(sums[...].reshape(18 * 24, 256), fold).reshape(18, 24, 128)

    k1[...] = jnp.zeros_like(k1)
    f1[...] = jnp.zeros_like(f1)
    rows = zsums[:, pl.ds(0, 12, stride=2), :] + zsums[:, pl.ds(1, 12, stride=2), :]
    f1[:, 2:14, :] = rows[0:8]
    k1[:, 2:14, :] = rows[8:18]
    up_ref[0:6] = k1[1:7, 4:12, :]
    up_ref[6:11] = f1[1:6, 4:12, :]
    down_ref[0:6] = k1[3:9, 4:12, :]
    down_ref[6:11] = f1[2:7, 4:12, :]
    side_ref[0:10] = k1[:, 4:12, :]
    side_ref[10:18] = f1[:, 4:12, :]


def next_kernel(k1, f1, copies_ref, c1, diag1, g1, d1, e1, out):
    def setup1(start):
        at = pl.ds(start, 4)
        couplings, inverse, diagonal = coupling(k1[pl.ds(start + 1, 4)], near_inside(k1, start + 1, 4), (4, 5))
        for number in range(6):
            c1.at[number][at] = couplings[number]
        diag1[at] = diagonal
        scaled = inverse * f1[at]
        g1[at] = scaled
        d1[at] = FIRST * scaled

    blocks(0, 8, 4, setup1)
    at = pl.ds(1, 6)
    scaled = g1[at] - d1[at] + spread(c1, (at,), near(d1, 1, 6))
    g1[at] = scaled
    e1[at] = KEEP * d1[at] + ADD * scaled
    at = pl.ds(2, 4)
    rest = diag1[at] * (g1[at] - e1[at] + spread(c1, (at,), near(e1, 2, 4)))
    for half in range(2):
        out[half] = 0.5 * (rest[2 * half] + rest[2 * half + 1])
        out[half + 2] = 0.125 * (k1[2 * half + 3] + k1[2 * half + 4])
    row, lane = iota((128, 256), 0), iota((128, 256), 1)
    fold = ones_where((lane == row // 2) | (lane == 192 + row // 2))
    folded = dot(out[...].reshape(64, 128), fold).reshape(4, 16, 256)
    lines = [folded[number, 6:7, 0:128] + folded[number, 7:8, 0:128]
             + folded[number, 8:9, 128:256] + folded[number, 9:10, 128:256] for number in range(4)]
    payload = jnp.concatenate(lines, 0)


    def copy(start):
        copies_ref[pl.ds(start, 8)] = jnp.broadcast_to(payload[None], (8, 4, 128))

    blocks(0, copies_ref.shape[0], 8, copy)


def near2(ref, start, size):
    here = ref[pl.ds(start, size)]
    below, above = ref[pl.ds(start - 1, size)], ref[pl.ds(start + 1, size)]
    z_low, z_high = shifted(here, -1, 3), shifted(here, 1, 3)
    turned = shifted(here, 64, 3)
    turned0, turned1 = turned[:, 0:1], turned[:, 1:2]
    first = iota(turned0.shape, 3) < 64
    y_high = [jnp.where(first, turned0, turned1), jnp.where(first, turned1, shifted(turned0, 1, 2))]
    y_low = [jnp.where(first, shifted(turned1, -1, 2), turned0), jnp.where(first, turned0, turned1)]
    return below, above, jnp.concatenate(y_low, 1), jnp.concatenate(y_high, 1), z_low, z_high


def near2_inside(ref, start, size):
    x_low, x_high, y_low, y_high, z_low, z_high = near2(ref, start, size)
    core, row, lane = (iota(z_low.shape, dim) for dim in (1, 2, 3))
    last = z_low.shape[2] - 1
    y_low = jnp.where((core == 0) & (row == 0) & (lane < 64), 0.0, y_low)
    y_high = jnp.where((core == 1) & (row == last) & (lane >= 64), 0.0, y_high)
    z_low = jnp.where(lane % 64 == 0, 0.0, z_low)
    z_high = jnp.where(lane % 64 == 63, 0.0, z_high)
    return x_low, x_high, y_low, y_high, z_low, z_high


def near3(value):
    count = value.shape[0]
    before, after = shifted(value[count - 1:], -32, 3), shifted(value[0:1], 32, 3)
    x_low = jnp.concatenate([before, value[:count - 1]], 0) if count > 1 else before
    x_high = jnp.concatenate([value[1:], after], 0) if count > 1 else after
    core0, core1 = value[:, 0:1], value[:, 1:2]
    y_low = jnp.concatenate([shifted(core1, -1, 2), core0], 1)
    y_high = jnp.concatenate([core1, shifted(core0, 1, 2)], 1)
    return x_low, x_high, y_low, y_high, shifted(value, -1, 3), shifted(value, 1, 3)


def near3_inside(value):
    x_low, x_high, y_low, y_high, z_low, z_high = near3(value)
    plane, core, row, lane = (iota(value.shape, dim) for dim in range(4))
    count, rows = value.shape[0], value.shape[2]
    x_low = jnp.where((plane == 0) & (lane < 32), 0.0, x_low)
    x_high = jnp.where((plane == count - 1) & (lane >= 96), 0.0, x_high)
    y_low = jnp.where((core == 0) & (row == 0), 0.0, y_low)
    y_high = jnp.where((core == 1) & (row == rows - 1), 0.0, y_high)
    z_low = jnp.where(lane % 32 == 0, 0.0, z_low)
    z_high = jnp.where(lane % 32 == 31, 0.0, z_high)
    return x_low, x_high, y_low, y_high, z_low, z_high


def make_coarse_kernel(count_x, count_y):
    planes2, rows, count3 = 2 * count_x, count_y // 2, count_x // 4
    size = 16
    line = (2, rows, 128)

    def coarse_kernel(place_ref, mine_ref, other_ref, near_ref,
                      k2, c2, diag2, g2, d2, e2, h2, sums, c3, e3, x0):
        at_x, at_y = place_ref[0], place_ref[1]
        zero = jnp.zeros((4, *line), F32)
        for ends in (pl.ds(0, 4), pl.ds(planes2 + 4, 4)):
            for ref in (k2, g2, d2, e2):
                ref[ends] = zero
            for number in range(6):
                c2.at[number][ends] = zero

        core = at_y % 2

        def load(index):
            for half in range(2):
                start = index * (4 * rows) + half
                to = 2 * index + half + 4
                for ref, side in ((mine_ref, core), (other_ref, 1 - core)):
                    k2[to, side] = ref[pl.ds(start + 2, rows, stride=4), :]
                    e2[to, side] = ref[pl.ds(start, rows, stride=4), :]

        def load_some(start):
            for index in range(4):
                load(start + index)

        blocks(0, count_x, 4, load_some)

        def setup(start):
            at = pl.ds(start, size)
            couplings, inverse, diagonal = coupling(k2[at], near2_inside(k2, start, size), (2, 3, 4, 5))
            for number in range(6):
                c2.at[number][at] = couplings[number]
            diag2[at] = diagonal
            scaled = inverse * e2[at]
            g2[at] = scaled
            d2[at] = FIRST * scaled

        blocks(4, planes2 + 4, size, setup)

        def second(start):
            at = pl.ds(start, size)
            here = d2[at]
            scaled = g2[at] - here + spread(c2, (at,), near2(d2, start, size))
            h2[at] = scaled
            e2[at] = KEEP * here + ADD * scaled

        blocks(4, planes2 + 4, size, second)

        def left(start):
            at = pl.ds(start, size)
            rest = diag2[at] * (h2[at] - e2[at] + spread(c2, (at,), near2(e2, start, size)))
            rest = rest.reshape(size // 2, 2, *line)
            here = k2[at].reshape(size // 2, 2, *line)
            to = (start - 4) // 2
            sums[pl.ds(to, size // 2)] = 0.5 * (rest[:, 0] + rest[:, 1])
            sums[pl.ds(to + count_x, size // 2)] = 0.125 * (here[:, 0] + here[:, 1])

        blocks(4, planes2 + 4, size, left)

        flat = count3 * 2 * rows
        row, lane = iota((512, 128), 0), iota((512, 128), 1)
        fold = ones_where(lane == 32 * (row // 128) + (row % 64) // 2)
        quarters = [jnp.concatenate([sums[pl.ds(first + quarter * count3, count3)].reshape(flat, 128)
                                     for first in (0, count_x)], 0) for quarter in range(4)]
        folded = dot(jnp.concatenate(quarters, 1), fold)
        f3 = folded[0:flat].reshape(count3, *line)
        k3 = folded[flat:].reshape(count3, *line)
        couplings, inverse, _ = coupling(k3, near3_inside(k3), (0, 1, 2, 3, 4, 5))
        for number in range(6):
            c3[number] = couplings[number]
        scaled = inverse * f3
        step = COARSE_FACTORS[0][1] * scaled
        total = step
        for keep, add in COARSE_FACTORS[1:]:
            scaled = scaled - step + spread(c3, (), near3(step))
            step = keep * step + add * scaled
            total = total + step
        e3[...] = total

        base = 2 * at_x
        parts = []
        for number in range(5):
            x3 = at_x - 2 + number
            inside = (x3 >= 0) & (x3 < count_x)
            safe = jnp.clip(x3, 0, count_x - 1)
            plane = pltpu.roll(e3[safe % count3].reshape(2 * rows, 128), (128 - 32 * (safe // count3)) % 128, 1)
            parts.append(jnp.where(inside, plane, 0.0))
        row, lane = iota((128, 128), 0), iota((128, 128), 1)
        unfold = ones_where((row < 32) & ((lane % 64) // 2 == row))
        up = dot(jnp.concatenate(parts, 0), unfold).reshape(5, *line)
        local = pl.ds(base, 10)
        twice = jnp.stack([up, up], 1).reshape(10, *line)
        x0[...] = d2[local] + e2[local] + twice
        inner = pl.ds(base + 1, 8)
        scaled = g2[inner] - x0[1:9] + spread(c2, (inner,), near2(x0, 1, 8))
        h2[0:8] = scaled
        d2[0:8] = FIRST * scaled
        inner = pl.ds(base + 2, 6)
        here = d2[1:7]
        scaled = h2[1:7] - here + spread(c2, (inner,), near2(d2, 1, 6))
        found = x0[2:8] + (1.0 + KEEP) * here + ADD * scaled

        row, lane = iota((128, 256), 0), iota((128, 256), 1)
        widen = ones_where(row == 64 * (lane // 128) + (lane % 128) // 2)
        wide = dot(found.reshape(6 * 2 * rows, 128), widen)
        target, source = iota((16, 4 * rows), 0), iota((16, 4 * rows), 1)
        half, source = source // (2 * rows), source % (2 * rows)
        source = 2 * (source % rows) + source // rows
        inside = (target >= 2) & (target < 14) & (source == at_y - 1 + (target - 2) // 4)
        spread_rows = ones_where(inside & (((target - 2) % 4) // 2 == half))
        both = [jnp.concatenate([wide[2 * rows * index:2 * rows * (index + 1), 128 * half:128 * half + 128]
                                 for index in range(6)], 1) for half in range(2)]
        near_e = dot_left(spread_rows, jnp.concatenate(both, 0))
        for index in range(6):
            near_ref[index] = near_e[:, 128 * index:128 * index + 128]

    return coarse_kernel


def prepare_kernel(k_ref, f_ref, after_ref, w0, g0, x0, d0):
    def cut(value):
        return shifted(value, 4, 1)[:, 0:16]

    def setup0(start):
        at = pl.ds(start, 4)
        faces = face_sums(k_ref, start + 3, 4)
        for number in range(4):
            w0.at[number][at] = cut(faces[number])
        scaled = cut(2.0 * faces[3] * f_ref[pl.ds(start + 2, 4)])
        g0[at] = scaled
        d0[at] = FIRST * scaled

    blocks(0, 16, 4, setup0)

    def guess0(start):
        at = pl.ds(start, 7)
        here = d0[at]
        scaled = g0[at] - here + spread_faces(w0, d0, start, 7)
        x0[at] = (1.0 + KEEP) * here + ADD * scaled

    blocks(1, 15, 7, guess0)


def gate_kernel(*refs):
    pass


def prepare1_kernel(k_ref, f_ref, x_low_ref, x_high_ref, y_low_ref, y_high_ref, after_ref, w1, g1, x1, k1, f1, d1):
    row = iota((8, 128), 0)

    def join(low, middle, high):
        middle = shifted(middle, 4, 1)
        return jnp.concatenate([jnp.where(row < 6, low, middle), jnp.where(row < 2, middle, high)], 1)

    def alone(tiles):
        tiles = shifted(tiles, 4, 1)
        return jnp.concatenate([tiles, tiles], 1)

    middle = jnp.concatenate([x_low_ref[3:6], k_ref[3:7, 4:12, :], x_high_ref[0:3]], 0)
    k1[0:3] = alone(x_low_ref[0:3])
    k1[3:13] = join(y_low_ref[0:10], middle, y_high_ref[0:10])
    k1[13:16] = alone(x_high_ref[3:6])
    middle = jnp.concatenate([x_low_ref[9:11], f_ref[2:6, 4:12, :], x_high_ref[6:8]], 0)
    f1[1:4] = alone(x_low_ref[6:9])
    f1[4:12] = join(y_low_ref[10:18], middle, y_high_ref[10:18])
    f1[12:15] = alone(x_high_ref[8:11])

    def setup1(start):
        at = pl.ds(start, 7)
        faces = face_sums(k1, start, 7)
        for number in range(4):
            w1.at[number][at] = faces[number]
        scaled = 2.0 * faces[3] * f1[at]
        g1[at] = scaled
        d1[at] = FIRST * scaled

    blocks(1, 15, 7, setup1)
    at = pl.ds(2, 12)
    here = d1[at]
    scaled = g1[at] - here + spread_faces(w1, d1, 2, 12)
    x1[at] = (1.0 + KEEP) * here + ADD * scaled


def post_kernel(near_ref, w1, g1, x1, w0, g0, x0, correction_ref, residual_ref,
                y1, d1, h1, wide, y0, d0, h0, v0):
    up = near_ref[...]
    y1[2:14] = x1[2:14] + jnp.stack([up, up], 1).reshape(12, 16, 128)
    scaled = g1[3:13] - y1[3:13] + spread_faces(w1, y1, 3, 10)
    h1[3:13] = scaled
    d1[3:13] = FIRST * scaled
    here = d1[4:12]
    scaled = h1[4:12] - here + spread_faces(w1, d1, 4, 8)
    found = y1[4:12] + (1.0 + KEEP) * here + ADD * scaled
    wide[:, pl.ds(0, 8, stride=2), :] = found[:, 4:12]
    wide[:, pl.ds(1, 8, stride=2), :] = found[:, 4:12]
    unfold = ones_where(iota((128, 256), 0) == iota((128, 256), 1) // 2)
    up = dot(wide[...].reshape(128, 128), unfold).reshape(8, 16, 256)

    for index in range(1, 15):
        y0[index] = x0[index] + up[index // 2]

    def first0(start):
        at = pl.ds(start, 6)
        scaled = g0[at] - y0[at] + spread_faces(w0, y0, start, 6)
        h0[at] = scaled
        d0[at] = FIRST * scaled

    blocks(2, 14, 6, first0)

    def second0(start):
        at = pl.ds(start, 5)
        here = d0[at]
        scaled = h0[at] - here + spread_faces(w0, d0, start, 5)
        h0[at] = scaled
        v0[at] = KEEP * here + ADD * scaled

    blocks(3, 13, 5, second0)

    def last0(start):
        at, to = pl.ds(start, 4), pl.ds(start - 4, 4)
        here = v0[at]
        correction_ref[to] = (y0[at] + d0[at] + here)[:, 4:12]
        scaled = h0[at] - here + spread_faces(w0, v0, start, 4)
        residual_ref[to] = scaled[:, 4:12] * (0.5 / w0.at[3][at][:, 4:12])

    blocks(4, 12, 4, last0)


def call(kernel, limit, shapes, scratch, *operands, scalars=0, flops=0):
    specs = [pl.BlockSpec(memory_space=pltpu.SMEM)] * scalars
    specs += [pl.BlockSpec(memory_space=pltpu.VMEM)] * (len(operands) - scalars)
    return pl.pallas_call(
        kernel,
        out_shape=[jax.ShapeDtypeStruct(shape, F32) for shape in shapes],
        in_specs=specs,
        out_specs=[pl.BlockSpec(memory_space=pltpu.VMEM)] * len(shapes),
        scratch_shapes=[pltpu.VMEM(shape, F32) for shape in scratch],
        compiler_params=pltpu.CompilerParams(vmem_limit_bytes=limit * MIB),
        cost_estimate=pl.CostEstimate(flops=flops, bytes_accessed=0, transcendentals=0) if flops else None,
        interpret=INTERPRET,
    )(*operands)


def both_sides(up, down, axes):
    count = math.prod(lax.axis_size(axis) for axis in axes)
    low = lax.ppermute(up, axes, [(i, i + 1) for i in range(count - 1)])
    high = lax.ppermute(down, axes, [(i + 1, i) for i in range(count - 1)])
    return low, high


def body(f, k):
    count_x, chips = lax.axis_size("gx"), lax.axis_size("chip")
    count_y = 2 * chips
    along_x, along_y = ("gx",), ("chip", "core")
    tile, full, half = f.shape[1:], (24, 256), (16, 256)
    tile1, full1 = (8, 128), (16, 128)
    core = lax.axis_index("core").astype(jnp.int32).reshape(1)
    one, two, own = pl.pallas_call(
        pack_x_kernel,
        out_shape=[jax.ShapeDtypeStruct((planes, *tile), F32) for planes in (13, 13, 16)],
        in_specs=[pl.BlockSpec(memory_space=pltpu.SMEM)] + [pl.BlockSpec(memory_space=pltpu.HBM)] * 2,
        out_specs=[pl.BlockSpec(memory_space=pltpu.VMEM)] * 3,
        scratch_shapes=[pltpu.SemaphoreType.DMA((6,))],
        compiler_params=pltpu.CompilerParams(vmem_limit_bytes=4 * MIB),
        interpret=INTERPRET,
    )(core, k, f)
    route = [(2 * i, 2 * i + 2) for i in range(count_x - 1)] + [(2 * i + 3, 2 * i + 1) for i in range(count_x - 1)]
    one = lax.ppermute(one, ("gx", "core"), route)
    two = lax.ppermute(two, ("gx", "core"), [(to, source) for source, to in route])
    packed, outer = call(pack_y_kernel, 4, [(Y_TILES, *tile)] * 2, [], core, own, one, two, scalars=1)
    sibling = lax.ppermute(packed, "core", [(0, 1), (1, 0)])
    after = lax.ppermute(outer, along_y, [pair for i in range(1, count_y - 1, 2) for pair in ((i, i + 1), (i + 1, i))])

    k0, f0, k1, f1, up, down, side = call(
        fine_kernel, 16,
        [(22, *full), (20, *full), (10, *full1), (8, *full1), (11, *tile1), (11, *tile1), (18, *tile1)],
        [(6, 20, *full)] + [(20, *full)] * 4 + [(18, *full), (18, 24, 128)],
        core, outer, one, two, sibling, after, scalars=1)
    x_low, x_high = both_sides(up, down, along_x)
    y_low, y_high = both_sides(side, side, along_y)
    copies, = call(
        next_kernel, 8,
        [(count_x * chips, 4, 128)],
        [(6, 8, *full1)] + [(8, *full1)] * 4 + [(4, *full1)],
        k1, f1)

    mine = lax.all_to_all(copies, ("gx", "chip"), 0, 0).reshape(-1, 128)
    waited = (mine, x_low, x_high, y_low, y_high)
    mine = pl.pallas_call(
        gate_kernel,
        out_shape=jax.ShapeDtypeStruct(mine.shape, F32),
        in_specs=[pl.BlockSpec(memory_space=pltpu.VMEM)] * len(waited),
        out_specs=pl.BlockSpec(memory_space=pltpu.VMEM),
        input_output_aliases={0: 0},
        compiler_params=pltpu.CompilerParams(vmem_limit_bytes=4 * MIB),
        interpret=INTERPRET,
    )(*waited)
    other = lax.ppermute(mine, "core", [(0, 1), (1, 0)])

    prepared = call(
        prepare_kernel, 16,
        [(4, 16, *half)] + [(16, *half)] * 2,
        [(16, *half)],
        k0, f0, mine)
    prepared1 = call(
        prepare1_kernel, 8,
        [(4, 16, *full1)] + [(16, *full1)] * 2,
        [(16, *full1)] * 3,
        k1, f1, x_low, x_high, y_low, y_high, mine)

    place = jnp.stack([lax.axis_index("gx"), lax.axis_index(("chip", "core"))]).astype(jnp.int32)
    plane2 = (2, count_y // 2, 128)
    padded = (2 * count_x + 8, *plane2)
    near_e, = call(
        make_coarse_kernel(count_x, count_y), 20,
        [(6, 16, 128)],
        [padded, (6, *padded)] + [padded] * 5
        + [(2 * count_x, *plane2), (6, count_x // 4, *plane2), (count_x // 4, *plane2), (10, *plane2)],
        place, mine, other, scalars=1, flops=6000000000)

    correction, residual = call(
        post_kernel, 16,
        [f.shape, f.shape],
        [(16, *full1)] * 3 + [(8, *full1)] + [(16, *half)] * 4,
        near_e, *prepared1, *prepared)
    return correction, residual


def solution(mesh):
    shape = (mesh.shape["gx"], mesh.shape["gy"] // 2, 2)
    mesh = jax.sharding.Mesh(mesh.devices.reshape(shape), ("gx", "chip", "core"))
    spec = P("gx", ("chip", "core"), None)
    return jax.shard_map(body, mesh=mesh, in_specs=(spec, spec), out_specs=(spec, spec), check_vma=False)
```

```python
import math

import jax
import jax.numpy as jnp
from jax import lax
from jax.experimental import pallas as pl
from jax.experimental.pallas import tpu as pltpu
from jax.sharding import PartitionSpec as P

INTERPRET = False
COARSE_STEPS = 8
F32 = jnp.float32
MIB = 1024 * 1024


def step_factors(low_end, steps):
    center, radius = 0.5 * (2.0 + low_end), 0.5 * (2.0 - low_end)
    sigma = center / radius
    ratio = 1.0 / sigma
    factors = [(0.0, 1.0 / center)]
    for _ in range(steps - 1):
        ratio_next = 1.0 / (2.0 * sigma - ratio)
        factors.append((ratio_next * ratio, 2.0 * ratio_next / radius))
        ratio = ratio_next
    return factors


(_, FIRST), (KEEP, ADD) = step_factors(0.4, 2)
COARSE_FACTORS = step_factors(0.02, COARSE_STEPS)


def iota(shape, dim):
    return lax.broadcasted_iota(jnp.int32, shape, dim)


def shifted(value, step, axis):
    return pltpu.roll(value, (-step) % value.shape[axis], axis)


def parts_of(value):
    parts = []
    for _ in range(3):
        part = value.astype(jnp.bfloat16)
        parts.append(part)
        value = value - part.astype(F32)
    return parts


def ones_where(condition):
    return jnp.where(condition, 1.0, 0.0).astype(jnp.bfloat16)


def dot(a, ones):
    rows = a.shape[0]
    out = jnp.dot(jnp.concatenate(parts_of(a), 0), ones, preferred_element_type=F32)
    return out[0:rows] + out[rows:2 * rows] + out[2 * rows:]


def dot_left(ones, a):
    columns = a.shape[1]
    out = jnp.dot(ones, jnp.concatenate(parts_of(a), 1), preferred_element_type=F32)
    return out[:, 0:columns] + out[:, columns:2 * columns] + out[:, 2 * columns:]


def blocks(first, last, size, step):
    count = (last - first) // size
    assert first + count * size == last
    if count == 1:
        step(first)
        return

    def one(number, carry):
        step(first + number * size)
        return carry

    lax.fori_loop(0, count, one, 0)


def near(ref, start, size):
    here = ref[pl.ds(start, size)]
    return (ref[pl.ds(start - 1, size)], ref[pl.ds(start + 1, size)],
            shifted(here, -1, 1), shifted(here, 1, 1), shifted(here, -1, 2), shifted(here, 1, 2))


def near_inside(ref, start, size):
    x_low, x_high, y_low, y_high, z_low, z_high = near(ref, start, size)
    lane = iota(z_low.shape, 2)
    z_low = jnp.where(lane == 0, 0.0, z_low)
    z_high = jnp.where(lane == z_low.shape[2] - 1, 0.0, z_high)
    return x_low, x_high, y_low, y_high, z_low, z_high


def coupling(center, around, masked):
    total = 6.0 * center
    for value in around:
        total = total + value
    inside = center > 0.0
    half_inverse = jnp.where(inside, 1.0 / jnp.where(inside, total, 1.0), 0.0)
    couplings = []
    for number, value in enumerate(around):
        c = (center + value) * half_inverse
        couplings.append(jnp.where(value > 0.0, c, 0.0) if number in masked else c)
    return couplings, 2.0 * half_inverse, 0.5 * total


def pick(c_ref, number, where):
    return c_ref.at[number][where] if where else c_ref[number]


def spread(c_ref, where, around):
    total = pick(c_ref, 0, where) * around[0]
    for number in range(1, 6):
        total = total + pick(c_ref, number, where) * around[number]
    return total


def face_sums(k_ref, start, size):
    center = k_ref[pl.ds(start, size)]
    around = near_inside(k_ref, start, size)
    total = 6.0 * center
    for value in around:
        total = total + value
    inside = center > 0.0
    half_inverse = jnp.where(inside, 1.0 / jnp.where(inside, total, 1.0), 0.0)
    return (center + around[1], center + around[3], jnp.where(around[5] > 0.0, center + around[5], 0.0), half_inverse)


def spread_faces(w_ref, v_ref, start, size):
    at = pl.ds(start, size)
    here, along_y, along_z = v_ref[at], w_ref.at[1][at], w_ref.at[2][at]
    total = w_ref.at[0][at] * v_ref[pl.ds(start + 1, size)]
    total = total + w_ref.at[0][pl.ds(start - 1, size)] * v_ref[pl.ds(start - 1, size)]
    total = total + along_y * shifted(here, 1, 1) + shifted(along_y * here, -1, 1)
    total = total + along_z * shifted(here, 1, 2) + shifted(along_z * here, -1, 2)
    return w_ref.at[3][at] * total


PAIRS = ([("k", dx, 7 - dx) for dx in (1, 2, 3)], [("f", dx, 6 - dx) for dx in (1, 2, 3)])
Y_TILES = 28


def pack_x_kernel(core_ref, k_ref, f_ref, one_ref, two_ref, own_ref, done):
    core = core_ref[0]
    pieces = ((k_ref, 1 - core, one_ref, 0, 7), (f_ref, 2 - 2 * core, one_ref, 7, 6),
              (k_ref, core, two_ref, 0, 7), (f_ref, 2 * core, two_ref, 7, 6),
              (k_ref, 0, own_ref, 0, 8), (f_ref, 0, own_ref, 8, 8))
    copies = [pltpu.make_async_copy(ref.at[pl.ds(first, size)], to.at[pl.ds(place, size)], done.at[number])
              for number, (ref, first, to, place, size) in enumerate(pieces)]
    for copy in copies:
        copy.start()
    for copy in copies:
        copy.wait()


def chosen(first_core, one_ref, two_ref):
    def low(at):
        return jnp.where(first_core, one_ref[at], two_ref[at])

    def high(at):
        return jnp.where(first_core, two_ref[at], one_ref[at])

    return low, high


def pair_tiles():
    tile = 16
    for pairs in PAIRS:
        for side in ("low", "high"):
            for name, dx, far in pairs:
                yield tile, name, side, dx, far
                tile += 1


def halo_plane(name, side, dx, x_low, x_high):
    reach = 7 if name == "k" else 6
    base = 0 if name == "k" else 7
    return x_low(base + reach - dx) if side == "low" else x_high(base + dx - 1)


def pack_y_kernel(core_ref, own_ref, x_one_ref, x_two_ref, sibling_ref, next_ref):
    first_core = core_ref[0] == 0
    x_low, x_high = chosen(first_core, x_one_ref, x_two_ref)
    for ref in (sibling_ref, next_ref):
        ref[0:16] = own_ref[...]
    row = iota((8, own_ref.shape[2]), 0)
    for tile, name, side, dx, far in pair_tiles():
        near_plane = halo_plane(name, side, dx, x_low, x_high)
        far_plane = halo_plane(name, side, far, x_low, x_high)
        up = jnp.where(row < dx, shifted(far_plane, 8 - dx, 0), near_plane)
        down = jnp.where(row >= 8 - dx, shifted(far_plane, dx - 8, 0), near_plane)
        sibling_ref[tile] = jnp.where(first_core, up, down)
        next_ref[tile] = jnp.where(first_core, down, up)


def unpack(first_core, own_ref, x_one_ref, x_two_ref, sibling_ref, next_ref, k0, f0):
    x_low, x_high = chosen(first_core, x_one_ref, x_two_ref)
    below, above = chosen(first_core, next_ref, sibling_ref)
    for to, base, reach, name in ((k0, 0, 7, "k"), (f0, 8, 6, "f")):
        tiles = pl.ds(base, 8)
        to[reach:reach + 8, 0:8] = below(tiles)
        to[reach:reach + 8, 8:16] = own_ref[tiles]
        to[reach:reach + 8, 16:24] = above(tiles)
        first = 0 if name == "k" else 7
        to[0:reach, 8:16] = x_low(pl.ds(first, reach))
        to[reach + 8:2 * reach + 8, 8:16] = x_high(pl.ds(first, reach))
        for plane in (0, 2 * reach + 7):
            to[plane, 0:8] = jnp.zeros(own_ref.shape[1:], F32)
            to[plane, 16:24] = jnp.zeros(own_ref.shape[1:], F32)
    for tile, name, side, dx, far in pair_tiles():
        to, reach = (k0, 7) if name == "k" else (f0, 6)
        near_plane = reach - dx if side == "low" else reach + 7 + dx
        far_plane = reach - far if side == "low" else reach + 7 + far
        low, high = below(tile), above(tile)
        to[near_plane, 0:8] = low
        to[near_plane, 16:24] = high
        if far != dx:
            to[far_plane, 0:8] = shifted(low, dx - 8, 0)
            to[far_plane, 16:24] = shifted(high, 8 - dx, 0)


def fine_kernel(core_ref, own_ref, x_one_ref, x_two_ref, sibling_ref, next_ref,
                k0, f0, k1, f1, up_ref, down_ref, side_ref,
                c0, diag0, g0, d0, e0, sums, zsums):
    unpack(core_ref[0] == 0, own_ref, x_one_ref, x_two_ref, sibling_ref, next_ref, k0, f0)

    def setup(start):
        at = pl.ds(start, 4)
        couplings, inverse, diagonal = coupling(k0[pl.ds(start + 1, 4)], near_inside(k0, start + 1, 4), (4, 5))
        for number in range(6):
            c0.at[number][at] = couplings[number]
        diag0[at] = diagonal
        scaled = inverse * f0[at]
        g0[at] = scaled
        d0[at] = FIRST * scaled

    blocks(0, 20, 4, setup)

    def second(start):
        at = pl.ds(start, 6)
        here = d0[at]
        scaled = g0[at] - here + spread(c0, (at,), near(d0, start, 6))
        g0[at] = scaled
        e0[at] = KEEP * here + ADD * scaled

    blocks(1, 19, 6, second)

    def left(start):
        at = pl.ds(start, 4)
        rest = diag0[at] * (g0[at] - e0[at] + spread(c0, (at,), near(e0, start, 4)))
        sums[start // 2 - 1] = 0.5 * (rest[0] + rest[1])
        sums[start // 2] = 0.5 * (rest[2] + rest[3])

    blocks(2, 18, 4, left)
    for index in range(10):
        sums[index + 8] = 0.125 * (k0[2 * index + 1] + k0[2 * index + 2])
    fold = ones_where(iota((256, 128), 0) // 2 == iota((256, 128), 1))
    zsums[...] = dot(sums[...].reshape(18 * 24, 256), fold).reshape(18, 24, 128)

    k1[...] = jnp.zeros_like(k1)
    f1[...] = jnp.zeros_like(f1)
    rows = zsums[:, pl.ds(0, 12, stride=2), :] + zsums[:, pl.ds(1, 12, stride=2), :]
    f1[:, 2:14, :] = rows[0:8]
    k1[:, 2:14, :] = rows[8:18]
    up_ref[0:6] = k1[1:7, 4:12, :]
    up_ref[6:11] = f1[1:6, 4:12, :]
    down_ref[0:6] = k1[3:9, 4:12, :]
    down_ref[6:11] = f1[2:7, 4:12, :]
    side_ref[0:10] = k1[:, 4:12, :]
    side_ref[10:18] = f1[:, 4:12, :]


def next_kernel(k1, f1, copies_ref, c1, diag1, g1, d1, e1, out):
    def setup1(start):
        at = pl.ds(start, 4)
        couplings, inverse, diagonal = coupling(k1[pl.ds(start + 1, 4)], near_inside(k1, start + 1, 4), (4, 5))
        for number in range(6):
            c1.at[number][at] = couplings[number]
        diag1[at] = diagonal
        scaled = inverse * f1[at]
        g1[at] = scaled
        d1[at] = FIRST * scaled

    blocks(0, 8, 4, setup1)
    at = pl.ds(1, 6)
    scaled = g1[at] - d1[at] + spread(c1, (at,), near(d1, 1, 6))
    g1[at] = scaled
    e1[at] = KEEP * d1[at] + ADD * scaled
    at = pl.ds(2, 4)
    rest = diag1[at] * (g1[at] - e1[at] + spread(c1, (at,), near(e1, 2, 4)))
    for half in range(2):
        out[half] = 0.5 * (rest[2 * half] + rest[2 * half + 1])
        out[half + 2] = 0.125 * (k1[2 * half + 3] + k1[2 * half + 4])
    row, lane = iota((128, 256), 0), iota((128, 256), 1)
    fold = ones_where((lane == row // 2) | (lane == 192 + row // 2))
    folded = dot(out[...].reshape(64, 128), fold).reshape(4, 16, 256)
    lines = [folded[number, 6:7, 0:128] + folded[number, 7:8, 0:128]
             + folded[number, 8:9, 128:256] + folded[number, 9:10, 128:256] for number in range(4)]
    payload = jnp.concatenate(lines, 0)


    def copy(start):
        copies_ref[pl.ds(start, 8)] = jnp.broadcast_to(payload[None], (8, 4, 128))

    blocks(0, copies_ref.shape[0], 8, copy)


def near2(ref, start, size):
    here = ref[pl.ds(start, size)]
    below, above = ref[pl.ds(start - 1, size)], ref[pl.ds(start + 1, size)]
    z_low, z_high = shifted(here, -1, 3), shifted(here, 1, 3)
    turned = shifted(here, 64, 3)
    turned0, turned1 = turned[:, 0:1], turned[:, 1:2]
    first = iota(turned0.shape, 3) < 64
    y_high = [jnp.where(first, turned0, turned1), jnp.where(first, turned1, shifted(turned0, 1, 2))]
    y_low = [jnp.where(first, shifted(turned1, -1, 2), turned0), jnp.where(first, turned0, turned1)]
    return below, above, jnp.concatenate(y_low, 1), jnp.concatenate(y_high, 1), z_low, z_high


def near2_inside(ref, start, size):
    x_low, x_high, y_low, y_high, z_low, z_high = near2(ref, start, size)
    core, row, lane = (iota(z_low.shape, dim) for dim in (1, 2, 3))
    last = z_low.shape[2] - 1
    y_low = jnp.where((core == 0) & (row == 0) & (lane < 64), 0.0, y_low)
    y_high = jnp.where((core == 1) & (row == last) & (lane >= 64), 0.0, y_high)
    z_low = jnp.where(lane % 64 == 0, 0.0, z_low)
    z_high = jnp.where(lane % 64 == 63, 0.0, z_high)
    return x_low, x_high, y_low, y_high, z_low, z_high


def near3(value):
    count = value.shape[0]
    before, after = shifted(value[count - 1:], -32, 3), shifted(value[0:1], 32, 3)
    x_low = jnp.concatenate([before, value[:count - 1]], 0) if count > 1 else before
    x_high = jnp.concatenate([value[1:], after], 0) if count > 1 else after
    core0, core1 = value[:, 0:1], value[:, 1:2]
    y_low = jnp.concatenate([shifted(core1, -1, 2), core0], 1)
    y_high = jnp.concatenate([core1, shifted(core0, 1, 2)], 1)
    return x_low, x_high, y_low, y_high, shifted(value, -1, 3), shifted(value, 1, 3)


def near3_inside(value):
    x_low, x_high, y_low, y_high, z_low, z_high = near3(value)
    plane, core, row, lane = (iota(value.shape, dim) for dim in range(4))
    count, rows = value.shape[0], value.shape[2]
    x_low = jnp.where((plane == 0) & (lane < 32), 0.0, x_low)
    x_high = jnp.where((plane == count - 1) & (lane >= 96), 0.0, x_high)
    y_low = jnp.where((core == 0) & (row == 0), 0.0, y_low)
    y_high = jnp.where((core == 1) & (row == rows - 1), 0.0, y_high)
    z_low = jnp.where(lane % 32 == 0, 0.0, z_low)
    z_high = jnp.where(lane % 32 == 31, 0.0, z_high)
    return x_low, x_high, y_low, y_high, z_low, z_high


def make_coarse_kernel(count_x, count_y):
    planes2, rows, count3 = 2 * count_x, count_y // 2, count_x // 4
    size = 32
    line = (2, rows, 128)

    def coarse_kernel(place_ref, mine_ref, other_ref, near_ref,
                      k2, c2, diag2, g2, d2, e2, h2, sums, c3, e3, x0):
        at_x, at_y = place_ref[0], place_ref[1]
        zero = jnp.zeros((4, *line), F32)
        for ends in (pl.ds(0, 4), pl.ds(planes2 + 4, 4)):
            for ref in (k2, g2, d2, e2):
                ref[ends] = zero
            for number in range(6):
                c2.at[number][ends] = zero

        core = at_y % 2

        def load(index):
            for half in range(2):
                start = index * (4 * rows) + half
                to = 2 * index + half + 4
                for ref, side in ((mine_ref, core), (other_ref, 1 - core)):
                    k2[to, side] = ref[pl.ds(start + 2, rows, stride=4), :]
                    e2[to, side] = ref[pl.ds(start, rows, stride=4), :]

        def load_some(start):
            for index in range(4):
                load(start + index)

        blocks(0, count_x, 4, load_some)

        def setup(start):
            at = pl.ds(start, size)
            couplings, inverse, diagonal = coupling(k2[at], near2_inside(k2, start, size), (2, 3, 4, 5))
            for number in range(6):
                c2.at[number][at] = couplings[number]
            diag2[at] = diagonal
            scaled = inverse * e2[at]
            g2[at] = scaled
            d2[at] = FIRST * scaled

        blocks(4, planes2 + 4, size, setup)

        def second(start):
            at = pl.ds(start, size)
            here = d2[at]
            scaled = g2[at] - here + spread(c2, (at,), near2(d2, start, size))
            h2[at] = scaled
            e2[at] = KEEP * here + ADD * scaled

        blocks(4, planes2 + 4, size, second)

        def left(start):
            at = pl.ds(start, size)
            rest = diag2[at] * (h2[at] - e2[at] + spread(c2, (at,), near2(e2, start, size)))
            rest = rest.reshape(size // 2, 2, *line)
            here = k2[at].reshape(size // 2, 2, *line)
            to = (start - 4) // 2
            sums[pl.ds(to, size // 2)] = 0.5 * (rest[:, 0] + rest[:, 1])
            sums[pl.ds(to + count_x, size // 2)] = 0.125 * (here[:, 0] + here[:, 1])

        blocks(4, planes2 + 4, size, left)

        flat = count3 * 2 * rows
        row, lane = iota((512, 128), 0), iota((512, 128), 1)
        fold = ones_where(lane == 32 * (row // 128) + (row % 64) // 2)
        quarters = [jnp.concatenate([sums[pl.ds(first + quarter * count3, count3)].reshape(flat, 128)
                                     for first in (0, count_x)], 0) for quarter in range(4)]
        folded = dot(jnp.concatenate(quarters, 1), fold)
        f3 = folded[0:flat].reshape(count3, *line)
        k3 = folded[flat:].reshape(count3, *line)
        couplings, inverse, _ = coupling(k3, near3_inside(k3), (0, 1, 2, 3, 4, 5))
        for number in range(6):
            c3[number] = couplings[number]
        scaled = inverse * f3
        step = COARSE_FACTORS[0][1] * scaled
        total = step
        for keep, add in COARSE_FACTORS[1:]:
            scaled = scaled - step + spread(c3, (), near3(step))
            step = keep * step + add * scaled
            total = total + step
        e3[...] = total

        base = 2 * at_x
        parts = []
        for number in range(5):
            x3 = at_x - 2 + number
            inside = (x3 >= 0) & (x3 < count_x)
            safe = jnp.clip(x3, 0, count_x - 1)
            plane = pltpu.roll(e3[safe % count3].reshape(2 * rows, 128), (128 - 32 * (safe // count3)) % 128, 1)
            parts.append(jnp.where(inside, plane, 0.0))
        row, lane = iota((128, 128), 0), iota((128, 128), 1)
        unfold = ones_where((row < 32) & ((lane % 64) // 2 == row))
        up = dot(jnp.concatenate(parts, 0), unfold).reshape(5, *line)
        local = pl.ds(base, 10)
        twice = jnp.stack([up, up], 1).reshape(10, *line)
        x0[...] = d2[local] + e2[local] + twice
        inner = pl.ds(base + 1, 8)
        scaled = g2[inner] - x0[1:9] + spread(c2, (inner,), near2(x0, 1, 8))
        h2[0:8] = scaled
        d2[0:8] = FIRST * scaled
        inner = pl.ds(base + 2, 6)
        here = d2[1:7]
        scaled = h2[1:7] - here + spread(c2, (inner,), near2(d2, 1, 6))
        found = x0[2:8] + (1.0 + KEEP) * here + ADD * scaled

        row, lane = iota((128, 256), 0), iota((128, 256), 1)
        widen = ones_where(row == 64 * (lane // 128) + (lane % 128) // 2)
        wide = dot(found.reshape(6 * 2 * rows, 128), widen)
        target, source = iota((16, 4 * rows), 0), iota((16, 4 * rows), 1)
        half, source = source // (2 * rows), source % (2 * rows)
        source = 2 * (source % rows) + source // rows
        inside = (target >= 2) & (target < 14) & (source == at_y - 1 + (target - 2) // 4)
        spread_rows = ones_where(inside & (((target - 2) % 4) // 2 == half))
        both = [jnp.concatenate([wide[2 * rows * index:2 * rows * (index + 1), 128 * half:128 * half + 128]
                                 for index in range(6)], 1) for half in range(2)]
        near_e = dot_left(spread_rows, jnp.concatenate(both, 0))
        for index in range(6):
            near_ref[index] = near_e[:, 128 * index:128 * index + 128]

    return coarse_kernel


def prepare_kernel(k_ref, f_ref, after_ref, w0, g0, x0, d0):
    def cut(value):
        return shifted(value, 4, 1)[:, 0:16]

    def setup0(start):
        at = pl.ds(start, 4)
        faces = face_sums(k_ref, start + 3, 4)
        for number in range(4):
            w0.at[number][at] = cut(faces[number])
        scaled = cut(2.0 * faces[3] * f_ref[pl.ds(start + 2, 4)])
        g0[at] = scaled
        d0[at] = FIRST * scaled

    blocks(0, 16, 4, setup0)

    def guess0(start):
        at = pl.ds(start, 7)
        here = d0[at]
        scaled = g0[at] - here + spread_faces(w0, d0, start, 7)
        x0[at] = (1.0 + KEEP) * here + ADD * scaled

    blocks(1, 15, 7, guess0)


def gate_kernel(*refs):
    pass


def prepare1_kernel(k_ref, f_ref, x_low_ref, x_high_ref, y_low_ref, y_high_ref, after_ref, w1, g1, x1, k1, f1, d1):
    row = iota((8, 128), 0)

    def join(low, middle, high):
        middle = shifted(middle, 4, 1)
        return jnp.concatenate([jnp.where(row < 6, low, middle), jnp.where(row < 2, middle, high)], 1)

    def alone(tiles):
        tiles = shifted(tiles, 4, 1)
        return jnp.concatenate([tiles, tiles], 1)

    middle = jnp.concatenate([x_low_ref[3:6], k_ref[3:7, 4:12, :], x_high_ref[0:3]], 0)
    k1[0:3] = alone(x_low_ref[0:3])
    k1[3:13] = join(y_low_ref[0:10], middle, y_high_ref[0:10])
    k1[13:16] = alone(x_high_ref[3:6])
    middle = jnp.concatenate([x_low_ref[9:11], f_ref[2:6, 4:12, :], x_high_ref[6:8]], 0)
    f1[1:4] = alone(x_low_ref[6:9])
    f1[4:12] = join(y_low_ref[10:18], middle, y_high_ref[10:18])
    f1[12:15] = alone(x_high_ref[8:11])

    def setup1(start):
        at = pl.ds(start, 7)
        faces = face_sums(k1, start, 7)
        for number in range(4):
            w1.at[number][at] = faces[number]
        scaled = 2.0 * faces[3] * f1[at]
        g1[at] = scaled
        d1[at] = FIRST * scaled

    blocks(1, 15, 7, setup1)
    at = pl.ds(2, 12)
    here = d1[at]
    scaled = g1[at] - here + spread_faces(w1, d1, 2, 12)
    x1[at] = (1.0 + KEEP) * here + ADD * scaled


def post_kernel(near_ref, w1, g1, x1, w0, g0, x0, correction_ref, residual_ref,
                y1, d1, h1, wide, y0, d0, h0, v0):
    up = near_ref[...]
    y1[2:14] = x1[2:14] + jnp.stack([up, up], 1).reshape(12, 16, 128)
    scaled = g1[3:13] - y1[3:13] + spread_faces(w1, y1, 3, 10)
    h1[3:13] = scaled
    d1[3:13] = FIRST * scaled
    here = d1[4:12]
    scaled = h1[4:12] - here + spread_faces(w1, d1, 4, 8)
    found = y1[4:12] + (1.0 + KEEP) * here + ADD * scaled
    wide[:, pl.ds(0, 8, stride=2), :] = found[:, 4:12]
    wide[:, pl.ds(1, 8, stride=2), :] = found[:, 4:12]
    unfold = ones_where(iota((128, 256), 0) == iota((128, 256), 1) // 2)
    up = dot(wide[...].reshape(128, 128), unfold).reshape(8, 16, 256)

    for index in range(1, 15):
        y0[index] = x0[index] + up[index // 2]

    def first0(start):
        at = pl.ds(start, 6)
        scaled = g0[at] - y0[at] + spread_faces(w0, y0, start, 6)
        h0[at] = scaled
        d0[at] = FIRST * scaled

    blocks(2, 14, 6, first0)

    def second0(start):
        at = pl.ds(start, 5)
        here = d0[at]
        scaled = h0[at] - here + spread_faces(w0, d0, start, 5)
        h0[at] = scaled
        v0[at] = KEEP * here + ADD * scaled

    blocks(3, 13, 5, second0)

    def last0(start):
        at, to = pl.ds(start, 4), pl.ds(start - 4, 4)
        here = v0[at]
        correction_ref[to] = (y0[at] + d0[at] + here)[:, 4:12]
        scaled = h0[at] - here + spread_faces(w0, v0, start, 4)
        residual_ref[to] = scaled[:, 4:12] * (0.5 / w0.at[3][at][:, 4:12])

    blocks(4, 12, 4, last0)


def call(kernel, limit, shapes, scratch, *operands, scalars=0, flops=0):
    specs = [pl.BlockSpec(memory_space=pltpu.SMEM)] * scalars
    specs += [pl.BlockSpec(memory_space=pltpu.VMEM)] * (len(operands) - scalars)
    return pl.pallas_call(
        kernel,
        out_shape=[jax.ShapeDtypeStruct(shape, F32) for shape in shapes],
        in_specs=specs,
        out_specs=[pl.BlockSpec(memory_space=pltpu.VMEM)] * len(shapes),
        scratch_shapes=[pltpu.VMEM(shape, F32) for shape in scratch],
        compiler_params=pltpu.CompilerParams(vmem_limit_bytes=limit * MIB),
        cost_estimate=pl.CostEstimate(flops=flops, bytes_accessed=0, transcendentals=0) if flops else None,
        interpret=INTERPRET,
    )(*operands)


def both_sides(up, down, axes):
    count = math.prod(lax.axis_size(axis) for axis in axes)
    low = lax.ppermute(up, axes, [(i, i + 1) for i in range(count - 1)])
    high = lax.ppermute(down, axes, [(i + 1, i) for i in range(count - 1)])
    return low, high


def body(f, k):
    count_x, chips = lax.axis_size("gx"), lax.axis_size("chip")
    count_y = 2 * chips
    along_x, along_y = ("gx",), ("chip", "core")
    tile, full, half = f.shape[1:], (24, 256), (16, 256)
    tile1, full1 = (8, 128), (16, 128)
    core = lax.axis_index("core").astype(jnp.int32).reshape(1)
    one, two, own = pl.pallas_call(
        pack_x_kernel,
        out_shape=[jax.ShapeDtypeStruct((planes, *tile), F32) for planes in (13, 13, 16)],
        in_specs=[pl.BlockSpec(memory_space=pltpu.SMEM)] + [pl.BlockSpec(memory_space=pltpu.HBM)] * 2,
        out_specs=[pl.BlockSpec(memory_space=pltpu.VMEM)] * 3,
        scratch_shapes=[pltpu.SemaphoreType.DMA((6,))],
        compiler_params=pltpu.CompilerParams(vmem_limit_bytes=4 * MIB),
        interpret=INTERPRET,
    )(core, k, f)
    route = [(2 * i, 2 * i + 2) for i in range(count_x - 1)] + [(2 * i + 3, 2 * i + 1) for i in range(count_x - 1)]
    one = lax.ppermute(one, ("gx", "core"), route)
    two = lax.ppermute(two, ("gx", "core"), [(to, source) for source, to in route])
    packed, outer = call(pack_y_kernel, 4, [(Y_TILES, *tile)] * 2, [], core, own, one, two, scalars=1)
    sibling = lax.ppermute(packed, "core", [(0, 1), (1, 0)])
    after = lax.ppermute(outer, along_y, [pair for i in range(1, count_y - 1, 2) for pair in ((i, i + 1), (i + 1, i))])

    k0, f0, k1, f1, up, down, side = call(
        fine_kernel, 16,
        [(22, *full), (20, *full), (10, *full1), (8, *full1), (11, *tile1), (11, *tile1), (18, *tile1)],
        [(6, 20, *full)] + [(20, *full)] * 4 + [(18, *full), (18, 24, 128)],
        core, outer, one, two, sibling, after, scalars=1)
    x_low, x_high = both_sides(up, down, along_x)
    y_low, y_high = both_sides(side, side, along_y)
    copies, = call(
        next_kernel, 8,
        [(count_x * chips, 4, 128)],
        [(6, 8, *full1)] + [(8, *full1)] * 4 + [(4, *full1)],
        k1, f1)

    mine = lax.all_to_all(copies, ("gx", "chip"), 0, 0).reshape(-1, 128)
    waited = (mine, x_low, x_high, y_low, y_high)
    mine = pl.pallas_call(
        gate_kernel,
        out_shape=jax.ShapeDtypeStruct(mine.shape, F32),
        in_specs=[pl.BlockSpec(memory_space=pltpu.VMEM)] * len(waited),
        out_specs=pl.BlockSpec(memory_space=pltpu.VMEM),
        input_output_aliases={0: 0},
        compiler_params=pltpu.CompilerParams(vmem_limit_bytes=4 * MIB),
        interpret=INTERPRET,
    )(*waited)
    other = lax.ppermute(mine, "core", [(0, 1), (1, 0)])

    prepared = call(
        prepare_kernel, 16,
        [(4, 16, *half)] + [(16, *half)] * 2,
        [(16, *half)],
        k0, f0, mine)
    prepared1 = call(
        prepare1_kernel, 8,
        [(4, 16, *full1)] + [(16, *full1)] * 2,
        [(16, *full1)] * 3,
        k1, f1, x_low, x_high, y_low, y_high, mine)

    place = jnp.stack([lax.axis_index("gx"), lax.axis_index(("chip", "core"))]).astype(jnp.int32)
    plane2 = (2, count_y // 2, 128)
    padded = (2 * count_x + 8, *plane2)
    near_e, = call(
        make_coarse_kernel(count_x, count_y), 20,
        [(6, 16, 128)],
        [padded, (6, *padded)] + [padded] * 5
        + [(2 * count_x, *plane2), (6, count_x // 4, *plane2), (count_x // 4, *plane2), (10, *plane2)],
        place, mine, other, scalars=1, flops=6000000000)

    correction, residual = call(
        post_kernel, 16,
        [f.shape, f.shape],
        [(16, *full1)] * 3 + [(8, *full1)] + [(16, *half)] * 4,
        near_e, *prepared1, *prepared)
    return correction, residual


def solution(mesh):
    shape = (mesh.shape["gx"], mesh.shape["gy"] // 2, 2)
    mesh = jax.sharding.Mesh(mesh.devices.reshape(shape), ("gx", "chip", "core"))
    spec = P("gx", ("chip", "core"), None)
    return jax.shard_map(body, mesh=mesh, in_specs=(spec, spec), out_specs=(spec, spec), check_vma=False)
```
